128 devices in a mesh: row: 8 (over z, core), col: 16 (over x, y).
Axes of the slice: x: 4, y: 4, z: 4, core: 2. Of those that a mesh axis runs over, the one named last changes fastest.
Arguments:
- coarse: bfloat16 [512, 64, 256], P(('row', 'col')), may hold values from -6 to 6
- noisy: bfloat16 [16, 256, 4096], P(None, 'row', 'col'), may hold values from -6 to 6
- cotangent: bfloat16 [64, 256, 4096], P(None, 'row', 'col'), may hold values from -6 to 6
- interp_rows: bfloat16 [8, 32, 4], replicated, may hold values from -1.5 to 1.5
- interp_cols: bfloat16 [128, 256], replicated, may hold values from -0.5 to 0.5
- first_weight: bfloat16 [3, 3, 64, 80], replicated, may hold values from -0.21875 to 0.21875
- second_weight: bfloat16 [3, 3, 64, 64], replicated, may hold values from -0.25 to 0.25
- block_ids: int32 [128, 4], P(('row', 'col')), may hold values from 0 to 127, as said below
- weight_ids: int32 [128, 4], P(('row', 'col')), may hold values from 0 to 7
- col_start: int32 [16], P('col'), may hold values from 0 to 128
Outputs:
- fine_out: bfloat16 [64, 256, 4096], P(None, 'row', 'col')
- first_grad: float32 [3, 3, 64, 80], replicated
- second_grad: float32 [3, 3, 64, 64], replicated
- coarse_grad: float32 [512, 64, 256], P(('row', 'col'))
The draws below stay inside these ranges and needn't reach their ends.
Inputs may be any that keep to these rules, and one draw needn't show every extreme that they name: block_ids of a tile in fine-tile row r lie from r * 16 - 2 to (r + 1) * 16 + 1.
All inputs are finite; a program needn't handle non-finite values.
Results may differ from the reference program's by a relative error of at most 0.0075.
Values may be sent and summed in bfloat16 or wider, within the bound.
A program may use at most 192 MiB of HBM per device.

```python
import jax
import jax.numpy as jnp
from jax import lax

CH = 64
FS = 16
WIDTH = 64
CBR = 4
CCOLS = 256
CW = 128
HB = 2
K = 4
NW = 8
FR = 32
FC = 256
TILES = 128
TCOLS = 16
CROWS = 512
NFY = 256
NFX = 4096
CIN = 80
N_ROW = 8
N_COL = 16


def draw_block_ids(key, part):
    key = jax.random.fold_in(key, 11)
    subkeys = jax.random.split(key, 3)
    tile_index = jnp.arange(TILES, dtype=jnp.int32)[:, None]
    band_row = tile_index // TCOLS
    lowest = jnp.maximum(band_row * TCOLS - HB, 0)
    highest = jnp.minimum((band_row + 1) * TCOLS + HB, TILES)
    span_size = jnp.broadcast_to(highest - lowest, (TILES, K))
    first_draw = jax.random.randint(subkeys[0], (TILES, K), 0, span_size)
    second_draw = jax.random.randint(subkeys[1], (TILES, K), 0, span_size)
    nearest = jnp.minimum(first_draw, second_draw)
    upward = jax.random.randint(subkeys[2], (TILES, K), 0, 2)
    chosen = jnp.where(upward == 1, highest - 1 - nearest, lowest + nearest)
    chosen = chosen.at[0, 0].set(0).at[TILES - 1, 0].set(TILES - 1)
    return chosen.astype(jnp.int32)


def set_ends(result, rng, low, high):
    index_at = [jax.random.randint(jax.random.fold_in(rng, axis), (), 0, length) for axis, length in enumerate(result.shape)]
    main_axis = result.shape.index(max(result.shape))
    beside = index_at[:main_axis] + [(index_at[main_axis] + 1) % result.shape[main_axis]] + index_at[main_axis + 1:]
    return result.at[tuple(index_at)].set(low).at[tuple(beside)].set(high)


def steps_of(key, extent, cuts, smallest, high):
    factor_of, own = 1.0, jax.random.fold_in(key, 6)
    for dim, blocks in cuts:
        steps = jnp.exp(jax.random.uniform(jax.random.fold_in(own, dim), (blocks,), jnp.float32, smallest / len(cuts), high / len(cuts)))
        factor_of = factor_of * jnp.repeat(steps, extent[dim] // blocks).reshape([-1 if axis == dim else 1 for axis in range(len(extent))])
    return factor_of


def centred(key, shape, width, bound, cuts=(), kind=jnp.bfloat16):
    array = jax.random.normal(key, shape, jnp.float32) * width
    if len(cuts) > 0:
        array = steps_of(key, shape, cuts, -0.22, 0.18) * array
    return jnp.clip(array, min=-bound, max=bound).astype(kind)


def setup_inputs(seed: int = 0) -> dict:
    key_list = jax.random.split(jax.random.key(seed), 11)
    return {
        "coarse": centred(key_list[0], (CROWS, CH, CCOLS), 1.0, 6.0, ((0, 128),)),
        "noisy": centred(key_list[1], (FS, NFY, NFX), 1.0, 6.0, ((1, 8), (2, 16))),
        "cotangent": centred(key_list[2], (WIDTH, NFY, NFX), 1.0, 6.0, ((1, 8), (2, 16))),
        "interp_rows": centred(key_list[3], (NW, FR, CBR), (CBR * K) ** -0.5, 1.5),
        "interp_cols": centred(key_list[4], (CW, FC), CW ** -0.5, 0.5),
        "first_weight": centred(key_list[5], (3, 3, WIDTH, CIN), (9 * CIN) ** -0.5, 0.21875),
        "second_weight": centred(key_list[6], (3, 3, WIDTH, WIDTH), (9 * WIDTH) ** -0.5, 0.25),
        "block_ids": draw_block_ids(jax.random.fold_in(key_list[10], 71), 0),
        "weight_ids": set_ends(jax.random.randint(key_list[8], (TILES, K), 0, NW), jax.random.fold_in(key_list[8], 1), 0, NW - 1).astype(jnp.int32),
        "col_start": set_ends(jax.random.randint(key_list[9], (TCOLS,), 0, CCOLS - CW + 1), jax.random.fold_in(key_list[9], 1), 0, CCOLS - CW).astype(jnp.int32),
    }


def shifted(padded, row_off, col_off, tile_rows, tile_cols):
    return padded[:, row_off:row_off + tile_rows, col_off:col_off + tile_cols].reshape(padded.shape[0], tile_rows * tile_cols)

def conv_apply(weights, padded, tile_rows, tile_cols):
    summed = None
    for row_off in range(3):
        for col_off in range(3):
            product = jnp.dot(weights[row_off, col_off], shifted(padded, row_off, col_off, tile_rows, tile_cols), preferred_element_type=jnp.float32)
            summed = product if summed is None else summed + product
    return summed.reshape(weights.shape[2], tile_rows, tile_cols)

def conv_adjoint(weights, padded, tile_rows, tile_cols):
    summed = None
    for row_off in range(3):
        for col_off in range(3):
            product = lax.dot_general(weights[row_off, col_off], shifted(padded, 2 - row_off, 2 - col_off, tile_rows, tile_cols), (((0,), (0,)), ((), ())), preferred_element_type=jnp.float32)
            summed = product if summed is None else summed + product
    return summed.reshape(weights.shape[3], tile_rows, tile_cols)

def weight_grad(gradient, padded, tile_rows, tile_cols):
    flat = gradient.reshape(gradient.shape[0], tile_rows * tile_cols)
    rows_out = []
    for row_off in range(3):
        rows_out.append(jnp.stack([lax.dot_general(flat, shifted(padded, row_off, col_off, tile_rows, tile_cols), (((1,), (1,)), ((), ())), preferred_element_type=jnp.float32) for col_off in range(3)]))
    return jnp.stack(rows_out)

def pad_cells(field):
    return jnp.pad(field, ((0, 0), (1, 1), (1, 1)))

def silu_slope(active):
    sigma = jax.nn.sigmoid(active)
    return sigma * (1.0 + active * (1.0 - sigma))

def regrid_tile(coarse, interp_rows, interp_cols, tile_ids, tile_wsel, offset):
    pieces = []
    for slot in range(K):
        rows_cut = lax.dynamic_slice_in_dim(coarse, (tile_ids[slot] * CBR).astype(jnp.int32), CBR, 0)
        pieces.append(lax.dynamic_slice_in_dim(rows_cut, offset.astype(jnp.int32), CW, 2))
    blocks = jnp.stack(pieces).astype(jnp.float32)
    table = interp_rows[tile_wsel].astype(jnp.float32)
    section = jnp.einsum('kfi,kicw->cfw', table, blocks, precision=lax.Precision.HIGHEST).astype(jnp.bfloat16)
    return jnp.einsum('cfw,wx->cfx', section.astype(jnp.float32), interp_cols.astype(jnp.float32), precision=lax.Precision.HIGHEST).astype(jnp.bfloat16)

def reference(coarse, noisy, cotangent, interp_rows, interp_cols, first_weight, second_weight, block_ids, weight_ids, col_start):
    tile_index = jnp.arange(TILES, dtype=jnp.int32)
    starts_all = col_start[tile_index % TCOLS]
    tiles = lax.map(lambda items: regrid_tile(coarse, interp_rows, interp_cols, items[0], items[1], items[2]), (block_ids, weight_ids, starts_all))
    cond = tiles.reshape(N_ROW, N_COL, CH, FR, FC).transpose(2, 0, 3, 1, 4).reshape(CH, NFY, NFX)
    inputs = jnp.concatenate([noisy, cond], 0)
    input_pad = pad_cells(inputs)
    first_act = conv_apply(first_weight, input_pad, NFY, NFX)
    hidden = jax.nn.silu(first_act).astype(jnp.bfloat16)
    hidden_pad = pad_cells(hidden)
    fine_out = conv_apply(second_weight, hidden_pad, NFY, NFX).astype(jnp.bfloat16)
    second_grad = weight_grad(cotangent, hidden_pad, NFY, NFX)
    hidden_grad = conv_adjoint(second_weight, pad_cells(cotangent), NFY, NFX)
    act_grad = (hidden_grad * silu_slope(first_act)).astype(jnp.bfloat16)
    first_grad = weight_grad(act_grad, input_pad, NFY, NFX)
    cond_grad = conv_adjoint(first_weight[:, :, :, FS:], pad_cells(act_grad), NFY, NFX).astype(jnp.bfloat16)

    def accumulate(carry, items):
        index, tile_ids, tile_wsel = items
        band_row = index // TCOLS
        band_col = index % TCOLS
        offset = col_start[band_col].astype(jnp.int32)
        tile_grad = lax.dynamic_slice_in_dim(cond_grad, (band_row * FR).astype(jnp.int32), FR, 1)
        tile_grad = lax.dynamic_slice_in_dim(tile_grad, (band_col * FC).astype(jnp.int32), FC, 2)
        section_grad = jnp.einsum('cfx,wx->cfw', tile_grad.astype(jnp.float32), interp_cols.astype(jnp.float32), precision=lax.Precision.HIGHEST).astype(jnp.bfloat16)
        table = interp_rows[tile_wsel].astype(jnp.float32)
        block_grads = jnp.einsum('kfi,cfw->kicw', table, section_grad.astype(jnp.float32), precision=lax.Precision.HIGHEST)
        for slot in range(K):
            first_row = (tile_ids[slot] * CBR).astype(jnp.int32)
            current = lax.dynamic_slice(carry, (first_row, jnp.int32(0), offset), (CBR, CH, CW))
            carry = lax.dynamic_update_slice(carry, current + block_grads[slot], (first_row, jnp.int32(0), offset))
        return (carry, None)
    coarse_grad, unused = lax.scan(accumulate, jnp.zeros((CROWS, CH, CCOLS), jnp.float32), (tile_index, block_ids, weight_ids))
    return (fine_out, first_grad, second_grad, coarse_grad)
```

```python
import jax
import jax.numpy as jnp
from jax import lax
from jax.experimental import pallas as pl
from jax.experimental.pallas import tpu as pltpu
from jax.sharding import PartitionSpec as P

F32 = jnp.float32
BF16 = jnp.bfloat16
MESH = pl.DeviceIdType.MESH

NR = 8
NC = 16
HB = 2
K = 4
FR = 32
CH = 64
FS = 16
CIN = 80
CW = 128
NB = NC + 2 * HB

DIRS = ((0, 1), (0, -1), (1, 1), (1, -1), (-1, 1), (-1, -1))
COT, INP, HID, ACT = range(4)


def iota(shape, dim):
    return lax.broadcasted_iota(jnp.int32, shape, dim)


def dot(a, b):
    return jnp.dot(a, b, preferred_element_type=F32)


def dot_nt(a, b):
    return lax.dot_general(a, b, (((1,), (1,)), ((), ())), preferred_element_type=F32)


def kernel(
    block_ids,
    weight_ids,
    col_start,
    coarse,
    noisy,
    cot,
    rowsx,
    cols,
    wf1,
    wf2,
    wb1,
    wb2,
    fine_out,
    first_out,
    second_out,
    coarse_out,
    v_cot,
    v_in,
    v_hid,
    v_act,
    hgrad,
    edge,
    edge_in,
    edge_got,
    edge_got_in,
    halo,
    cs,
    slab,
    gath,
    pieces,
    lmat,
    sec,
    pgrad,
    sbuf,
    rbuf,
    acc1,
    acc2,
    gbuf,
    gpart,
    grow,
    gall,
    x_send,
    x_recv,
    cs_send,
    cs_recv,
    ag_send,
    ag_recv,
    hb_send,
    rs_send,
    rs_recv,
    w1_send,
    w1_recv,
    w2_send,
    w2_recv,
    w3_send,
    w3_recv,
):
    r = lax.axis_index("row")
    c = lax.axis_index("col")

    def row_at(d):
        return lax.rem(r + (d + NR), NR)

    def col_at(d):
        return lax.rem(c + (d + NC), NC)

    def remote(src, dst, send, recv, device):
        return pltpu.make_async_remote_copy(
            src_ref=src, dst_ref=dst, send_sem=send, recv_sem=recv, device_id=device, device_id_type=MESH
        )

    barrier = pltpu.get_barrier_semaphore()

    def greet_cols(d, _):
        for dr in (-1, 0, 1):
            if dr == 0:
                @pl.when(d > 0)
                def _():
                    pl.semaphore_signal(barrier, inc=1, device_id=(r, col_at(d)), device_id_type=MESH)
            else:
                pl.semaphore_signal(barrier, inc=1, device_id=(row_at(dr), col_at(d)), device_id_type=MESH)
        return 0

    lax.fori_loop(0, NC, greet_cols, 0)
    for dr in range(2, NR - 1):
        pl.semaphore_signal(barrier, inc=1, device_id=(row_at(dr), c), device_id_type=MESH)
    pl.semaphore_wait(barrier, 3 * NC - 1 + NR - 3)

    cs[c] = jnp.full((8, 128), col_start[0], jnp.int32)

    def cs_copy(d):
        return remote(cs.at[c], cs.at[c], cs_send.at[d], cs_recv.at[c], (r, col_at(d)))

    def cs_arrival(d):
        other = col_at(d)
        return remote(cs.at[other], cs.at[other], cs_send.at[d], cs_recv.at[other], (r, other))

    def start_cs(d, _):
        cs_copy(d).start()
        return 0

    lax.fori_loop(1, NC, start_cs, 0)

    i0, i1 = iota((256, 256), 0), iota((256, 256), 1)
    perm = jnp.where(
        (lax.rem(i0, 16) == lax.div(i1, 16)) & (lax.div(i0, 16) == lax.rem(i1, 16)), 1.0, 0.0
    ).astype(BF16)

    def flip_in(src, dst, c0, h0):
        block = src[c0 : c0 + 16, h0 : h0 + 16, :].reshape(256, 256)
        moved = dot(perm, block).astype(BF16).reshape(16, 16, 256)
        dst[1 + h0 : 17 + h0, 1, c0 : c0 + 16, :] = moved

    for c0 in range(0, CH, 16):
        for h0 in range(0, FR, 16):
            flip_in(cot, v_cot, c0, h0)

    bufs = {
        COT: (v_cot, edge.at[0], edge_got.at[0], CH),
        INP: (v_in, edge_in, edge_got_in, CIN),
        HID: (v_hid, edge.at[1], edge_got.at[1], CH),
        ACT: (v_act, edge.at[2], edge_got.at[2], CH),
    }

    def halo_copies(x):
        v, e, got, _ = bufs[x]
        copies = [
            remote(e, got.at[i], x_send.at[x, i], x_recv.at[x, i], (row_at(dr), col_at(dc)))
            for i, (dr, dc) in enumerate(DIRS)
        ]
        copies.append(remote(v.at[FR, 1], v.at[0, 1], x_send.at[x, 6], x_recv.at[x, 6], (row_at(1), c)))
        copies.append(remote(v.at[1, 1], v.at[FR + 1, 1], x_send.at[x, 7], x_recv.at[x, 7], (row_at(-1), c)))
        return copies

    def halo_start(x):
        v, e, _, chans = bufs[x]
        lane = iota((chans, 128), 1)

        def pack(h, held):
            left = v[h + 1, 1, :, 0:128].astype(F32)[:, 0:1]
            right = v[h + 1, 1, :, 128:256].astype(F32)[:, 127:128]
            held = jnp.where(lane == h, left, held)
            return jnp.where(lane == h + 64, right, held)

        e[...] = lax.fori_loop(0, FR, pack, jnp.zeros((chans, 128), F32)).astype(BF16)
        for copy in halo_copies(x):
            copy.start()

    def halo_finish(x):
        v, _, got, chans = bufs[x]
        for copy in halo_copies(x):
            copy.wait()
        lane = iota((chans, 128), 1)

        @pl.when(r == 0)
        def _():
            v[0, 1] = jnp.zeros((chans, 256), BF16)

        @pl.when(r == NR - 1)
        def _():
            v[FR + 1, 1] = jnp.zeros((chans, 256), BF16)

        top = (r > 0).astype(F32)
        bottom = (r < NR - 1).astype(F32)
        west = (c > 0).astype(F32)
        east = (c < NC - 1).astype(F32)

        def side(mid, up, down, s_mid, s_up, s_down, there):
            a = pltpu.roll(got[mid].astype(F32), s_mid, 1)
            b = pltpu.roll(got[up].astype(F32), s_up, 1) * top
            d = pltpu.roll(got[down].astype(F32), s_down, 1) * bottom
            return jnp.where(lane == 0, b, jnp.where(lane == FR + 1, d, a)) * there

        halo[0, 0:chans] = side(0, 2, 4, 65, 33, 97, west)
        halo[1, 0:chans] = side(1, 3, 5, 1, 97, 33, east)

        def shift(j, _):
            t0 = v[j, 1, :, 0:128].astype(F32)
            t1 = v[j, 1, :, 128:256].astype(F32)
            w = pltpu.roll(halo[0, 0:chans], lax.rem(128 - j, 128), 1)
            e = pltpu.roll(halo[1, 0:chans], 127 - j, 1)
            r0, r1 = pltpu.roll(t0, 1, 1), pltpu.roll(t1, 1, 1)
            s0, s1 = pltpu.roll(t0, 127, 1), pltpu.roll(t1, 127, 1)
            v[j, 0, :, 0:128] = jnp.where(lane == 0, w, r0).astype(BF16)
            v[j, 0, :, 128:256] = jnp.where(lane == 0, r0, r1).astype(BF16)
            v[j, 2, :, 0:128] = jnp.where(lane == 127, s1, s0).astype(BF16)
            v[j, 2, :, 128:256] = jnp.where(lane == 127, e, s1).astype(BF16)
            return 0

        lax.fori_loop(0, FR + 2, shift, 0)

    def conv_pair(weights, v, p, chans):
        return dot(weights[...], v[pl.ds(2 * p, 4)].reshape(12 * chans, 256))

    halo_start(COT)

    for h0 in range(0, FR, 16):
        flip_in(noisy, v_in, 0, h0)

    def wait_cs(d, _):
        cs_copy(d).wait_send()
        cs_arrival(d).wait_recv()
        return 0

    lax.fori_loop(1, NC, wait_cs, 0)

    def ag_copy(d):
        to = col_at(d)
        return remote(slab.at[to], gath.at[HB + c], ag_send.at[d], ag_recv.at[HB + c], (r, to))

    def hb_copy(n, down):
        if down:
            return remote(slab.at[n], gath.at[c - (NC - HB)], hb_send.at[n], ag_recv.at[c - (NC - HB)], (row_at(1), n))
        return remote(slab.at[n], gath.at[NC + HB + c], hb_send.at[n], ag_recv.at[NC + HB + c], (row_at(-1), n))

    whole = coarse[...].reshape(256, 256)

    def cut(d, _):
        to = col_at(d)
        start = cs[to][0:1, :]
        pick = jnp.where(iota((256, 128), 0) == iota((256, 128), 1) + start, 1.0, 0.0).astype(BF16)
        slab[to] = dot(whole, pick).astype(BF16).reshape(4, CH, CW)

        @pl.when(d > 0)
        def _():
            ag_copy(d).start()

        @pl.when(d == 0)
        def _():
            gath[HB + c] = slab[c]

        @pl.when(c >= NC - HB)
        def _():
            hb_copy(to, True).start()

        @pl.when(c < HB)
        def _():
            hb_copy(to, False).start()

        return 0

    lax.fori_loop(0, NC, cut, 0)

    halo_finish(COT)

    def hidden_grad(p, _):
        hgrad[pl.ds(2 * p, 2)] = conv_pair(wb2, v_cot, p, CH).reshape(2, CH, 256)
        return 0

    lax.fori_loop(0, FR // 2, hidden_grad, 0)

    lane256 = iota((FR, 256), 1)
    table = jnp.zeros((FR, 256), BF16)
    for k in range(K):
        table = jnp.where(lax.div(lane256, 64) == k, rowsx[weight_ids[0, k]], table)
    spread = jnp.where(lax.div(iota((512, FR), 0), 16) == iota((512, FR), 1), 1.0, 0.0).astype(BF16)
    same = lax.rem(iota((512, 256), 0), 16) == lax.rem(iota((512, 256), 1), 16)
    lmat[...] = jnp.where(same, dot(spread, table), 0.0).astype(BF16)

    def wait_ag(d, _):
        ag_copy(d).wait_send()
        remote(slab.at[0], gath.at[HB + col_at(d)], ag_send.at[d], ag_recv.at[HB + col_at(d)], (r, col_at(d))).wait_recv()
        return 0

    lax.fori_loop(1, NC, wait_ag, 0)
    for b in (0, 1, NB - 2, NB - 1):
        remote(slab.at[0], gath.at[b], hb_send.at[0], ag_recv.at[b], (row_at(1), c)).wait_recv()

    def wait_hb(n, _):
        @pl.when((c >= NC - HB) | (c < HB))
        def _():
            remote(slab.at[n], gath.at[0], hb_send.at[n], ag_recv.at[0], (row_at(1), n)).wait_send()

        return 0

    lax.fori_loop(0, NC, wait_hb, 0)

    first_block = r * NC - HB
    for k in range(K):
        piece = gath[jnp.clip(block_ids[0, k] - first_block, 0, NB - 1)]
        for g in range(4):
            pieces[g, 64 * k : 64 * k + 64, :] = piece[:, 16 * g : 16 * g + 16, :].reshape(64, CW)
    for g in range(4):
        sec[:, 16 * g : 16 * g + 16, :] = dot(lmat[...], pieces[g]).astype(BF16).reshape(FR, 16, CW)

    def regrid(q, _):
        rows = sec[pl.ds(4 * q, 4)].reshape(256, CW)
        v_in[pl.ds(1 + 4 * q, 4), 1, FS:CIN, :] = dot(rows, cols[...]).astype(BF16).reshape(4, CH, 256)
        return 0

    lax.fori_loop(0, FR // 4, regrid, 0)

    halo_start(INP)
    halo_finish(INP)

    def first_level(p, _):
        pre = conv_pair(wf1, v_in, p, CIN).reshape(2, CH, 256)
        s = 1.0 / (1.0 + jnp.exp(-pre))
        v_hid[pl.ds(1 + 2 * p, 2), 1] = (pre * s).astype(BF16)
        slope = s * (1.0 + pre * (1.0 - s))
        v_act[pl.ds(1 + 2 * p, 2), 1] = (hgrad[pl.ds(2 * p, 2)] * slope).astype(BF16)
        return 0

    lax.fori_loop(0, FR // 2, first_level, 0)
    halo_start(HID)
    halo_start(ACT)

    def weight_grad(acc, left, v, chans):
        acc[...] = jnp.zeros(acc.shape, F32)

        def step(p, _):
            rows = left[pl.ds(1 + 2 * p, 2), 1].reshape(128, 256)
            for j in range(4):
                acc[j, :, 0 : 3 * chans] += dot_nt(rows, v[2 * p + j].reshape(3 * chans, 256))
            return 0

        lax.fori_loop(0, FR // 2, step, 0)

    weight_grad(acc1, v_act, v_in, CIN)
    halo_finish(HID)
    weight_grad(acc2, v_cot, v_hid, CH)
    for which, acc in ((0, acc1), (1, acc2)):
        for a in range(3):
            total = acc[a, 0:64, :] + acc[a + 1, 64:128, :]
            gbuf[8 * which : 8 * which + 8, a] = total.reshape(8, 8, 256)

    def w1_copy(d):
        to = col_at(d)
        return remote(gbuf.at[to], gpart.at[c], w1_send.at[d], w1_recv.at[c], (r, to))

    def start_w1(d, _):
        w1_copy(d).start()
        return 0

    lax.fori_loop(1, NC, start_w1, 0)
    gpart[c] = gbuf[c]

    halo_finish(ACT)

    def cond_grad(p, _):
        grad = conv_pair(wb1, v_act, p, CH).astype(BF16)
        sec[pl.ds(2 * p, 2)] = dot_nt(grad, cols[...]).astype(BF16).reshape(2, CH, CW)
        return 0

    lax.fori_loop(0, FR // 2, cond_grad, 0)
    eye = jnp.where(i0 == i1, 1.0, 0.0).astype(BF16)
    lmat_t = dot_nt(eye, lmat[...]).astype(BF16)
    for g in range(4):
        part = dot(lmat_t, sec[:, 16 * g : 16 * g + 16, :].reshape(512, CW))
        pgrad[:, :, 16 * g : 16 * g + 16, :] = part.reshape(K, 4, 16, CW)

    def contribution(b):
        total = None
        for k in range(K):
            hit = (block_ids[0, k] - first_block == b).astype(F32)
            term = pgrad[k] * hit
            total = term if total is None else total + term
        return total.astype(BF16)

    def rs_copy(d):
        to = col_at(d)
        return remote(sbuf.at[HB + to], rbuf.at[c], rs_send.at[d], rs_recv.at[c], (r, to))

    def rs_halo(n):
        b, dr, to = ((0, -1, NC - 2), (1, -1, NC - 1), (NB - 2, 1, 0), (NB - 1, 1, 1))[n]
        return remote(sbuf.at[b], rbuf.at[NC + c], rs_send.at[NC + n], rs_recv.at[NC + c], (row_at(dr), to))

    for n, b in enumerate((0, 1, NB - 2, NB - 1)):
        sbuf[b] = contribution(b)
        rs_halo(n).start()

    def send_grad(d, _):
        to = col_at(d)
        sbuf[HB + to] = contribution(HB + to)

        @pl.when(d > 0)
        def _():
            rs_copy(d).start()

        @pl.when(d == 0)
        def _():
            rbuf[c] = sbuf[HB + c]

        return 0

    lax.fori_loop(0, NC, send_grad, 0)

    def wait_w1(d, _):
        w1_copy(d).wait_send()
        other = col_at(d)
        remote(gbuf.at[other], gpart.at[other], w1_send.at[d], w1_recv.at[other], (r, other)).wait_recv()
        return 0

    lax.fori_loop(1, NC, wait_w1, 0)
    total = gpart[0]
    for n in range(1, NC):
        total = total + gpart[n]
    grow[r] = total

    def w2_copy(d):
        return remote(grow.at[r], grow.at[r], w2_send.at[d], w2_recv.at[r], (row_at(d), c))

    for d in range(1, NR):
        w2_copy(d).start()

    def second_level(p, _):
        hgrad[pl.ds(2 * p, 2)] = conv_pair(wf2, v_hid, p, CH).reshape(2, CH, 256)
        return 0

    lax.fori_loop(0, FR // 2, second_level, 0)

    for d in range(1, NR):
        w2_copy(d).wait_send()
        other = row_at(d)
        remote(grow.at[other], grow.at[other], w2_send.at[d], w2_recv.at[other], (other, c)).wait_recv()
    total = grow[0]
    for n in range(1, NR):
        total = total + grow[n]
    gall[c] = total

    def w3_copy(d):
        return remote(gall.at[c], gall.at[c], w3_send.at[d], w3_recv.at[c], (r, col_at(d)))

    def start_w3(d, _):
        w3_copy(d).start()
        return 0

    lax.fori_loop(1, NC, start_w3, 0)

    for c0 in range(0, CH, 16):
        for h0 in range(0, FR, 16):
            block = hgrad[h0 : h0 + 16, c0 : c0 + 16, :].astype(BF16).reshape(256, 256)
            fine_out[c0 : c0 + 16, h0 : h0 + 16, :] = dot(perm, block).astype(BF16).reshape(16, 16, 256)

    def place(n, _):
        other = col_at(n)

        @pl.when(n > 0)
        def _():
            rs_copy(n).wait_send()
            remote(sbuf.at[0], rbuf.at[other], rs_send.at[n], rs_recv.at[other], (r, other)).wait_recv()

        return 0

    lax.fori_loop(0, NC, place, 0)
    for n in range(4):
        rs_halo(n).wait_send()
    outer = (c < HB) | (c >= NC - HB)

    def add_from(base):
        def add(n, held):
            start = cs[n][0:1, :]
            start = jnp.concatenate([start, start], axis=1)
            spot = jnp.where(iota((CW, 256), 1) == iota((CW, 256), 0) + start, 1.0, 0.0).astype(BF16)
            coarse_out[...] += dot(rbuf[base + n].reshape(256, CW), spot).reshape(4, CH, 256)
            return 0

        lax.fori_loop(0, NC, add, 0)

    coarse_out[...] = jnp.zeros((4, CH, 256), F32)
    add_from(0)

    @pl.when(outer)
    def _():
        def wait(n, _):
            remote(sbuf.at[0], rbuf.at[NC + n], rs_send.at[0], rs_recv.at[NC + n], (row_at(1), n)).wait_recv()
            return 0

        lax.fori_loop(0, NC, wait, 0)
        add_from(NC)

    def wait_w3(d, _):
        w3_copy(d).wait_send()
        other = col_at(d)
        remote(gall.at[other], gall.at[other], w3_send.at[d], w3_recv.at[other], (r, other)).wait_recv()
        return 0

    lax.fori_loop(1, NC, wait_w3, 0)
    for a in range(3):
        for e in range(3):
            for og in range(8):
                first_out[a, e, 8 * og : 8 * og + 8, :] = gall[og, a, :, e * CIN : (e + 1) * CIN]
                second_out[a, e, 8 * og : 8 * og + 8, :] = gall[8 + og, a, :, e * CH : (e + 1) * CH]


def pair_matrix(w):
    outs, ins = w.shape[2], w.shape[3]
    flat = w.transpose(2, 0, 1, 3).reshape(outs, 9 * ins)
    none = jnp.zeros((outs, 3 * ins), w.dtype)
    return jnp.concatenate(
        [jnp.concatenate([flat, none], axis=1), jnp.concatenate([none, flat], axis=1)], axis=0
    )


def adjoint(w):
    return w[::-1, ::-1].transpose(0, 1, 3, 2)


def local(
    coarse,
    noisy,
    cotangent,
    interp_rows,
    interp_cols,
    first_weight,
    second_weight,
    block_ids,
    weight_ids,
    col_start,
):
    rowsx = jnp.tile(jnp.repeat(interp_rows, 16, axis=2), (1, 1, K))
    smem = pl.BlockSpec(memory_space=pltpu.SMEM)
    vmem = pl.BlockSpec(memory_space=pltpu.VMEM)
    dma = pltpu.SemaphoreType.DMA
    return pl.pallas_call(
        kernel,
        out_shape=(
            jax.ShapeDtypeStruct((CH, FR, 256), BF16),
            jax.ShapeDtypeStruct((3, 3, CH, CIN), F32),
            jax.ShapeDtypeStruct((3, 3, CH, CH), F32),
            jax.ShapeDtypeStruct((4, CH, 256), F32),
        ),
        in_specs=[smem] * 3 + [vmem] * 9,
        out_specs=(vmem,) * 4,
        scratch_shapes=[
            pltpu.VMEM((FR + 2, 3, CH, 256), BF16),
            pltpu.VMEM((FR + 2, 3, CIN, 256), BF16),
            pltpu.VMEM((FR + 2, 3, CH, 256), BF16),
            pltpu.VMEM((FR + 2, 3, CH, 256), BF16),
            pltpu.VMEM((FR, CH, 256), F32),
            pltpu.VMEM((3, CH, 128), BF16),
            pltpu.VMEM((CIN, 128), BF16),
            pltpu.VMEM((3, 6, CH, 128), BF16),
            pltpu.VMEM((6, CIN, 128), BF16),
            pltpu.VMEM((2, CIN, 128), F32),
            pltpu.VMEM((NC, 8, 128), jnp.int32),
            pltpu.VMEM((NC, 4, CH, CW), BF16),
            pltpu.VMEM((NB, 4, CH, CW), BF16),
            pltpu.VMEM((4, 256, CW), BF16),
            pltpu.VMEM((512, 256), BF16),
            pltpu.VMEM((FR, CH, CW), BF16),
            pltpu.VMEM((K, 4, CH, CW), F32),
            pltpu.VMEM((NB, 4, CH, CW), BF16),
            pltpu.VMEM((2 * NC, 4, CH, CW), BF16),
            pltpu.VMEM((4, 128, 256), F32),
            pltpu.VMEM((4, 128, 256), F32),
            pltpu.VMEM((NC, 3, 8, 256), F32),
            pltpu.VMEM((NC, 3, 8, 256), F32),
            pltpu.VMEM((NR, 3, 8, 256), F32),
            pltpu.VMEM((NC, 3, 8, 256), F32),
            dma((4, 8)),
            dma((4, 8)),
            dma((NC,)),
            dma((NC,)),
            dma((NC,)),
            dma((NB,)),
            dma((NC,)),
            dma((NC + 4,)),
            dma((2 * NC,)),
            dma((NC,)),
            dma((NC,)),
            dma((NR,)),
            dma((NR,)),
            dma((NC,)),
            dma((NC,)),
        ],
        compiler_params=pltpu.CompilerParams(
            collective_id=0, has_side_effects=True, vmem_limit_bytes=56 * 1024 * 1024
        ),
        cost_estimate=pl.CostEstimate(flops=4_000_000_000, bytes_accessed=8_000_000, transcendentals=524_288),
    )(
        block_ids,
        weight_ids,
        col_start,
        coarse,
        noisy,
        cotangent,
        rowsx,
        interp_cols,
        pair_matrix(first_weight),
        pair_matrix(second_weight),
        pair_matrix(adjoint(first_weight[:, :, :, FS:])),
        pair_matrix(adjoint(second_weight)),
    )


def solution(mesh):
    in_specs = (
        P(("row", "col"), None, None),
        P(None, "row", "col"),
        P(None, "row", "col"),
        P(),
        P(),
        P(),
        P(),
        P(("row", "col"), None),
        P(("row", "col"), None),
        P("col"),
    )
    out_specs = (P(None, "row", "col"), P(), P(), P(("row", "col"), None, None))
    return jax.shard_map(local, mesh=mesh, in_specs=in_specs, out_specs=out_specs, check_vma=False)
```

```python
import jax
import jax.numpy as jnp
from jax import lax
from jax.experimental import pallas as pl
from jax.experimental.pallas import tpu as pltpu
from jax.sharding import PartitionSpec as P

F32 = jnp.float32
BF16 = jnp.bfloat16
MESH = pl.DeviceIdType.MESH

NR = 8
NC = 16
HB = 2
K = 4
FR = 32
CH = 64
FS = 16
CIN = 80
CW = 128
NB = NC + 2 * HB

DIRS = ((0, 1), (0, -1), (1, 1), (1, -1), (-1, 1), (-1, -1))
COT, INP, HID, ACT = range(4)


def iota(shape, dim):
    return lax.broadcasted_iota(jnp.int32, shape, dim)


def dot(a, b):
    return jnp.dot(a, b, preferred_element_type=F32)


def dot_nt(a, b):
    return lax.dot_general(a, b, (((1,), (1,)), ((), ())), preferred_element_type=F32)


def one_hot(hit):
    return jnp.where(hit, 1.0, 0.0).astype(BF16)


def permutation():
    i0, i1 = iota((256, 256), 0), iota((256, 256), 1)
    return one_hot((lax.rem(i0, 16) == lax.div(i1, 16)) & (lax.div(i0, 16) == lax.rem(i1, 16)))


def kernel(
    block_ids,
    weight_ids,
    col_start,
    coarse,
    noisy,
    cot,
    rows,
    cols,
    first_w,
    second_w,
    fine_hbm,
    grads_out,
    coarse_out,
    v_cot,
    v_in,
    v_hid,
    v_act,
    g_cot,
    g_act,
    hgrad,
    pre,
    fine,
    wf1,
    wf2,
    wb1,
    wb2,
    edge,
    edge_in,
    edge_got,
    edge_got_in,
    around,
    around_in,
    fix,
    cs,
    slab,
    gath,
    pieces,
    lmat,
    sec,
    pgrad,
    sbuf,
    rbuf,
    rhalo,
    spots,
    acc1,
    acc2,
    gbuf,
    gpart,
    grow,
    x_send,
    x_recv,
    cs_send,
    cs_recv,
    ag_send,
    ag_recv,
    rs_send,
    rs_recv,
    rh_send,
    rh_recv,
    w1_send,
    w1_recv,
    w2_send,
    w2_recv,
    w3_send,
    w3_recv,
    out_sem,
):
    r = lax.axis_index("row")
    c = lax.axis_index("col")
    lane = iota((CH, 128), 1)

    def row_at(d):
        return lax.rem(r + (d + NR), NR)

    def col_at(d):
        return lax.rem(c + (d + NC), NC)

    def remote(src, dst, send, recv, device):
        return pltpu.make_async_remote_copy(
            src_ref=src, dst_ref=dst, send_sem=send, recv_sem=recv, device_id=device, device_id_type=MESH
        )

    barrier = pltpu.get_barrier_semaphore()
    met = [(0, d) for d in range(1, NC)] + [(d, 0) for d in range(1, NR)]
    met += [(dr, dc) for dr in (-1, 1) for dc in (-1, 1)]
    for dr, dc in met:
        pl.semaphore_signal(barrier, inc=1, device_id=(row_at(dr), col_at(dc)), device_id_type=MESH)

    perm = permutation()

    def flip_in(src, dst, c0, h0):
        block = src[c0 : c0 + 16, h0 : h0 + 16, :].reshape(256, 256)
        dst[1 + h0 : 17 + h0, c0 : c0 + 16, :] = dot(perm, block).astype(BF16).reshape(16, 16, 256)

    for c0 in range(0, CH, 16):
        for h0 in range(0, FR, 16):
            flip_in(cot, v_cot, c0, h0)
    for h0 in range(0, FR, 16):
        flip_in(noisy, v_in, 0, h0)

    def place(ins, at):
        return one_hot(iota((ins, 256), 1) == iota((ins, 256), 0) + at)

    wf1[...] = sum(dot(first_w[a].reshape(3 * CH, CIN), place(CIN, a * CIN)) for a in range(3)).astype(BF16)
    for row in range(2):
        flat = sum(dot(second_w[a].reshape(3 * CH, CH), place(CH, (a + row) * CH)) for a in range(3))
        wf2[:, row] = flat.astype(BF16).reshape(3, CH, 256)
    for w, back, ins, skip in ((first_w, wb1, CIN, FS), (second_w, wb2, CH, 0)):
        pick = one_hot(iota((CH, ins), 1) == iota((CH, ins), 0) + skip)
        none = jnp.zeros((CH, ins), BF16)
        for e in range(3):
            taps = [w[2 - a, 2 - e] for a in range(3)]
            back[e, 0] = dot_nt(pick, jnp.concatenate(taps + [none], axis=0)).astype(BF16)
            back[e, 1] = dot_nt(pick, jnp.concatenate([none] + taps, axis=0)).astype(BF16)

    lane256 = iota((FR, 256), 1)
    repeat = one_hot(lax.rem(lax.div(iota((4, 256), 1), 16), 4) == iota((4, 256), 0))
    table = jnp.zeros((FR, 256), F32)
    for k in range(K):
        table = jnp.where(lax.div(lane256, 64) == k, dot(rows[weight_ids[0, k]], repeat), table)
    spread = one_hot(lax.div(iota((512, FR), 0), 16) == iota((512, FR), 1))
    same = lax.rem(iota((512, 256), 0), 16) == lax.rem(iota((512, 256), 1), 16)
    lmat[...] = jnp.where(same, dot(spread, table.astype(BF16)), 0.0).astype(BF16)

    def put_shifted(g, h, t0, t1, count):
        low = iota(t0.shape, 1) == 0
        high = iota(t0.shape, 1) == 127
        r0, r1 = pltpu.roll(t0, 1, 1), pltpu.roll(t1, 1, 1)
        s0, s1 = pltpu.roll(t0, 127, 1), pltpu.roll(t1, 127, 1)

        def put(e, half, value):
            g[pl.ds(h, count), e, :, 128 * half : 128 * half + 128] = value.astype(BF16).reshape(count, CH, 128)

        put(0, 0, jnp.where(high, s1, s0))
        put(0, 1, jnp.where(high, 0.0, s1))
        put(1, 0, t0)
        put(1, 1, t1)
        put(2, 0, jnp.where(low, 0.0, r0))
        put(2, 1, jnp.where(low, r0, r1))

    def shift_cot(h, _):
        put_shifted(g_cot, h, v_cot[h + 1, :, 0:128].astype(F32), v_cot[h + 1, :, 128:256].astype(F32), 1)
        return 0

    bufs = {
        COT: (v_cot, edge.at[0], edge_got.at[0], around.at[0], CH),
        INP: (v_in, edge_in, edge_got_in, around_in, CIN),
        HID: (v_hid, edge.at[1], edge_got.at[1], around.at[1], CH),
        ACT: (v_act, edge.at[2], edge_got.at[2], around.at[2], CH),
    }

    def halo_pack(x):
        v, e, _, _, chans = bufs[x]
        at = iota((chans, 128), 1)

        def pack(h, held):
            left = v[h + 1, :, 0:128].astype(F32)[:, 0:1]
            right = v[h + 1, :, 128:256].astype(F32)[:, 127:128]
            held = jnp.where(at == h, left, held)
            return jnp.where(at == h + 64, right, held)

        e[...] = lax.fori_loop(0, FR, pack, jnp.zeros((chans, 128), F32), unroll=4).astype(BF16)

    def halo_copies(x):
        v, e, got, _, _ = bufs[x]
        copies = [
            remote(e, got.at[i], x_send.at[x, i], x_recv.at[x, i], (row_at(dr), col_at(dc)))
            for i, (dr, dc) in enumerate(DIRS)
        ]
        copies.append(remote(v.at[FR], v.at[0], x_send.at[x, 6], x_recv.at[x, 6], (row_at(1), c)))
        copies.append(remote(v.at[1], v.at[FR + 1], x_send.at[x, 7], x_recv.at[x, 7], (row_at(-1), c)))
        return copies

    def halo_start(x):
        halo_pack(x)
        for copy in halo_copies(x):
            copy.start()

    def halo_finish(x):
        v, _, got, ring, chans = bufs[x]
        for copy in halo_copies(x):
            copy.wait()
        at = iota((chans, 128), 1)

        @pl.when(r == 0)
        def _():
            v[0] = jnp.zeros((chans, 256), BF16)

        @pl.when(r == NR - 1)
        def _():
            v[FR + 1] = jnp.zeros((chans, 256), BF16)

        top = (r > 0).astype(F32)
        bottom = (r < NR - 1).astype(F32)
        west = (c > 0).astype(F32)
        east = (c < NC - 1).astype(F32)

        def side(mid, up, down, first, there):
            a = pltpu.roll(got[mid].astype(F32), 65, 1)
            b = pltpu.roll(got[up].astype(F32), 33, 1) * top
            d = pltpu.roll(got[down].astype(F32), 97, 1) * bottom
            return jnp.where(at == first, b, jnp.where(at == first + FR + 1, d, a)) * there

        both = jnp.where(at < 64, side(0, 2, 4, 0, west), side(1, 3, 5, 64, east))
        ring[0] = both.astype(BF16)
        ring[1] = pltpu.roll(both, 127, 1).astype(BF16)
        ring[2] = pltpu.roll(both, 126, 1).astype(BF16)

    def combine(prod, n, low, high):
        at = iota((n, 128), 1)
        a0, a1 = prod[0:n, 0:128], prod[0:n, 128:256]
        b0, b1 = prod[n : 2 * n, 0:128], prod[n : 2 * n, 128:256]
        d0, d1 = prod[2 * n : 3 * n, 0:128], prod[2 * n : 3 * n, 128:256]
        r0, r1 = pltpu.roll(a0, 1, 1), pltpu.roll(a1, 1, 1)
        s0, s1 = pltpu.roll(d0, 127, 1), pltpu.roll(d1, 127, 1)
        t0 = b0 + jnp.where(at == 0, low, r0) + jnp.where(at == 127, s1, s0)
        t1 = b1 + jnp.where(at == 0, r0, r1) + jnp.where(at == 127, high, s1)
        return t0, t1

    def set_fix(x, left, right):
        ring, chans = bufs[x][3], bufs[x][4]
        cells = ring[...].reshape(3 * chans, 128)
        fix[...] = jnp.where(lane < 64, dot(left, cells), dot(right, cells))

    def fix_low(h):
        return pltpu.roll(fix[...], lax.rem(128 - h, 128), 1)

    def fix_high(h):
        return pltpu.roll(fix[...], 63 - h, 1)

    def set_pair_fix(x, weights):
        set_fix(x, weights[0, 0][:, 0 : 3 * CH], weights[2, 0][:, 0 : 3 * CH])

    def conv_pair(weights, v, p):
        prod = dot(weights[...].reshape(6 * CH, 256), v[pl.ds(2 * p, 4)].reshape(256, 256))
        low = jnp.concatenate([fix_low(2 * p), fix_low(2 * p + 1)], axis=0)
        high = jnp.concatenate([fix_high(2 * p), fix_high(2 * p + 1)], axis=0)
        return combine(prod, 2 * CH, low, high)

    halo_pack(COT)

    pl.semaphore_wait(barrier, len(met))

    cs[c] = jnp.full((8, 128), col_start[0], jnp.int32)

    def cs_copy(d):
        return remote(cs.at[c], cs.at[c], cs_send.at[d], cs_recv.at[c], (r, col_at(d)))

    def cs_arrival(d):
        other = col_at(d)
        return remote(cs.at[other], cs.at[other], cs_send.at[d], cs_recv.at[other], (r, other))

    for d in range(1, NC):
        cs_copy(d).start()
    for copy in halo_copies(COT):
        copy.start()
    lax.fori_loop(0, FR, shift_cot, 0, unroll=2)
    for d in range(1, NC):
        cs_copy(d).wait_send()
        cs_arrival(d).wait_recv()

    def ag_copy(d):
        to = col_at(d)
        return remote(slab.at[to], gath.at[HB + c], ag_send.at[d], ag_recv.at[HB + c], (r, to))

    whole = coarse[...].reshape(256, 256)

    def cut(d, _):
        to = col_at(d)
        start = cs[to][0:1, :]
        pick = one_hot(iota((256, 128), 0) == iota((256, 128), 1) + start)
        slab[to] = dot(whole, pick).astype(BF16).reshape(4, CH, CW)

        @pl.when(d > 0)
        def _():
            ag_copy(d).start()

        @pl.when(d == 0)
        def _():
            gath[HB + c] = slab[c]

        return 0

    lax.fori_loop(0, NC, cut, 0)

    def set_spot(n, _):
        start = cs[n][0:1, :]
        start = jnp.concatenate([start, start], axis=1)
        spots[n] = one_hot(iota((CW, 256), 1) == iota((CW, 256), 0) + start)
        return 0

    lax.fori_loop(0, NC, set_spot, 0)

    halo_finish(COT)
    set_pair_fix(COT, wb2)

    def hidden_grad(p, _):
        t0, t1 = conv_pair(wb2, v_cot, p)
        hgrad[pl.ds(2 * p, 2), :, 0:128] = t0.reshape(2, CH, 128)
        hgrad[pl.ds(2 * p, 2), :, 128:256] = t1.reshape(2, CH, 128)
        return 0

    lax.fori_loop(0, FR // 2, hidden_grad, 0, unroll=2)

    def ag_arrival(slot):
        return remote(slab.at[0], gath.at[slot], ag_send.at[0], ag_recv.at[slot], (r, col_at(1)))

    def pass_on(n):
        src, dst, dr = ((NC, 0, 1), (NC + 1, 1, 1), (HB, NC + HB, -1), (HB + 1, NC + HB + 1, -1))[n]
        return remote(gath.at[src], gath.at[dst], ag_send.at[NC + n], ag_recv.at[dst], (row_at(dr), c))

    for n, at in enumerate((NC - 2, NC - 1, 0, 1)):
        @pl.when(c != at)
        def _():
            ag_arrival(HB + at).wait_recv()

        pass_on(n).start()
    for at in range(2, NC - 2):
        @pl.when(c != at)
        def _():
            ag_arrival(HB + at).wait_recv()

    for d in range(1, NC):
        ag_copy(d).wait_send()
    for n in range(4):
        pass_on(n).wait()

    first_block = r * NC - HB
    for k in range(K):
        piece = gath[jnp.clip(block_ids[0, k] - first_block, 0, NB - 1)]
        for g in range(4):
            pieces[g, 64 * k : 64 * k + 64, :] = piece[:, 16 * g : 16 * g + 16, :].reshape(64, CW)
    for g in range(4):
        sec[:, 16 * g : 16 * g + 16, :] = dot(lmat[...], pieces[g]).astype(BF16).reshape(FR, 16, CW)

    def regrid(q, _):
        flat = sec[pl.ds(4 * q, 4)].reshape(256, CW)
        v_in[pl.ds(1 + 4 * q, 4), FS:CIN, :] = dot(flat, cols[...]).astype(BF16).reshape(4, CH, 256)
        return 0

    lax.fori_loop(0, FR // 4, regrid, 0, unroll=2)

    halo_start(INP)

    def first_row(h, _):
        prod = dot(wf1[:, 0 : 3 * CIN], v_in[pl.ds(h, 3)].reshape(3 * CIN, 256))
        t0, t1 = combine(prod, CH, 0.0, 0.0)
        pre[h, :, 0:128] = t0
        pre[h, :, 128:256] = t1
        return 0

    lax.fori_loop(1, FR - 1, first_row, 0, unroll=2)

    halo_finish(INP)
    first_row(0, 0)
    first_row(FR - 1, 0)
    set_fix(INP, wf1[0:CH, 0 : 3 * CIN], wf1[2 * CH : 3 * CH, 0 : 3 * CIN])

    def activate(h, _):
        t0 = pre[h, :, 0:128] + jnp.where(lane == 0, fix_low(h), 0.0)
        t1 = pre[h, :, 128:256] + jnp.where(lane == 127, fix_high(h), 0.0)
        back = []
        for half, t in ((0, t0), (1, t1)):
            at = slice(128 * half, 128 * half + 128)
            s = 1.0 / (1.0 + jnp.exp(-t))
            v_hid[h + 1, :, at] = (t * s).astype(BF16)
            grad = hgrad[h, :, at] * (s * (1.0 + t * (1.0 - s)))
            v_act[h + 1, :, at] = grad.astype(BF16)
            back.append(grad)
        put_shifted(g_act, h, back[0], back[1], 1)
        return 0

    lax.fori_loop(0, FR, activate, 0, unroll=2)
    halo_start(HID)
    halo_start(ACT)

    edges = ((jnp.where(lane < 64, 1.0, 0.0)).astype(BF16), (jnp.where(lane < 64, 0.0, 1.0)).astype(BF16))

    def edge_terms(x, of):
        ring, chans = bufs[x][3], bufs[x][4]
        mine = bufs[of][1][...]
        both = jnp.concatenate([mine * edges[0], mine * edges[1]], axis=0)
        return dot_nt(both, ring[...].reshape(3 * chans, 128))

    acc1[...] = jnp.zeros(acc1.shape, F32)

    def first_grad(h, _):
        acc1[:, 0 : 3 * CIN] += dot_nt(g_act[h].reshape(3 * CH, 256), v_in[pl.ds(h, 3)].reshape(3 * CIN, 256))
        return 0

    lax.fori_loop(0, FR, first_grad, 0, unroll=2)
    extra = edge_terms(INP, ACT)
    acc1[0:CH, 0 : 3 * CIN] += extra[0:CH]
    acc1[2 * CH :, 0 : 3 * CIN] += extra[CH:]
    gbuf[0:8] = acc1[...].reshape(8, 24, 256)

    halo_finish(HID)
    acc2[...] = jnp.zeros(acc2.shape, F32)

    def second_grad(p, _):
        acc2[...] += dot_nt(g_cot[pl.ds(2 * p, 2)].reshape(6 * CH, 256), v_hid[pl.ds(2 * p, 4)].reshape(256, 256))
        return 0

    lax.fori_loop(0, FR // 2, second_grad, 0, unroll=2)
    extra = edge_terms(HID, COT)
    acc2[0 : 3 * CH, :] += pltpu.roll(acc2[3 * CH :, :], 192, 1)
    acc2[0:CH, 0 : 3 * CH] += extra[0:CH]
    acc2[2 * CH : 3 * CH, 0 : 3 * CH] += extra[CH:]
    gbuf[8:16] = acc2[0 : 3 * CH, :].reshape(8, 24, 256)

    def w1_copy(d):
        to = col_at(d)
        return remote(gbuf.at[to], gpart.at[c], w1_send.at[d], w1_recv.at[c], (r, to))

    for d in range(1, NC):
        w1_copy(d).start()
    gpart[c] = gbuf[c]

    halo_finish(ACT)
    set_pair_fix(ACT, wb1)

    def cond_grad(p, _):
        t0, t1 = conv_pair(wb1, v_act, p)
        fine[pl.ds(2 * p, 2), :, 0:128] = t0.astype(BF16).reshape(2, CH, 128)
        fine[pl.ds(2 * p, 2), :, 128:256] = t1.astype(BF16).reshape(2, CH, 128)
        return 0

    lax.fori_loop(0, FR // 2, cond_grad, 0, unroll=2)

    def section_grad(q, _):
        flat = fine[pl.ds(8 * q, 8)].reshape(512, 256)
        sec[pl.ds(8 * q, 8)] = dot_nt(flat, cols[...]).astype(BF16).reshape(8, CH, CW)
        return 0

    lax.fori_loop(0, FR // 8, section_grad, 0)
    eye = one_hot(iota((256, 256), 0) == iota((256, 256), 1))
    lmat_t = dot_nt(eye, lmat[...]).astype(BF16)
    for g in range(4):
        part = dot(lmat_t, sec[:, 16 * g : 16 * g + 16, :].reshape(512, CW))
        pgrad[:, :, 16 * g : 16 * g + 16, :] = part.reshape(K, 4, 16, CW)

    def contribution(b):
        total = None
        for k in range(K):
            hit = (block_ids[0, k] - first_block == b).astype(F32)
            term = pgrad[k] * hit
            total = term if total is None else total + term
        return total

    def rh_copy(n):
        b, dr = ((0, -1), (1, -1), (NB - 2, 1), (NB - 1, 1))[n]
        return remote(sbuf.at[b], rhalo.at[n], rh_send.at[n], rh_recv.at[n], (row_at(dr), c))

    for n, b in enumerate((0, 1, NB - 2, NB - 1)):
        sbuf[b] = contribution(b).astype(BF16)
        rh_copy(n).start()

    def rs_copy(to):
        return remote(sbuf.at[HB + to], rbuf.at[c], rs_send.at[to], rs_recv.at[c], (r, to))

    def send_block(to):
        @pl.when(to != c)
        def _():
            rs_copy(to).start()

        @pl.when(to == c)
        def _():
            rbuf[c] = sbuf[HB + to]

    def inner(n, _):
        to = 2 + lax.rem(c + n, NC - 4)
        sbuf[HB + to] = contribution(HB + to).astype(BF16)
        send_block(to)
        return 0

    lax.fori_loop(0, 8, inner, 0)
    for n in range(4):
        rh_copy(n).wait()

    def outer(n, _):
        i = lax.rem(n + c, 4)
        to = lax.rem(NC - 2 + i, NC)
        sbuf[HB + to] = (contribution(HB + to) + rhalo[i].astype(F32)).astype(BF16)
        send_block(to)
        inner(8 + n, 0)
        return 0

    lax.fori_loop(0, 4, outer, 0)

    for d in range(1, NC):
        w1_copy(d).wait_send()
        other = col_at(d)
        remote(gbuf.at[other], gpart.at[other], w1_send.at[d], w1_recv.at[other], (r, other)).wait_recv()
    total = gpart[0]
    for n in range(1, NC):
        total = total + gpart[n]
    grow[r] = total

    def w2_copy(d):
        return remote(grow.at[r], grow.at[r], w2_send.at[d], w2_recv.at[r], (row_at(d), c))

    for d in range(1, NR):
        w2_copy(d).start()

    set_pair_fix(HID, wf2)

    def second_level(p, _):
        t0, t1 = conv_pair(wf2, v_hid, p)
        fine[pl.ds(2 * p, 2), :, 0:128] = t0.astype(BF16).reshape(2, CH, 128)
        fine[pl.ds(2 * p, 2), :, 128:256] = t1.astype(BF16).reshape(2, CH, 128)
        return 0

    lax.fori_loop(0, FR // 4, second_level, 0, unroll=2)

    for d in range(1, NR):
        w2_copy(d).wait_send()
        other = row_at(d)
        remote(grow.at[other], grow.at[other], w2_send.at[d], w2_recv.at[other], (other, c)).wait_recv()
    total = grow[0]
    for n in range(1, NR):
        total = total + grow[n]
    grads_out[c] = total

    def w3_copy(d):
        return remote(grads_out.at[c], grads_out.at[c], w3_send.at[d], w3_recv.at[c], (r, col_at(d)))

    for d in range(1, NC):
        w3_copy(d).start()

    lax.fori_loop(FR // 4, FR // 2, second_level, 0, unroll=2)
    out = pltpu.make_async_copy(fine, fine_hbm, out_sem)
    out.start()

    for n in range(NC):
        @pl.when(n != c)
        def _():
            rs_copy(n).wait_send()
            remote(sbuf.at[0], rbuf.at[n], rs_send.at[n], rs_recv.at[n], (r, n)).wait_recv()

    def add(q, _):
        flat = [rbuf[4 * q + n].reshape(256, CW) for n in range(4)]
        spot = spots[pl.ds(4 * q, 4)].reshape(4 * CW, 256)
        coarse_out[...] += dot(jnp.concatenate(flat, axis=1), spot).reshape(4, CH, 256)
        return 0

    coarse_out[...] = jnp.zeros((4, CH, 256), F32)
    lax.fori_loop(0, NC // 4, add, 0)

    for d in range(1, NC):
        w3_copy(d).wait_send()
        other = col_at(d)
        remote(grads_out.at[other], grads_out.at[other], w3_send.at[d], w3_recv.at[other], (r, other)).wait_recv()
    out.wait()


def results(fine, grads, block, fine_out, first_out, second_out, coarse_out):
    perm = permutation()
    for h0 in range(0, FR, 16):
        rows = fine[h0 : h0 + 16].reshape(256, 256)
        fine_out[:, h0 : h0 + 16, :] = dot(perm, rows).astype(BF16).reshape(16, 16, 256)

    @pl.when(pl.program_id(0) == 0)
    def _():
        coarse_out[...] = block[...]
        first = grads[0:8].reshape(3 * CH, 256)
        second = grads[8:16].reshape(3 * CH, 256)
        for a in range(3):
            for e in range(3):
                first_out[a, e] = first[e * CH : (e + 1) * CH, a * CIN : (a + 1) * CIN]
                second_out[a, e] = second[e * CH : (e + 1) * CH, a * CH : (a + 1) * CH]


def local(
    coarse,
    noisy,
    cotangent,
    interp_rows,
    interp_cols,
    first_weight,
    second_weight,
    block_ids,
    weight_ids,
    col_start,
):
    smem = pl.BlockSpec(memory_space=pltpu.SMEM)
    vmem = pl.BlockSpec(memory_space=pltpu.VMEM)
    dma = pltpu.SemaphoreType.DMA
    fine, grads, block = pl.pallas_call(
        kernel,
        out_shape=(
            jax.ShapeDtypeStruct((FR, CH, 256), BF16),
            jax.ShapeDtypeStruct((NC, 24, 256), F32),
            jax.ShapeDtypeStruct((4, CH, 256), F32),
        ),
        in_specs=[smem] * 3 + [vmem] * 7,
        out_specs=(pl.BlockSpec(memory_space=pl.ANY), vmem, vmem),
        scratch_shapes=[
            pltpu.VMEM((FR + 2, CH, 256), BF16),
            pltpu.VMEM((FR + 2, CIN, 256), BF16),
            pltpu.VMEM((FR + 2, CH, 256), BF16),
            pltpu.VMEM((FR + 2, CH, 256), BF16),
            pltpu.VMEM((FR, 3, CH, 256), BF16),
            pltpu.VMEM((FR, 3, CH, 256), BF16),
            pltpu.VMEM((FR, CH, 256), F32),
            pltpu.VMEM((FR, CH, 256), F32),
            pltpu.VMEM((FR, CH, 256), BF16),
            pltpu.VMEM((3 * CH, 256), BF16),
            pltpu.VMEM((3, 2, CH, 256), BF16),
            pltpu.VMEM((3, 2, CH, 256), BF16),
            pltpu.VMEM((3, 2, CH, 256), BF16),
            pltpu.VMEM((3, CH, 128), BF16),
            pltpu.VMEM((CIN, 128), BF16),
            pltpu.VMEM((3, 6, CH, 128), BF16),
            pltpu.VMEM((6, CIN, 128), BF16),
            pltpu.VMEM((3, 3, CH, 128), BF16),
            pltpu.VMEM((3, CIN, 128), BF16),
            pltpu.VMEM((CH, 128), F32),
            pltpu.VMEM((NC, 8, 128), jnp.int32),
            pltpu.VMEM((NC, 4, CH, CW), BF16),
            pltpu.VMEM((NB, 4, CH, CW), BF16),
            pltpu.VMEM((4, 256, CW), BF16),
            pltpu.VMEM((512, 256), BF16),
            pltpu.VMEM((FR, CH, CW), BF16),
            pltpu.VMEM((K, 4, CH, CW), F32),
            pltpu.VMEM((NB, 4, CH, CW), BF16),
            pltpu.VMEM((NC, 4, CH, CW), BF16),
            pltpu.VMEM((4, 4, CH, CW), BF16),
            pltpu.VMEM((NC, CW, 256), BF16),
            pltpu.VMEM((3 * CH, 256), F32),
            pltpu.VMEM((6 * CH, 256), F32),
            pltpu.VMEM((NC, 24, 256), F32),
            pltpu.VMEM((NC, 24, 256), F32),
            pltpu.VMEM((NR, 24, 256), F32),
            dma((4, 8)),
            dma((4, 8)),
            dma((NC,)),
            dma((NC,)),
            dma((NC + 4,)),
            dma((NB,)),
            dma((NC,)),
            dma((NC,)),
            dma((4,)),
            dma((4,)),
            dma((NC,)),
            dma((NC,)),
            dma((NR,)),
            dma((NR,)),
            dma((NC,)),
            dma((NC,)),
            dma,
        ],
        compiler_params=pltpu.CompilerParams(
            collective_id=0, has_side_effects=True, vmem_limit_bytes=56 * 1024 * 1024
        ),
        cost_estimate=pl.CostEstimate(flops=4_000_000_000, bytes_accessed=8_000_000, transcendentals=524_288),
    )(
        block_ids,
        weight_ids,
        col_start,
        coarse,
        noisy,
        cotangent,
        interp_rows,
        interp_cols,
        first_weight,
        second_weight,
    )
    whole = lambda *shape: pl.BlockSpec(shape, lambda g: (0,) * len(shape))
    return pl.pallas_call(
        results,
        grid=(CH // 16,),
        out_shape=(
            jax.ShapeDtypeStruct((CH, FR, 256), BF16),
            jax.ShapeDtypeStruct((3, 3, CH, CIN), F32),
            jax.ShapeDtypeStruct((3, 3, CH, CH), F32),
            jax.ShapeDtypeStruct((4, CH, 256), F32),
        ),
        in_specs=[
            pl.BlockSpec((FR, 16, 256), lambda g: (0, g, 0)),
            whole(NC, 24, 256),
            whole(4, CH, 256),
        ],
        out_specs=(
            pl.BlockSpec((16, FR, 256), lambda g: (g, 0, 0)),
            whole(3, 3, CH, CIN),
            whole(3, 3, CH, CH),
            whole(4, CH, 256),
        ),
        compiler_params=pltpu.CompilerParams(vmem_limit_bytes=32 * 1024 * 1024),
        cost_estimate=pl.CostEstimate(flops=270_000_000, bytes_accessed=4_000_000, transcendentals=0),
    )(fine, grads, block)


def solution(mesh):
    in_specs = (
        P(("row", "col"), None, None),
        P(None, "row", "col"),
        P(None, "row", "col"),
        P(),
        P(),
        P(),
        P(),
        P(("row", "col"), None),
        P(("row", "col"), None),
        P("col"),
    )
    out_specs = (P(None, "row", "col"), P(), P(), P(("row", "col"), None, None))
    return jax.shard_map(local, mesh=mesh, in_specs=in_specs, out_specs=out_specs, check_vma=False)
```

```python
import jax
import jax.numpy as jnp
from jax import lax
from jax.experimental import pallas as pl
from jax.experimental.pallas import tpu as pltpu
from jax.sharding import PartitionSpec as P

F32 = jnp.float32
BF16 = jnp.bfloat16
MESH = pl.DeviceIdType.MESH

NR = 8
NC = 16
HB = 2
K = 4
FR = 32
CH = 64
FS = 16
CIN = 80
CW = 128
NB = NC + 2 * HB

PEERS = (
    ((2, 2), (1, 2), (2, 1), (3, 2), (2, 3), (1, 1), (3, 3), (1, 3))
    + ((3, 1), (0, 2), (2, 0), (0, 1), (1, 0), (0, 3), (3, 0))
)
COT, INP, HID, ACT = range(4)


def iota(shape, dim):
    return lax.broadcasted_iota(jnp.int32, shape, dim)


def dot(a, b):
    return jnp.dot(a, b, preferred_element_type=F32)


def dot_nt(a, b):
    return lax.dot_general(a, b, (((1,), (1,)), ((), ())), preferred_element_type=F32)


def dot_tn(a, b):
    return lax.dot_general(a, b, (((0,), (0,)), ((), ())), preferred_element_type=F32)


def one_hot(hit):
    return jnp.where(hit, 1.0, 0.0).astype(BF16)


def permutation():
    i0, i1 = iota((256, 256), 0), iota((256, 256), 1)
    return one_hot((lax.rem(i0, 16) == lax.div(i1, 16)) & (lax.div(i0, 16) == lax.rem(i1, 16)))


def kernel(
    block_ids,
    weight_ids,
    col_start,
    *rest,
):
    hbm, rest = rest[:7], rest[7:]
    body(block_ids, weight_ids, col_start, hbm, *rest)


def body(
    block_ids,
    weight_ids,
    col_start,
    hbm,
    fine_hbm,
    grads_out,
    coarse_out,
    coarse,
    noisy,
    cot,
    rows,
    cols,
    first_w,
    second_w,
    v_cot,
    v_in,
    v_hid,
    v_act,
    g_cot,
    g_act,
    hgrad,
    pre,
    fine,
    wf1,
    wf2,
    wb1,
    wb2,
    edge,
    edge_in,
    edge_got,
    edge_got_in,
    around,
    around_in,
    fix,
    cs,
    slab,
    gath,
    pieces,
    lmat,
    sec,
    pgrad,
    sbuf,
    rbuf,
    rhalo,
    spots,
    acc1,
    acc2,
    gbuf,
    gpart,
    grow,
    x_send,
    x_recv,
    cs_send,
    cs_recv,
    ag_send,
    ag_recv,
    rs_send,
    rs_recv,
    rh_send,
    rh_recv,
    w1_send,
    w1_recv,
    w2_send,
    w2_recv,
    w3_send,
    w3_recv,
    out_sem,
    in_sem,
):
    r = lax.axis_index("row")
    c = lax.axis_index("col")
    lane = iota((CH, 128), 1)

    def row_at(d):
        return lax.rem(r + (d + NR), NR)

    def col_at(d):
        return lax.rem(c + (d + NC), NC)

    def peer(n):
        dx, dy = PEERS[n]
        return lax.rem(lax.div(c, 4) + dx, 4) * 4 + lax.rem(c + dy, 4)

    def source(n):
        dx, dy = PEERS[n]
        return lax.rem(lax.div(c, 4) + 4 - dx, 4) * 4 + lax.rem(c + 4 - dy, 4)

    def remote(src, dst, send, recv, device):
        return pltpu.make_async_remote_copy(
            src_ref=src, dst_ref=dst, send_sem=send, recv_sem=recv, device_id=device, device_id_type=MESH
        )

    barrier = pltpu.get_barrier_semaphore()
    met = [(0, d) for d in range(1, NC)] + [(d, 0) for d in range(1, NR)]
    for dr, dc in met:
        pl.semaphore_signal(barrier, inc=1, device_id=(row_at(dr), col_at(dc)), device_id_type=MESH)

    fetched = [
        pltpu.make_async_copy(src, dst, in_sem.at[n])
        for n, (src, dst) in enumerate(zip(hbm, (coarse, noisy, cot, rows, cols, first_w, second_w)))
    ]
    for n in (2, 1, 5, 6, 3, 0, 4):
        fetched[n].start()
    for copy in fetched:
        copy.wait()
    perm = permutation()

    def flip_in(src, dst, c0, h0):
        block = src[c0 : c0 + 16, h0 : h0 + 16, :].reshape(256, 256)
        dst[1 + h0 : 17 + h0, c0 : c0 + 16, :] = dot(perm, block).astype(BF16).reshape(16, 16, 256)

    for c0 in range(0, CH, 16):
        for h0 in range(0, FR, 16):
            flip_in(cot, v_cot, c0, h0)
    for h0 in range(0, FR, 16):
        flip_in(noisy, v_in, 0, h0)

    def place(ins, at):
        return one_hot(iota((ins, 256), 1) == iota((ins, 256), 0) + at)

    wf1[...] = sum(dot(first_w[a].reshape(3 * CH, CIN), place(CIN, a * CIN)) for a in range(3)).astype(BF16)
    for row in range(2):
        flat = sum(dot(second_w[a].reshape(3 * CH, CH), place(CH, (a + row) * CH)) for a in range(3))
        wf2[:, row] = flat.astype(BF16).reshape(3, CH, 256)
    for w, back, ins, skip in ((first_w, wb1, CIN, FS), (second_w, wb2, CH, 0)):
        pick = one_hot(iota((CH, ins), 1) == iota((CH, ins), 0) + skip)
        none = jnp.zeros((CH, ins), BF16)
        for e in range(3):
            taps = [w[2 - a, 2 - e] for a in range(3)]
            back[e, 0] = dot_nt(pick, jnp.concatenate(taps + [none], axis=0)).astype(BF16)
            back[e, 1] = dot_nt(pick, jnp.concatenate([none] + taps, axis=0)).astype(BF16)

    lane256 = iota((FR, 256), 1)
    repeat = one_hot(lax.rem(lax.div(iota((4, 256), 1), 16), 4) == iota((4, 256), 0))
    table = jnp.zeros((FR, 256), F32)
    for k in range(K):
        table = jnp.where(lax.div(lane256, 64) == k, dot_tn(rows[weight_ids[0, k]], repeat), table)
    spread = one_hot(lax.div(iota((512, FR), 0), 16) == iota((512, FR), 1))
    same = lax.rem(iota((512, 256), 0), 16) == lax.rem(iota((512, 256), 1), 16)
    lmat[...] = jnp.where(same, dot(spread, table.astype(BF16)), 0.0).astype(BF16)

    def put_shifted(g, h, t0, t1, count):
        low = iota(t0.shape, 1) == 0
        high = iota(t0.shape, 1) == 127
        r0, r1 = pltpu.roll(t0, 1, 1), pltpu.roll(t1, 1, 1)
        s0, s1 = pltpu.roll(t0, 127, 1), pltpu.roll(t1, 127, 1)

        def put(e, half, value):
            g[pl.ds(h, count), e, :, 128 * half : 128 * half + 128] = value.astype(BF16).reshape(count, CH, 128)

        put(0, 0, jnp.where(high, s1, s0))
        put(0, 1, jnp.where(high, 0.0, s1))
        put(1, 0, t0)
        put(1, 1, t1)
        put(2, 0, jnp.where(low, 0.0, r0))
        put(2, 1, jnp.where(low, r0, r1))

    def shift_cot(h, _):
        put_shifted(g_cot, h, v_cot[h + 1, :, 0:128].astype(F32), v_cot[h + 1, :, 128:256].astype(F32), 1)
        return 0

    bufs = {
        COT: (v_cot, edge.at[0], edge_got.at[0], around.at[0], CH),
        INP: (v_in, edge_in, edge_got_in, around_in, CIN),
        HID: (v_hid, edge.at[1], edge_got.at[1], around.at[1], CH),
        ACT: (v_act, edge.at[2], edge_got.at[2], around.at[2], CH),
    }

    def halo_pack(x):
        v, e, _, _, chans = bufs[x]
        at = iota((chans, 128), 1)

        def pack(h, held):
            t0 = v[h + 1, :, 0:128].astype(F32)
            t1 = v[h + 1, :, 128:256].astype(F32)
            ends = pltpu.roll(jnp.where(at == 127, t1, t0), 2 * h, 1)
            return jnp.where(((at - 2 * h + 1) & 127) < 2, ends, held)

        e[...] = lax.fori_loop(0, FR, pack, jnp.zeros((chans, 128), F32), unroll=8).astype(BF16)

    def halo_copies(x, far):
        v, e, got, _, _ = bufs[x]

        def one(n, src, dst, dr, dc):
            return remote(src, dst, x_send.at[x, n], x_recv.at[x, n], (row_at(dr), col_at(dc)))

        if far:
            return [
                one(2, got.at[0], got.at[2], 1, 0),
                one(3, got.at[1], got.at[3], 1, 0),
                one(4, got.at[0], got.at[4], -1, 0),
                one(5, got.at[1], got.at[5], -1, 0),
            ]
        return [
            one(0, e, got.at[0], 0, 1),
            one(1, e, got.at[1], 0, -1),
            one(6, v.at[FR], v.at[0], 1, 0),
            one(7, v.at[1], v.at[FR + 1], -1, 0),
        ]

    def halo_start(x):
        halo_pack(x)
        for copy in halo_copies(x, False):
            copy.start()

    def set_ring(x, corners):
        _, _, got, ring, chans = bufs[x]
        at = iota((chans, 128), 1)
        top = (r > 0).astype(F32)
        bottom = (r < NR - 1).astype(F32)
        west = (c > 0).astype(F32)
        east = (c < NC - 1).astype(F32)

        def side(mid, up, down, by, by_corner, first, there):
            cells = pltpu.roll(got[mid].astype(F32), by, 1)
            if corners:
                b = pltpu.roll(got[up].astype(F32), by_corner, 1) * top
                d = pltpu.roll(got[down].astype(F32), by_corner, 1) * bottom
                last = (first + 2 * FR + 2) % 128
                cells = jnp.where(at == first, b, jnp.where(at == last, d, cells))
            return cells * there

        both = jnp.where(lax.rem(at, 2) == 0, side(0, 2, 4, 3, 67, 0, west), side(1, 3, 5, 1, 65, 127, east))
        ring[0] = both.astype(BF16)
        ring[1] = pltpu.roll(both, 126, 1).astype(BF16)
        ring[2] = pltpu.roll(both, 124, 1).astype(BF16)

    def halo_near(x):
        v, chans = bufs[x][0], bufs[x][4]
        near = halo_copies(x, False)
        for copy in near[:2]:
            copy.wait()
        for copy in halo_copies(x, True):
            copy.start()
        for copy in near[2:]:
            copy.wait()

        @pl.when(r == 0)
        def _():
            v[0] = jnp.zeros((chans, 256), BF16)

        @pl.when(r == NR - 1)
        def _():
            v[FR + 1] = jnp.zeros((chans, 256), BF16)

    def halo_corners(x):
        for copy in halo_copies(x, True):
            copy.wait()
        set_ring(x, True)

    def combine(prod, n, ends):
        at = iota((n, 128), 1)
        a0, a1 = prod[0:n, 0:128], prod[0:n, 128:256]
        b0, b1 = prod[n : 2 * n, 0:128], prod[n : 2 * n, 128:256]
        d0, d1 = prod[2 * n : 3 * n, 0:128], prod[2 * n : 3 * n, 128:256]
        r0, r1 = pltpu.roll(a0, 1, 1), pltpu.roll(a1, 1, 1)
        s0, s1 = pltpu.roll(d0, 127, 1), pltpu.roll(d1, 127, 1)
        t0 = b0 + jnp.where(at == 0, ends, r0) + jnp.where(at == 127, s1, s0)
        t1 = b1 + jnp.where(at == 0, r0, r1) + jnp.where(at == 127, ends, s1)
        return t0, t1

    def set_fix(x, left, right):
        ring, chans = bufs[x][3], bufs[x][4]
        cells = ring[...].reshape(3 * chans, 128)
        fix[...] = jnp.where(lax.rem(lane, 2) == 0, dot(left, cells), dot(right, cells))

    def fix_of(h):
        return pltpu.roll(fix[...], lax.rem(128 - 2 * h, 128), 1)

    def set_pair_fix(x, weights):
        set_fix(x, weights[0, 0][:, 0 : 3 * CH], weights[2, 0][:, 0 : 3 * CH])

    def conv_pair(weights, v, p):
        prod = dot(weights[...].reshape(6 * CH, 256), v[pl.ds(2 * p, 4)].reshape(256, 256))
        ends = jnp.concatenate([fix_of(2 * p), fix_of(2 * p + 1)], axis=0)
        return combine(prod, 2 * CH, ends)

    halo_pack(COT)

    pl.semaphore_wait(barrier, len(met))

    cs[c] = jnp.full((8, 128), col_start[0], jnp.int32)

    def cs_copy(d):
        return remote(cs.at[c], cs.at[c], cs_send.at[d], cs_recv.at[c], (r, col_at(d)))

    def cs_arrival(d):
        other = col_at(d)
        return remote(cs.at[other], cs.at[other], cs_send.at[d], cs_recv.at[other], (r, other))

    for d in range(1, NC):
        cs_copy(d).start()
    for copy in halo_copies(COT, False):
        copy.start()
    lax.fori_loop(0, FR, shift_cot, 0, unroll=4)
    for d in range(1, NC):
        cs_copy(d).wait_send()
        cs_arrival(d).wait_recv()

    def ag_copy(n):
        to = peer(n)
        return remote(slab.at[to], gath.at[HB + c], ag_send.at[n], ag_recv.at[HB + c], (r, to))

    whole = coarse[...].reshape(256, 256)

    def cut(to):
        pick = one_hot(iota((256, 128), 0) == iota((256, 128), 1) + cs[to][0:1, :])
        return dot(whole, pick).astype(BF16).reshape(4, CH, CW)

    for n in range(NC - 1):
        slab[peer(n)] = cut(peer(n))
        ag_copy(n).start()
    gath[HB + c] = cut(c)

    def set_spot(n, _):
        start = cs[n][0:1, :]
        start = jnp.concatenate([start, start], axis=1)
        spots[n] = one_hot(iota((CW, 256), 1) == iota((CW, 256), 0) + start)
        return 0

    lax.fori_loop(0, NC, set_spot, 0)

    halo_near(COT)
    halo_corners(COT)
    set_pair_fix(COT, wb2)

    def hidden_grad(p, _):
        t0, t1 = conv_pair(wb2, v_cot, p)
        hgrad[pl.ds(2 * p, 2), :, 0:128] = t0.reshape(2, CH, 128)
        hgrad[pl.ds(2 * p, 2), :, 128:256] = t1.reshape(2, CH, 128)
        return 0

    lax.fori_loop(0, FR // 2, hidden_grad, 0, unroll=4)

    def ag_arrival(slot):
        return remote(slab.at[0], gath.at[slot], ag_send.at[0], ag_recv.at[slot], (r, col_at(1)))

    def pass_on(n):
        src, dst, dr = ((NC, 0, 1), (NC + 1, 1, 1), (HB, NC + HB, -1), (HB + 1, NC + HB + 1, -1))[n]
        return remote(gath.at[src], gath.at[dst], ag_send.at[NC + n], ag_recv.at[dst], (row_at(dr), c))

    for n, at in enumerate((NC - 2, NC - 1, 0, 1)):
        @pl.when(c != at)
        def _():
            ag_arrival(HB + at).wait_recv()

        pass_on(n).start()
    for at in range(2, NC - 2):
        @pl.when(c != at)
        def _():
            ag_arrival(HB + at).wait_recv()

    for n in range(NC - 1):
        ag_copy(n).wait_send()
    for n in range(4):
        pass_on(n).wait()

    first_block = r * NC - HB
    for k in range(K):
        piece = gath[jnp.clip(block_ids[0, k] - first_block, 0, NB - 1)]
        for g in range(4):
            pieces[g, 64 * k : 64 * k + 64, :] = piece[:, 16 * g : 16 * g + 16, :].reshape(64, CW)
    for g in range(4):
        sec[:, 16 * g : 16 * g + 16, :] = dot(lmat[...], pieces[g]).astype(BF16).reshape(FR, 16, CW)

    def regrid(q, _):
        flat = sec[pl.ds(4 * q, 4)].reshape(256, CW)
        v_in[pl.ds(1 + 4 * q, 4), FS:CIN, :] = dot(flat, cols[...]).astype(BF16).reshape(4, CH, 256)
        return 0

    lax.fori_loop(0, FR // 4, regrid, 0, unroll=4)

    halo_start(INP)

    def first_row(h, _):
        prod = dot(wf1[:, 0 : 3 * CIN], v_in[pl.ds(h, 3)].reshape(3 * CIN, 256))
        t0, t1 = combine(prod, CH, 0.0)
        pre[h, :, 0:128] = t0
        pre[h, :, 128:256] = t1
        return 0

    lax.fori_loop(1, FR - 1, first_row, 0, unroll=4)

    halo_near(INP)
    set_ring(INP, False)
    first_row(0, 0)
    first_row(FR - 1, 0)

    def set_first_fix():
        set_fix(INP, wf1[0:CH, 0 : 3 * CIN], wf1[2 * CH : 3 * CH, 0 : 3 * CIN])

    set_first_fix()

    def activate(h, _):
        ends = fix_of(h)
        t0 = pre[h, :, 0:128] + jnp.where(lane == 0, ends, 0.0)
        t1 = pre[h, :, 128:256] + jnp.where(lane == 127, ends, 0.0)
        back = []
        for half, t in ((0, t0), (1, t1)):
            at = slice(128 * half, 128 * half + 128)
            s = 1.0 / (1.0 + jnp.exp(-t))
            v_hid[h + 1, :, at] = (t * s).astype(BF16)
            grad = hgrad[h, :, at] * (s * (1.0 + t * (1.0 - s)))
            v_act[h + 1, :, at] = grad.astype(BF16)
            back.append(grad)
        put_shifted(g_act, h, back[0], back[1], 1)
        return 0

    lax.fori_loop(1, FR - 1, activate, 0, unroll=4)
    halo_corners(INP)
    set_first_fix()
    activate(0, 0)
    activate(FR - 1, 0)

    halo_start(ACT)
    halo_start(HID)

    edges = (one_hot(lax.rem(lane, 2) == 0), one_hot(lax.rem(lane, 2) == 1))

    def edge_terms(x, of):
        ring, chans = bufs[x][3], bufs[x][4]
        mine = bufs[of][1][...]
        both = jnp.concatenate([mine * edges[0], mine * edges[1]], axis=0)
        return dot_nt(both, ring[...].reshape(3 * chans, 128))

    acc1[...] = jnp.zeros(acc1.shape, F32)

    def first_grad(h, _):
        acc1[:, 0 : 3 * CIN] += dot_nt(g_act[h].reshape(3 * CH, 256), v_in[pl.ds(h, 3)].reshape(3 * CIN, 256))
        return 0

    lax.fori_loop(0, FR, first_grad, 0, unroll=4)

    extra = edge_terms(INP, ACT)
    acc1[0:CH, 0 : 3 * CIN] += extra[0:CH]
    acc1[2 * CH :, 0 : 3 * CIN] += extra[CH:]

    def w1_copy(which, n):
        to = peer(n)
        return remote(gbuf.at[which, to], gpart.at[which, c], w1_send.at[which, n], w1_recv.at[which, c], (r, to))

    def sum_row(which, acc):
        for half in range(2):
            rows = acc[0 : 3 * CH, 128 * half : 128 * half + 128]
            gbuf[which, 8 * half : 8 * half + 8] = rows.reshape(8, 24, 128)
        for n in range(NC - 1):
            w1_copy(which, n).start()
        gpart[which, c] = gbuf[which, c]

    sum_row(0, acc1)

    halo_near(ACT)
    halo_near(HID)
    halo_corners(HID)
    acc2[...] = jnp.zeros(acc2.shape, F32)

    def second_grad(p, _):
        acc2[...] += dot_nt(g_cot[pl.ds(2 * p, 2)].reshape(6 * CH, 256), v_hid[pl.ds(2 * p, 4)].reshape(256, 256))
        return 0

    lax.fori_loop(0, FR // 2, second_grad, 0, unroll=4)
    extra = edge_terms(HID, COT)
    acc2[0 : 3 * CH, :] += pltpu.roll(acc2[3 * CH :, :], 192, 1)
    acc2[0:CH, 0 : 3 * CH] += extra[0:CH]
    acc2[2 * CH : 3 * CH, 0 : 3 * CH] += extra[CH:]
    sum_row(1, acc2)

    def w2_copy(which, d):
        return remote(
            grow.at[which, r], grow.at[which, r], w2_send.at[which, d], w2_recv.at[which, r], (row_at(d), c)
        )

    def w2_arrival(which, d):
        there = grow.at[which, row_at(d)]
        return remote(there, there, w2_send.at[which, d], w2_recv.at[which, row_at(d)], (row_at(d), c))

    def w3_copy(which, n):
        here = grads_out.at[which, c]
        return remote(here, here, w3_send.at[which, n], w3_recv.at[which, c], (r, peer(n)))

    def w3_arrival(which, n):
        there = grads_out.at[which, source(n)]
        return remote(there, there, w3_send.at[which, n], w3_recv.at[which, source(n)], (r, source(n)))

    def sum_col(which):
        for n in range(NC - 1):
            w1_copy(which, n).wait_send()
            there = gpart.at[which, source(n)]
            remote(there, there, w1_send.at[which, n], w1_recv.at[which, source(n)], (r, source(n))).wait_recv()
        total = gpart[which, 0]
        for n in range(1, NC):
            total = total + gpart[which, n]
        grow[which, r] = total
        for d in range(1, NR):
            w2_copy(which, d).start()

    def spread_sum(which):
        for d in range(1, NR):
            w2_copy(which, d).wait_send()
            w2_arrival(which, d).wait_recv()
        total = grow[which, 0]
        for n in range(1, NR):
            total = total + grow[which, n]
        grads_out[which, c] = total
        for n in range(NC - 1):
            w3_copy(which, n).start()

    set_ring(ACT, False)
    set_pair_fix(ACT, wb1)

    def cond_grad(p, _):
        t0, t1 = conv_pair(wb1, v_act, p)
        fine[pl.ds(2 * p, 2), :, 0:128] = t0.astype(BF16).reshape(2, CH, 128)
        fine[pl.ds(2 * p, 2), :, 128:256] = t1.astype(BF16).reshape(2, CH, 128)
        return 0

    lax.fori_loop(1, FR // 2 - 1, cond_grad, 0, unroll=4)
    halo_corners(ACT)
    set_pair_fix(ACT, wb1)
    cond_grad(0, 0)
    cond_grad(FR // 2 - 1, 0)

    def section_grad(q, _):
        flat = fine[pl.ds(8 * q, 8)].reshape(512, 256)
        sec[pl.ds(8 * q, 8)] = dot_nt(flat, cols[...]).astype(BF16).reshape(8, CH, CW)
        return 0

    lax.fori_loop(0, FR // 8, section_grad, 0)
    eye = one_hot(iota((256, 256), 0) == iota((256, 256), 1))
    lmat_t = dot_nt(eye, lmat[...]).astype(BF16)
    for g in range(4):
        part = dot(lmat_t, sec[:, 16 * g : 16 * g + 16, :].reshape(512, CW))
        pgrad[:, :, 16 * g : 16 * g + 16, :] = part.reshape(K, 4, 16, CW)

    def contribution(b):
        total = None
        for k in range(K):
            hit = (block_ids[0, k] - first_block == b).astype(F32)
            term = pgrad[k] * hit
            total = term if total is None else total + term
        return total

    def rh_copy(n):
        b, dr = ((0, -1), (1, -1), (NB - 2, 1), (NB - 1, 1))[n]
        return remote(sbuf.at[b], rhalo.at[n], rh_send.at[n], rh_recv.at[n], (row_at(dr), c))

    for n, b in enumerate((0, 1, NB - 2, NB - 1)):
        sbuf[b] = contribution(b).astype(BF16)
        rh_copy(n).start()

    def rs_copy(n):
        to = peer(n)
        return remote(sbuf.at[HB + to], rbuf.at[c], rs_send.at[n], rs_recv.at[c], (r, to))

    def is_inner(to):
        return (to >= HB) & (to < NC - HB)

    def send_inner(n):
        to = peer(n)

        @pl.when(is_inner(to))
        def _():
            sbuf[HB + to] = contribution(HB + to).astype(BF16)
            rs_copy(n).start()

    def send_outer(n):
        @pl.when(jnp.logical_not(is_inner(peer(n))))
        def _():
            rs_copy(n).start()

    for n in range(8):
        send_inner(n)
    for n, b in enumerate((NC, NC + 1, HB, HB + 1)):
        rh_copy(n).wait_recv()
        sbuf[b] = (contribution(b) + rhalo[n].astype(F32)).astype(BF16)
    for n in range(8, NC - 1):
        send_inner(n)
        send_outer(n)
        send_outer(n - 8)
    send_outer(7)

    @pl.when(is_inner(c))
    def _():
        sbuf[HB + c] = contribution(HB + c).astype(BF16)

    rbuf[c] = sbuf[HB + c]

    sum_col(0)
    sum_col(1)
    set_pair_fix(HID, wf2)

    def second_level(p, _):
        t0, t1 = conv_pair(wf2, v_hid, p)
        fine[pl.ds(2 * p, 2), :, 0:128] = t0.astype(BF16).reshape(2, CH, 128)
        fine[pl.ds(2 * p, 2), :, 128:256] = t1.astype(BF16).reshape(2, CH, 128)
        return 0

    lax.fori_loop(0, FR // 4, second_level, 0, unroll=4)
    spread_sum(0)
    spread_sum(1)
    lax.fori_loop(FR // 4, FR // 2, second_level, 0, unroll=4)
    out = pltpu.make_async_copy(fine, fine_hbm, out_sem)
    out.start()

    for n in range(NC - 1):
        rs_copy(n).wait_send()
        there = rbuf.at[source(n)]
        remote(there, there, rs_send.at[n], rs_recv.at[source(n)], (r, source(n))).wait_recv()

    def add(q, _):
        flat = [rbuf[4 * q + n].reshape(256, CW) for n in range(4)]
        spot = spots[pl.ds(4 * q, 4)].reshape(4 * CW, 256)
        coarse_out[...] += dot(jnp.concatenate(flat, axis=1), spot).reshape(4, CH, 256)
        return 0

    coarse_out[...] = jnp.zeros((4, CH, 256), F32)
    lax.fori_loop(0, NC // 4, add, 0)

    for n in range(4):
        rh_copy(n).wait_send()
    for which in range(2):
        for n in range(NC - 1):
            w3_copy(which, n).wait_send()
            w3_arrival(which, n).wait_recv()
    out.wait()


def results(
    fine, grads, block, fine_out, first_out, second_out, coarse_out, rows, turned, sums, held, first, second, sem
):
    fetched = pltpu.make_async_copy(block, held, sem.at[0])
    moved = pltpu.make_async_copy(held, coarse_out, sem.at[8])
    arrivals = [
        pltpu.make_async_copy(fine.at[pl.ds(16 * n, 16)], rows.at[pl.ds(16 * n, 16)], sem.at[1 + n]) for n in range(2)
    ]
    summed = pltpu.make_async_copy(grads, sums, sem.at[3])
    leaving = [
        pltpu.make_async_copy(
            turned.at[:, pl.ds(16 * n, 16), :], fine_out.at[:, pl.ds(16 * n, 16), :], sem.at[4 + n]
        )
        for n in range(2)
    ]
    for copy in arrivals:
        copy.start()
    summed.start()
    fetched.start()
    perm = permutation()
    for n in range(2):
        arrivals[n].wait()
        for c0 in range(0, CH, 16):
            flat = rows[16 * n : 16 * n + 16, c0 : c0 + 16, :].reshape(256, 256)
            turned[c0 : c0 + 16, 16 * n : 16 * n + 16, :] = dot(perm, flat).astype(BF16).reshape(16, 16, 256)
        leaving[n].start()
    fetched.wait()
    moved.start()
    summed.wait()
    both = [
        jnp.concatenate([sums[w, 0:8].reshape(3 * CH, 128), sums[w, 8:16].reshape(3 * CH, 128)], axis=1)
        for w in range(2)
    ]
    for a in range(3):
        for e in range(3):
            first[a, e] = both[0][e * CH : (e + 1) * CH, a * CIN : (a + 1) * CIN]
            second[a, e] = both[1][e * CH : (e + 1) * CH, a * CH : (a + 1) * CH]
    last = [
        pltpu.make_async_copy(first, first_out, sem.at[6]),
        pltpu.make_async_copy(second, second_out, sem.at[7]),
    ]
    for copy in last:
        copy.start()
    for copy in leaving + last + [moved]:
        copy.wait()


def local(
    coarse,
    noisy,
    cotangent,
    interp_rows,
    interp_cols,
    first_weight,
    second_weight,
    block_ids,
    weight_ids,
    col_start,
):
    smem = pl.BlockSpec(memory_space=pltpu.SMEM)
    vmem = pl.BlockSpec(memory_space=pltpu.VMEM)
    dma = pltpu.SemaphoreType.DMA
    fine, grads, block = pl.pallas_call(
        kernel,
        out_shape=(
            jax.ShapeDtypeStruct((FR, CH, 256), BF16),
            jax.ShapeDtypeStruct((2, NC, 24, 128), F32),
            jax.ShapeDtypeStruct((4, CH, 256), F32),
        ),
        in_specs=[smem] * 3 + [pl.BlockSpec(memory_space=pl.ANY)] * 7,
        out_specs=(pl.BlockSpec(memory_space=pl.ANY), vmem, vmem),
        scratch_shapes=[
            pltpu.VMEM((4, CH, 256), BF16),
            pltpu.VMEM((FS, FR, 256), BF16),
            pltpu.VMEM((CH, FR, 256), BF16),
            pltpu.VMEM((8, 4, FR), BF16),
            pltpu.VMEM((CW, 256), BF16),
            pltpu.VMEM((3, 3, CH, CIN), BF16),
            pltpu.VMEM((3, 3, CH, CH), BF16),
            pltpu.VMEM((FR + 2, CH, 256), BF16),
            pltpu.VMEM((FR + 2, CIN, 256), BF16),
            pltpu.VMEM((FR + 2, CH, 256), BF16),
            pltpu.VMEM((FR + 2, CH, 256), BF16),
            pltpu.VMEM((FR, 3, CH, 256), BF16),
            pltpu.VMEM((FR, 3, CH, 256), BF16),
            pltpu.VMEM((FR, CH, 256), F32),
            pltpu.VMEM((FR, CH, 256), F32),
            pltpu.VMEM((FR, CH, 256), BF16),
            pltpu.VMEM((3 * CH, 256), BF16),
            pltpu.VMEM((3, 2, CH, 256), BF16),
            pltpu.VMEM((3, 2, CH, 256), BF16),
            pltpu.VMEM((3, 2, CH, 256), BF16),
            pltpu.VMEM((3, CH, 128), BF16),
            pltpu.VMEM((CIN, 128), BF16),
            pltpu.VMEM((3, 6, CH, 128), BF16),
            pltpu.VMEM((6, CIN, 128), BF16),
            pltpu.VMEM((3, 3, CH, 128), BF16),
            pltpu.VMEM((3, CIN, 128), BF16),
            pltpu.VMEM((CH, 128), F32),
            pltpu.VMEM((NC, 8, 128), jnp.int32),
            pltpu.VMEM((NC, 4, CH, CW), BF16),
            pltpu.VMEM((NB, 4, CH, CW), BF16),
            pltpu.VMEM((4, 256, CW), BF16),
            pltpu.VMEM((512, 256), BF16),
            pltpu.VMEM((FR, CH, CW), BF16),
            pltpu.VMEM((K, 4, CH, CW), F32),
            pltpu.VMEM((NB, 4, CH, CW), BF16),
            pltpu.VMEM((NC, 4, CH, CW), BF16),
            pltpu.VMEM((4, 4, CH, CW), BF16),
            pltpu.VMEM((NC, CW, 256), BF16),
            pltpu.VMEM((3 * CH, 256), F32),
            pltpu.VMEM((6 * CH, 256), F32),
            pltpu.VMEM((2, NC, 24, 128), F32),
            pltpu.VMEM((2, NC, 24, 128), F32),
            pltpu.VMEM((2, NR, 24, 128), F32),
            dma((4, 8)),
            dma((4, 8)),
            dma((NC,)),
            dma((NC,)),
            dma((NC + 4,)),
            dma((NB,)),
            dma((NC,)),
            dma((NC,)),
            dma((4,)),
            dma((4,)),
            dma((2, NC)),
            dma((2, NC)),
            dma((2, NR)),
            dma((2, NR)),
            dma((2, NC)),
            dma((2, NC)),
            dma,
            dma((7,)),
        ],
        compiler_params=pltpu.CompilerParams(
            collective_id=0, has_side_effects=True, vmem_limit_bytes=56 * 1024 * 1024
        ),
        cost_estimate=pl.CostEstimate(flops=4_000_000_000, bytes_accessed=8_000_000, transcendentals=524_288),
    )(
        block_ids,
        weight_ids,
        col_start,
        coarse,
        noisy,
        cotangent,
        interp_rows.transpose(0, 2, 1),
        interp_cols,
        first_weight,
        second_weight,
    )
    anywhere = pl.BlockSpec(memory_space=pl.ANY)
    return pl.pallas_call(
        results,
        out_shape=(
            jax.ShapeDtypeStruct((CH, FR, 256), BF16),
            jax.ShapeDtypeStruct((3, 3, CH, CIN), F32),
            jax.ShapeDtypeStruct((3, 3, CH, CH), F32),
            jax.ShapeDtypeStruct((4, CH, 256), F32),
        ),
        in_specs=[anywhere] * 3,
        out_specs=(anywhere,) * 4,
        scratch_shapes=[
            pltpu.VMEM((FR, CH, 256), BF16),
            pltpu.VMEM((CH, FR, 256), BF16),
            pltpu.VMEM((2, NC, 24, 128), F32),
            pltpu.VMEM((4, CH, 256), F32),
            pltpu.VMEM((3, 3, CH, CIN), F32),
            pltpu.VMEM((3, 3, CH, CH), F32),
            dma((9,)),
        ],
        compiler_params=pltpu.CompilerParams(vmem_limit_bytes=60 * 1024 * 1024),
        cost_estimate=pl.CostEstimate(flops=270_000_000, bytes_accessed=4_000_000, transcendentals=0),
    )(fine, grads, block)


def solution(mesh):
    in_specs = (
        P(("row", "col"), None, None),
        P(None, "row", "col"),
        P(None, "row", "col"),
        P(),
        P(),
        P(),
        P(),
        P(("row", "col"), None),
        P(("row", "col"), None),
        P("col"),
    )
    out_specs = (P(None, "row", "col"), P(), P(), P(("row", "col"), None, None))
    return jax.shard_map(local, mesh=mesh, in_specs=in_specs, out_specs=out_specs, check_vma=False)
```

```python
import jax
import jax.numpy as jnp
from jax import lax
from jax.experimental import pallas as pl
from jax.experimental.pallas import tpu as pltpu
from jax.sharding import PartitionSpec as P

F32 = jnp.float32
BF16 = jnp.bfloat16
MESH = pl.DeviceIdType.MESH

NR = 8
NC = 16
HB = 2
K = 4
FR = 32
CH = 64
FS = 16
CIN = 80
CW = 128
NB = NC + 2 * HB

PEERS = (
    ((2, 2), (1, 2), (2, 1), (3, 2), (2, 3), (1, 1), (3, 3), (1, 3))
    + ((3, 1), (0, 2), (2, 0), (0, 1), (1, 0), (0, 3), (3, 0))
)
COT, INP, HID, ACT = range(4)


def iota(shape, dim):
    return lax.broadcasted_iota(jnp.int32, shape, dim)


def dot(a, b):
    return jnp.dot(a, b, preferred_element_type=F32)


def dot_nt(a, b):
    return lax.dot_general(a, b, (((1,), (1,)), ((), ())), preferred_element_type=F32)


def dot_tn(a, b):
    return lax.dot_general(a, b, (((0,), (0,)), ((), ())), preferred_element_type=F32)


def one_hot(hit):
    return jnp.where(hit, 1.0, 0.0).astype(BF16)


def permutation():
    i0, i1 = iota((256, 256), 0), iota((256, 256), 1)
    return one_hot((lax.rem(i0, 16) == lax.div(i1, 16)) & (lax.div(i0, 16) == lax.rem(i1, 16)))


def kernel(
    block_ids,
    weight_ids,
    col_start,
    *rest,
):
    hbm, rest = rest[:7], rest[7:]
    body(block_ids, weight_ids, col_start, hbm, *rest)


def body(
    block_ids,
    weight_ids,
    col_start,
    hbm,
    fine_hbm,
    grads_out,
    coarse_out,
    coarse,
    noisy,
    cot,
    rows,
    cols,
    first_w,
    second_w,
    v_cot,
    v_in,
    v_hid,
    v_act,
    g_cot,
    g_act,
    hgrad,
    pre,
    fine,
    wf1,
    wf2,
    wb1,
    wb2,
    edge,
    edge_in,
    edge_got,
    edge_got_in,
    around,
    around_in,
    fix,
    cs,
    cs_all,
    slab,
    wide_a,
    wide_b,
    gath_a,
    gath_b,
    pieces,
    lmat,
    sec,
    pgrad,
    sbuf,
    rbuf,
    rhalo,
    spots,
    acc1,
    acc2,
    gbuf,
    gpart,
    grow,
    x_send,
    x_recv,
    cs_send,
    cs_recv,
    s1_send,
    s1_recv,
    s2_send,
    s2_recv,
    po_send,
    po_recv,
    rs_send,
    rs_recv,
    rh_send,
    rh_recv,
    w1_send,
    w1_recv,
    w2_send,
    w2_recv,
    w3_send,
    w3_recv,
    out_sem,
    in_sem,
):
    r = lax.axis_index("row")
    c = lax.axis_index("col")
    lane = iota((CH, 128), 1)

    def row_at(d):
        return lax.rem(r + (d + NR), NR)

    def col_at(d):
        return lax.rem(c + (d + NC), NC)

    def peer(n):
        dx, dy = PEERS[n]
        return lax.rem(lax.div(c, 4) + dx, 4) * 4 + lax.rem(c + dy, 4)

    def source(n):
        dx, dy = PEERS[n]
        return lax.rem(lax.div(c, 4) + 4 - dx, 4) * 4 + lax.rem(c + 4 - dy, 4)

    def remote(src, dst, send, recv, device):
        return pltpu.make_async_remote_copy(
            src_ref=src, dst_ref=dst, send_sem=send, recv_sem=recv, device_id=device, device_id_type=MESH
        )

    barrier = pltpu.get_barrier_semaphore()
    met = [(0, d) for d in range(1, NC)] + [(d, 0) for d in range(1, NR)]
    for dr, dc in met:
        pl.semaphore_signal(barrier, inc=1, device_id=(row_at(dr), col_at(dc)), device_id_type=MESH)

    fetched = [
        pltpu.make_async_copy(src, dst, in_sem.at[n])
        for n, (src, dst) in enumerate(zip(hbm, (coarse, noisy, cot, rows, cols, first_w, second_w)))
    ]
    for n in (2, 1, 5, 6, 3, 0, 4):
        fetched[n].start()
    for copy in fetched:
        copy.wait()
    perm = permutation()

    def flip_in(src, dst, c0, h0):
        block = src[c0 : c0 + 16, h0 : h0 + 16, :].reshape(256, 256)
        dst[1 + h0 : 17 + h0, c0 : c0 + 16, :] = dot(perm, block).astype(BF16).reshape(16, 16, 256)

    for c0 in range(0, CH, 16):
        for h0 in range(0, FR, 16):
            flip_in(cot, v_cot, c0, h0)
    for h0 in range(0, FR, 16):
        flip_in(noisy, v_in, 0, h0)

    def place(ins, at):
        return one_hot(iota((ins, 256), 1) == iota((ins, 256), 0) + at)

    wf1[...] = sum(dot(first_w[a].reshape(3 * CH, CIN), place(CIN, a * CIN)) for a in range(3)).astype(BF16)
    for row in range(2):
        flat = sum(dot(second_w[a].reshape(3 * CH, CH), place(CH, (a + row) * CH)) for a in range(3))
        wf2[:, row] = flat.astype(BF16).reshape(3, CH, 256)
    for w, back, ins, skip in ((first_w, wb1, CIN, FS), (second_w, wb2, CH, 0)):
        pick = one_hot(iota((CH, ins), 1) == iota((CH, ins), 0) + skip)
        none = jnp.zeros((CH, ins), BF16)
        for e in range(3):
            taps = [w[2 - a, 2 - e] for a in range(3)]
            back[e, 0] = dot_nt(pick, jnp.concatenate(taps + [none], axis=0)).astype(BF16)
            back[e, 1] = dot_nt(pick, jnp.concatenate([none] + taps, axis=0)).astype(BF16)

    lane256 = iota((FR, 256), 1)
    repeat = one_hot(lax.rem(lax.div(iota((4, 256), 1), 16), 4) == iota((4, 256), 0))
    table = jnp.zeros((FR, 256), F32)
    for k in range(K):
        table = jnp.where(lax.div(lane256, 64) == k, dot_tn(rows[weight_ids[0, k]], repeat), table)
    spread = one_hot(lax.div(iota((512, FR), 0), 16) == iota((512, FR), 1))
    same = lax.rem(iota((512, 256), 0), 16) == lax.rem(iota((512, 256), 1), 16)
    lmat[...] = jnp.where(same, dot(spread, table.astype(BF16)), 0.0).astype(BF16)

    def put_shifted(g, h, t0, t1, count):
        low = iota(t0.shape, 1) == 0
        high = iota(t0.shape, 1) == 127
        r0, r1 = pltpu.roll(t0, 1, 1), pltpu.roll(t1, 1, 1)
        s0, s1 = pltpu.roll(t0, 127, 1), pltpu.roll(t1, 127, 1)

        def put(e, half, value):
            g[pl.ds(h, count), e, :, 128 * half : 128 * half + 128] = value.astype(BF16).reshape(count, CH, 128)

        put(0, 0, jnp.where(high, s1, s0))
        put(0, 1, jnp.where(high, 0.0, s1))
        put(1, 0, t0)
        put(1, 1, t1)
        put(2, 0, jnp.where(low, 0.0, r0))
        put(2, 1, jnp.where(low, r0, r1))

    def shift_cot(h, _):
        put_shifted(g_cot, h, v_cot[h + 1, :, 0:128].astype(F32), v_cot[h + 1, :, 128:256].astype(F32), 1)
        return 0

    bufs = {
        COT: (v_cot, edge.at[0], edge_got.at[0], around.at[0], CH),
        INP: (v_in, edge_in, edge_got_in, around_in, CIN),
        HID: (v_hid, edge.at[1], edge_got.at[1], around.at[1], CH),
        ACT: (v_act, edge.at[2], edge_got.at[2], around.at[2], CH),
    }

    def halo_pack(x):
        v, e, _, _, chans = bufs[x]
        at = iota((chans, 128), 1)

        def pack(h, held):
            t0 = v[h + 1, :, 0:128].astype(F32)
            t1 = v[h + 1, :, 128:256].astype(F32)
            ends = pltpu.roll(jnp.where(at == 127, t1, t0), 2 * h, 1)
            return jnp.where(((at - 2 * h + 1) & 127) < 2, ends, held)

        e[...] = lax.fori_loop(0, FR, pack, jnp.zeros((chans, 128), F32), unroll=8).astype(BF16)

    def halo_copies(x, far):
        v, e, got, _, _ = bufs[x]

        def one(n, src, dst, dr, dc):
            return remote(src, dst, x_send.at[x, n], x_recv.at[x, n], (row_at(dr), col_at(dc)))

        if far:
            return [
                one(2, got.at[0], got.at[2], 1, 0),
                one(3, got.at[1], got.at[3], 1, 0),
                one(4, got.at[0], got.at[4], -1, 0),
                one(5, got.at[1], got.at[5], -1, 0),
            ]
        return [
            one(0, e, got.at[0], 0, 1),
            one(1, e, got.at[1], 0, -1),
            one(6, v.at[FR], v.at[0], 1, 0),
            one(7, v.at[1], v.at[FR + 1], -1, 0),
        ]

    def halo_start(x):
        halo_pack(x)
        for copy in halo_copies(x, False):
            copy.start()

    def set_ring(x, corners):
        _, _, got, ring, chans = bufs[x]
        at = iota((chans, 128), 1)
        top = (r > 0).astype(F32)
        bottom = (r < NR - 1).astype(F32)
        west = (c > 0).astype(F32)
        east = (c < NC - 1).astype(F32)

        def side(mid, up, down, by, by_corner, first, there):
            cells = pltpu.roll(got[mid].astype(F32), by, 1)
            if corners:
                b = pltpu.roll(got[up].astype(F32), by_corner, 1) * top
                d = pltpu.roll(got[down].astype(F32), by_corner, 1) * bottom
                last = (first + 2 * FR + 2) % 128
                cells = jnp.where(at == first, b, jnp.where(at == last, d, cells))
            return cells * there

        both = jnp.where(lax.rem(at, 2) == 0, side(0, 2, 4, 3, 67, 0, west), side(1, 3, 5, 1, 65, 127, east))
        ring[0] = both.astype(BF16)
        ring[1] = pltpu.roll(both, 126, 1).astype(BF16)
        ring[2] = pltpu.roll(both, 124, 1).astype(BF16)

    def halo_near(x):
        v, chans = bufs[x][0], bufs[x][4]
        near = halo_copies(x, False)
        for copy in near[:2]:
            copy.wait()
        for copy in halo_copies(x, True):
            copy.start()
        for copy in near[2:]:
            copy.wait()

        @pl.when(r == 0)
        def _():
            v[0] = jnp.zeros((chans, 256), BF16)

        @pl.when(r == NR - 1)
        def _():
            v[FR + 1] = jnp.zeros((chans, 256), BF16)

    def halo_corners(x):
        for copy in halo_copies(x, True):
            copy.wait()
        set_ring(x, True)

    def combine(prod, n, ends):
        at = iota((n, 128), 1)
        a0, a1 = prod[0:n, 0:128], prod[0:n, 128:256]
        b0, b1 = prod[n : 2 * n, 0:128], prod[n : 2 * n, 128:256]
        d0, d1 = prod[2 * n : 3 * n, 0:128], prod[2 * n : 3 * n, 128:256]
        r0, r1 = pltpu.roll(a0, 1, 1), pltpu.roll(a1, 1, 1)
        s0, s1 = pltpu.roll(d0, 127, 1), pltpu.roll(d1, 127, 1)
        t0 = b0 + jnp.where(at == 0, ends, r0) + jnp.where(at == 127, s1, s0)
        t1 = b1 + jnp.where(at == 0, r0, r1) + jnp.where(at == 127, ends, s1)
        return t0, t1

    def set_fix(x, left, right):
        ring, chans = bufs[x][3], bufs[x][4]
        cells = ring[...].reshape(3 * chans, 128)
        fix[...] = jnp.where(lax.rem(lane, 2) == 0, dot(left, cells), dot(right, cells))

    def fix_of(h):
        return pltpu.roll(fix[...], lax.rem(128 - 2 * h, 128), 1)

    def set_pair_fix(x, weights):
        set_fix(x, weights[0, 0][:, 0 : 3 * CH], weights[2, 0][:, 0 : 3 * CH])

    def conv_pair(weights, v, p):
        prod = dot(weights[...].reshape(6 * CH, 256), v[pl.ds(2 * p, 4)].reshape(256, 256))
        ends = jnp.concatenate([fix_of(2 * p), fix_of(2 * p + 1)], axis=0)
        return combine(prod, 2 * CH, ends)

    halo_pack(COT)

    pl.semaphore_wait(barrier, len(met))

    cs[c] = jnp.full((8, 128), col_start[0], jnp.int32)

    cx, cy = lax.div(c, 4), lax.rem(c, 4)

    def line(axis, d):
        return lax.rem(cx + d, 4) * 4 + cy if axis == 0 else cx * 4 + lax.rem(cy + d, 4)

    mine = (cx, cy)
    wide = (wide_a, wide_b)
    tight = (gath_a, gath_b)

    def s1_copy(axis, d):
        here = mine[axis]
        return remote(
            coarse.at[pl.ds(2 * axis, 2)],
            wide[axis].at[here],
            s1_send.at[axis, d],
            s1_recv.at[axis, here],
            (r, line(axis, d)),
        )

    def s1_arrival(axis, d):
        there = lax.rem(mine[axis] + d, 4)
        ref = wide[axis].at[there]
        return remote(ref, ref, s1_send.at[axis, d], s1_recv.at[axis, there], (r, line(axis, d)))

    def cs_copy(axis, d):
        return remote(
            cs.at[c], cs.at[c], cs_send.at[axis, d], cs_recv.at[axis, mine[axis]], (r, line(axis, d))
        )

    def cs_arrival(axis, d):
        ref = cs.at[line(axis, d)]
        there = lax.rem(mine[axis] + d, 4)
        return remote(ref, ref, cs_send.at[axis, d], cs_recv.at[axis, there], (r, line(axis, d)))

    def group_copy(d):
        group = pl.ds(4 * cx, 4)
        return remote(cs.at[group], cs_all.at[group], cs_send.at[2, d], cs_recv.at[2, cx], (r, line(0, d)))

    def group_arrival(d):
        there = lax.rem(cx + d, 4)
        ref = cs_all.at[pl.ds(4 * there, 4)]
        return remote(ref, ref, cs_send.at[2, d], cs_recv.at[2, there], (r, line(0, d)))

    for d in (2, 1, 3):
        for axis in range(2):
            cs_copy(axis, d).start()
    for d in (2, 1, 3):
        for axis in range(2):
            s1_copy(axis, d).start()
    for axis in range(2):
        wide[axis][mine[axis]] = coarse[2 * axis : 2 * axis + 2]
    for copy in halo_copies(COT, False):
        copy.start()
    lax.fori_loop(0, FR, shift_cot, 0, unroll=4)
    for axis in (1, 0):
        for d in range(1, 4):
            cs_copy(axis, d).wait_send()
            cs_arrival(axis, d).wait_recv()
    cs_all[pl.ds(4 * cx, 4)] = cs[pl.ds(4 * cx, 4)]

    def s2_copy(axis, d):
        here = mine[1 - axis]
        return remote(
            slab.at[axis, d],
            tight[axis].at[pl.ds(4 * here, 4)],
            s2_send.at[axis, d],
            s2_recv.at[axis, here],
            (r, line(1 - axis, d)),
        )

    def s2_arrival(axis, d):
        there = lax.rem(mine[1 - axis] + d, 4)
        ref = tight[axis].at[pl.ds(4 * there, 4)]
        return remote(ref, ref, s2_send.at[axis, d], s2_recv.at[axis, there], (r, line(1 - axis, d)))

    def cut(axis, to):
        pick = one_hot(iota((256, 128), 0) == iota((256, 128), 1) + cs[to][0:1, :])
        return dot(wide[axis][...].reshape(512, 256), pick).astype(BF16).reshape(4, 2, CH, CW)

    for axis in range(2):
        for d in range(1, 4):
            s1_arrival(axis, d).wait_recv()
        for d in (2, 1, 3):
            slab[axis, d] = cut(axis, line(1 - axis, d))
            s2_copy(axis, d).start()
    for d in (2, 1, 3):
        group_copy(d).start()
    for axis in range(2):
        tight[axis][pl.ds(4 * mine[1 - axis], 4)] = cut(axis, c)

    halo_near(COT)
    halo_corners(COT)
    set_pair_fix(COT, wb2)

    def hidden_grad(p, _):
        t0, t1 = conv_pair(wb2, v_cot, p)
        hgrad[pl.ds(2 * p, 2), :, 0:128] = t0.reshape(2, CH, 128)
        hgrad[pl.ds(2 * p, 2), :, 128:256] = t1.reshape(2, CH, 128)
        return 0

    lax.fori_loop(0, FR // 2, hidden_grad, 0, unroll=4)

    for d in range(1, 4):
        group_copy(d).wait_send()
        group_arrival(d).wait_recv()

    def set_spot(n, _):
        start = cs_all[n][0:1, :]
        start = jnp.concatenate([start, start], axis=1)
        spots[n] = one_hot(iota((CW, 256), 1) == iota((CW, 256), 0) + start)
        return 0

    lax.fori_loop(0, NC, set_spot, 0)

    for axis in range(2):
        for d in range(1, 4):
            s1_copy(axis, d).wait_send()
            s2_copy(axis, d).wait_send()
            s2_arrival(axis, d).wait_recv()

    def pass_on(n):
        half, src, dst, count, dr = (
            (0, 11, NC, 1, 1),
            (0, 15, NC + 1, 1, 1),
            (0, 0, NC + 2, 1, -1),
            (0, 4, NC + 3, 1, -1),
            (1, 14, NC, 2, 1),
            (1, 0, NC + 2, 2, -1),
        )[n]
        return remote(
            tight[half].at[pl.ds(src, count)],
            tight[half].at[pl.ds(dst, count)],
            po_send.at[n],
            po_recv.at[n],
            (row_at(dr), c),
        )

    for n in range(6):
        pass_on(n).start()
    for n in range(6):
        pass_on(n).wait()

    first_block = r * NC - HB
    for k in range(K):
        near = jnp.clip(block_ids[0, k] - first_block, 0, NB - 1)
        own = jnp.clip(near - HB, 0, NC - 1)
        outer = jnp.where(near < HB, NC + near, near)
        inside = (near >= HB) & (near < NC + HB)
        for half, at in ((0, lax.rem(own, 4) * 4 + lax.div(own, 4)), (1, own)):
            piece = tight[half][jnp.where(inside, at, outer)]
            for g in range(4):
                row = 64 * k + 32 * half
                pieces[g, row : row + 32, :] = piece[:, 16 * g : 16 * g + 16, :].reshape(32, CW)
    for g in range(4):
        sec[:, 16 * g : 16 * g + 16, :] = dot(lmat[...], pieces[g]).astype(BF16).reshape(FR, 16, CW)

    def regrid(q, _):
        flat = sec[pl.ds(4 * q, 4)].reshape(256, CW)
        v_in[pl.ds(1 + 4 * q, 4), FS:CIN, :] = dot(flat, cols[...]).astype(BF16).reshape(4, CH, 256)
        return 0

    lax.fori_loop(0, FR // 4, regrid, 0, unroll=4)

    halo_start(INP)

    def first_row(h, _):
        prod = dot(wf1[:, 0 : 3 * CIN], v_in[pl.ds(h, 3)].reshape(3 * CIN, 256))
        t0, t1 = combine(prod, CH, 0.0)
        pre[h, :, 0:128] = t0
        pre[h, :, 128:256] = t1
        return 0

    lax.fori_loop(1, FR - 1, first_row, 0, unroll=4)

    halo_near(INP)
    set_ring(INP, False)
    first_row(0, 0)
    first_row(FR - 1, 0)

    def set_first_fix():
        set_fix(INP, wf1[0:CH, 0 : 3 * CIN], wf1[2 * CH : 3 * CH, 0 : 3 * CIN])

    set_first_fix()

    def activate(h, _):
        ends = fix_of(h)
        t0 = pre[h, :, 0:128] + jnp.where(lane == 0, ends, 0.0)
        t1 = pre[h, :, 128:256] + jnp.where(lane == 127, ends, 0.0)
        back = []
        for half, t in ((0, t0), (1, t1)):
            at = slice(128 * half, 128 * half + 128)
            s = 1.0 / (1.0 + jnp.exp(-t))
            v_hid[h + 1, :, at] = (t * s).astype(BF16)
            grad = hgrad[h, :, at] * (s * (1.0 + t * (1.0 - s)))
            v_act[h + 1, :, at] = grad.astype(BF16)
            back.append(grad)
        put_shifted(g_act, h, back[0], back[1], 1)
        return 0

    lax.fori_loop(1, FR - 1, activate, 0, unroll=4)
    halo_corners(INP)
    set_first_fix()
    activate(0, 0)
    activate(FR - 1, 0)

    halo_start(ACT)
    halo_start(HID)

    edges = (one_hot(lax.rem(lane, 2) == 0), one_hot(lax.rem(lane, 2) == 1))

    def edge_terms(x, of):
        ring, chans = bufs[x][3], bufs[x][4]
        mine = bufs[of][1][...]
        both = jnp.concatenate([mine * edges[0], mine * edges[1]], axis=0)
        return dot_nt(both, ring[...].reshape(3 * chans, 128))

    acc1[...] = jnp.zeros(acc1.shape, F32)

    def first_grad(q, _):
        left = [g_act[4 * q + i].reshape(3 * CH, 256) for i in range(4)]
        right = [v_in[pl.ds(4 * q + i, 3)].reshape(3 * CIN, 256) for i in range(4)]
        acc1[:, 0 : 3 * CIN] += dot_nt(jnp.concatenate(left, axis=1), jnp.concatenate(right, axis=1))
        return 0

    lax.fori_loop(0, FR // 4, first_grad, 0, unroll=2)

    extra = edge_terms(INP, ACT)
    acc1[0:CH, 0 : 3 * CIN] += extra[0:CH]
    acc1[2 * CH :, 0 : 3 * CIN] += extra[CH:]

    def w1_copy(n):
        to = peer(n)
        return remote(gbuf.at[to], gpart.at[c], w1_send.at[n], w1_recv.at[c], (r, to))

    def keep(which, acc):
        for half in range(2):
            rows = acc[0 : 3 * CH, 128 * half : 128 * half + 128]
            gbuf[8 * half : 8 * half + 8, which] = rows.reshape(8, 24, 128)

    keep(0, acc1)

    halo_near(ACT)
    halo_near(HID)
    halo_corners(HID)
    acc2[...] = jnp.zeros(acc2.shape, F32)

    def second_grad(q, _):
        left = [g_cot[pl.ds(4 * q + i, 2)].reshape(6 * CH, 256) for i in (0, 2)]
        right = [v_hid[pl.ds(4 * q + i, 4)].reshape(256, 256) for i in (0, 2)]
        acc2[...] += dot_nt(jnp.concatenate(left, axis=1), jnp.concatenate(right, axis=1))
        return 0

    lax.fori_loop(0, FR // 4, second_grad, 0, unroll=2)
    extra = edge_terms(HID, COT)
    acc2[0 : 3 * CH, :] += pltpu.roll(acc2[3 * CH :, :], 192, 1)
    acc2[0:CH, 0 : 3 * CH] += extra[0:CH]
    acc2[2 * CH : 3 * CH, 0 : 3 * CH] += extra[CH:]
    keep(1, acc2)
    for n in range(NC - 1):
        w1_copy(n).start()
    gpart[c] = gbuf[c]

    def w2_copy(d):
        return remote(grow.at[r], grow.at[r], w2_send.at[d], w2_recv.at[r], (row_at(d), c))

    def w2_arrival(d):
        there = grow.at[row_at(d)]
        return remote(there, there, w2_send.at[d], w2_recv.at[row_at(d)], (row_at(d), c))

    def w3_copy(n):
        here = grads_out.at[c]
        return remote(here, here, w3_send.at[n], w3_recv.at[c], (r, peer(n)))

    def w3_arrival(n):
        there = grads_out.at[source(n)]
        return remote(there, there, w3_send.at[n], w3_recv.at[source(n)], (r, source(n)))

    def sum_col():
        for n in range(NC - 1):
            w1_copy(n).wait_send()
            there = gpart.at[source(n)]
            remote(there, there, w1_send.at[n], w1_recv.at[source(n)], (r, source(n))).wait_recv()
        total = gpart[0]
        for n in range(1, NC):
            total = total + gpart[n]
        grow[r] = total
        for d in range(1, NR):
            w2_copy(d).start()

    def spread_sum():
        for d in range(1, NR):
            w2_copy(d).wait_send()
            w2_arrival(d).wait_recv()
        total = grow[0]
        for n in range(1, NR):
            total = total + grow[n]
        grads_out[c] = total
        for n in range(NC - 1):
            w3_copy(n).start()

    set_ring(ACT, False)
    set_pair_fix(ACT, wb1)

    def cond_grad(p, _):
        t0, t1 = conv_pair(wb1, v_act, p)
        fine[pl.ds(2 * p, 2), :, 0:128] = t0.astype(BF16).reshape(2, CH, 128)
        fine[pl.ds(2 * p, 2), :, 128:256] = t1.astype(BF16).reshape(2, CH, 128)
        return 0

    lax.fori_loop(1, FR // 2 - 1, cond_grad, 0, unroll=4)
    halo_corners(ACT)
    set_pair_fix(ACT, wb1)
    cond_grad(0, 0)
    cond_grad(FR // 2 - 1, 0)

    def section_grad(q, _):
        flat = fine[pl.ds(8 * q, 8)].reshape(512, 256)
        sec[pl.ds(8 * q, 8)] = dot_nt(flat, cols[...]).astype(BF16).reshape(8, CH, CW)
        return 0

    lax.fori_loop(0, FR // 8, section_grad, 0)
    eye = one_hot(iota((256, 256), 0) == iota((256, 256), 1))
    lmat_t = dot_nt(eye, lmat[...]).astype(BF16)
    for g in range(4):
        part = dot(lmat_t, sec[:, 16 * g : 16 * g + 16, :].reshape(512, CW))
        pgrad[:, :, 16 * g : 16 * g + 16, :] = part.reshape(K, 4, 16, CW)

    def contribution(b):
        total = None
        for k in range(K):
            hit = (block_ids[0, k] - first_block == b).astype(F32)
            term = pgrad[k] * hit
            total = term if total is None else total + term
        return total

    def rh_copy(n):
        b, dr = ((0, -1), (1, -1), (NB - 2, 1), (NB - 1, 1))[n]
        return remote(sbuf.at[b], rhalo.at[n], rh_send.at[n], rh_recv.at[n], (row_at(dr), c))

    for n, b in enumerate((0, 1, NB - 2, NB - 1)):
        sbuf[b] = contribution(b).astype(BF16)
        rh_copy(n).start()

    def rs_copy(n):
        to = peer(n)
        return remote(sbuf.at[HB + to], rbuf.at[c], rs_send.at[n], rs_recv.at[c], (r, to))

    def is_inner(to):
        return (to >= HB) & (to < NC - HB)

    def send_inner(n):
        to = peer(n)

        @pl.when(is_inner(to))
        def _():
            sbuf[HB + to] = contribution(HB + to).astype(BF16)
            rs_copy(n).start()

    def send_outer(n):
        @pl.when(jnp.logical_not(is_inner(peer(n))))
        def _():
            rs_copy(n).start()

    for n in range(8):
        send_inner(n)
    for n, b in enumerate((NC, NC + 1, HB, HB + 1)):
        rh_copy(n).wait_recv()
        sbuf[b] = (contribution(b) + rhalo[n].astype(F32)).astype(BF16)
    for n in range(8, NC - 1):
        send_inner(n)
        send_outer(n)
        send_outer(n - 8)
    send_outer(7)

    @pl.when(is_inner(c))
    def _():
        sbuf[HB + c] = contribution(HB + c).astype(BF16)

    rbuf[c] = sbuf[HB + c]

    sum_col()
    set_pair_fix(HID, wf2)

    def second_level(p, _):
        t0, t1 = conv_pair(wf2, v_hid, p)
        fine[pl.ds(2 * p, 2), :, 0:128] = t0.astype(BF16).reshape(2, CH, 128)
        fine[pl.ds(2 * p, 2), :, 128:256] = t1.astype(BF16).reshape(2, CH, 128)
        return 0

    lax.fori_loop(0, FR // 4, second_level, 0, unroll=4)
    spread_sum()
    lax.fori_loop(FR // 4, FR // 2, second_level, 0, unroll=4)
    out = pltpu.make_async_copy(fine, fine_hbm, out_sem)
    out.start()

    for q in range(4):
        senders = [source(n) if n < NC - 1 else c for n in range(4 * q, 4 * q + 4)]
        for n in range(4 * q, min(4 * q + 4, NC - 1)):
            rs_copy(n).wait_send()
            there = rbuf.at[source(n)]
            remote(there, there, rs_send.at[n], rs_recv.at[source(n)], (r, source(n))).wait_recv()
        flat = jnp.concatenate([rbuf[n].reshape(256, CW) for n in senders], axis=1)
        spot = jnp.concatenate([spots[n] for n in senders], axis=0)
        part = dot(flat, spot).reshape(4, CH, 256)
        coarse_out[...] = part if q == 0 else coarse_out[...] + part

    for n in range(4):
        rh_copy(n).wait_send()
    for n in range(NC - 1):
        w3_copy(n).wait_send()
        w3_arrival(n).wait_recv()
    out.wait()


def results(
    fine, grads, block, fine_out, first_out, second_out, coarse_out, rows, turned, sums, held, first, second, sem
):
    fetched = pltpu.make_async_copy(block, held, sem.at[0])
    moved = pltpu.make_async_copy(held, coarse_out, sem.at[8])
    arrivals = [
        pltpu.make_async_copy(fine.at[pl.ds(16 * n, 16)], rows.at[pl.ds(16 * n, 16)], sem.at[1 + n]) for n in range(2)
    ]
    summed = pltpu.make_async_copy(grads, sums, sem.at[3])
    leaving = [
        pltpu.make_async_copy(
            turned.at[:, pl.ds(16 * n, 16), :], fine_out.at[:, pl.ds(16 * n, 16), :], sem.at[4 + n]
        )
        for n in range(2)
    ]
    for copy in arrivals:
        copy.start()
    summed.start()
    fetched.start()
    perm = permutation()
    for n in range(2):
        arrivals[n].wait()
        for c0 in range(0, CH, 16):
            flat = rows[16 * n : 16 * n + 16, c0 : c0 + 16, :].reshape(256, 256)
            turned[c0 : c0 + 16, 16 * n : 16 * n + 16, :] = dot(perm, flat).astype(BF16).reshape(16, 16, 256)
        leaving[n].start()
    fetched.wait()
    moved.start()
    summed.wait()
    both = [
        jnp.concatenate([sums[0:8, w].reshape(3 * CH, 128), sums[8:16, w].reshape(3 * CH, 128)], axis=1)
        for w in range(2)
    ]
    for a in range(3):
        for e in range(3):
            first[a, e] = both[0][e * CH : (e + 1) * CH, a * CIN : (a + 1) * CIN]
            second[a, e] = both[1][e * CH : (e + 1) * CH, a * CH : (a + 1) * CH]
    last = [
        pltpu.make_async_copy(first, first_out, sem.at[6]),
        pltpu.make_async_copy(second, second_out, sem.at[7]),
    ]
    for copy in last:
        copy.start()
    for copy in leaving + last + [moved]:
        copy.wait()


def local(
    coarse,
    noisy,
    cotangent,
    interp_rows,
    interp_cols,
    first_weight,
    second_weight,
    block_ids,
    weight_ids,
    col_start,
):
    smem = pl.BlockSpec(memory_space=pltpu.SMEM)
    vmem = pl.BlockSpec(memory_space=pltpu.VMEM)
    dma = pltpu.SemaphoreType.DMA
    fine, grads, block = pl.pallas_call(
        kernel,
        out_shape=(
            jax.ShapeDtypeStruct((FR, CH, 256), BF16),
            jax.ShapeDtypeStruct((NC, 2, 24, 128), F32),
            jax.ShapeDtypeStruct((4, CH, 256), F32),
        ),
        in_specs=[smem] * 3 + [pl.BlockSpec(memory_space=pl.ANY)] * 7,
        out_specs=(pl.BlockSpec(memory_space=pl.ANY), vmem, vmem),
        scratch_shapes=[
            pltpu.VMEM((4, CH, 256), BF16),
            pltpu.VMEM((FS, FR, 256), BF16),
            pltpu.VMEM((CH, FR, 256), BF16),
            pltpu.VMEM((8, 4, FR), BF16),
            pltpu.VMEM((CW, 256), BF16),
            pltpu.VMEM((3, 3, CH, CIN), BF16),
            pltpu.VMEM((3, 3, CH, CH), BF16),
            pltpu.VMEM((FR + 2, CH, 256), BF16),
            pltpu.VMEM((FR + 2, CIN, 256), BF16),
            pltpu.VMEM((FR + 2, CH, 256), BF16),
            pltpu.VMEM((FR + 2, CH, 256), BF16),
            pltpu.VMEM((FR, 3, CH, 256), BF16),
            pltpu.VMEM((FR, 3, CH, 256), BF16),
            pltpu.VMEM((FR, CH, 256), F32),
            pltpu.VMEM((FR, CH, 256), F32),
            pltpu.VMEM((FR, CH, 256), BF16),
            pltpu.VMEM((3 * CH, 256), BF16),
            pltpu.VMEM((3, 2, CH, 256), BF16),
            pltpu.VMEM((3, 2, CH, 256), BF16),
            pltpu.VMEM((3, 2, CH, 256), BF16),
            pltpu.VMEM((3, CH, 128), BF16),
            pltpu.VMEM((CIN, 128), BF16),
            pltpu.VMEM((3, 6, CH, 128), BF16),
            pltpu.VMEM((6, CIN, 128), BF16),
            pltpu.VMEM((3, 3, CH, 128), BF16),
            pltpu.VMEM((3, CIN, 128), BF16),
            pltpu.VMEM((CH, 128), F32),
            pltpu.VMEM((NC, 8, 128), jnp.int32),
            pltpu.VMEM((NC, 8, 128), jnp.int32),
            pltpu.VMEM((2, 4, 4, 2, CH, CW), BF16),
            pltpu.VMEM((4, 2, CH, 256), BF16),
            pltpu.VMEM((4, 2, CH, 256), BF16),
            pltpu.VMEM((NB, 2, CH, CW), BF16),
            pltpu.VMEM((NB, 2, CH, CW), BF16),
            pltpu.VMEM((4, 256, CW), BF16),
            pltpu.VMEM((512, 256), BF16),
            pltpu.VMEM((FR, CH, CW), BF16),
            pltpu.VMEM((K, 4, CH, CW), F32),
            pltpu.VMEM((NB, 4, CH, CW), BF16),
            pltpu.VMEM((NC, 4, CH, CW), BF16),
            pltpu.VMEM((4, 4, CH, CW), BF16),
            pltpu.VMEM((NC, CW, 256), BF16),
            pltpu.VMEM((3 * CH, 256), F32),
            pltpu.VMEM((6 * CH, 256), F32),
            pltpu.VMEM((NC, 2, 24, 128), F32),
            pltpu.VMEM((NC, 2, 24, 128), F32),
            pltpu.VMEM((NR, 2, 24, 128), F32),
            dma((4, 8)),
            dma((4, 8)),
            dma((3, 4)),
            dma((3, 4)),
            dma((2, 4)),
            dma((2, 4)),
            dma((2, 4)),
            dma((2, 4)),
            dma((6,)),
            dma((6,)),
            dma((NC,)),
            dma((NC,)),
            dma((4,)),
            dma((4,)),
            dma((NC,)),
            dma((NC,)),
            dma((NR,)),
            dma((NR,)),
            dma((NC,)),
            dma((NC,)),
            dma,
            dma((7,)),
        ],
        compiler_params=pltpu.CompilerParams(
            collective_id=0, has_side_effects=True, vmem_limit_bytes=56 * 1024 * 1024
        ),
        cost_estimate=pl.CostEstimate(flops=4_000_000_000, bytes_accessed=8_000_000, transcendentals=524_288),
    )(
        block_ids,
        weight_ids,
        col_start,
        coarse,
        noisy,
        cotangent,
        interp_rows.transpose(0, 2, 1),
        interp_cols,
        first_weight,
        second_weight,
    )
    anywhere = pl.BlockSpec(memory_space=pl.ANY)
    return pl.pallas_call(
        results,
        out_shape=(
            jax.ShapeDtypeStruct((CH, FR, 256), BF16),
            jax.ShapeDtypeStruct((3, 3, CH, CIN), F32),
            jax.ShapeDtypeStruct((3, 3, CH, CH), F32),
            jax.ShapeDtypeStruct((4, CH, 256), F32),
        ),
        in_specs=[anywhere] * 3,
        out_specs=(anywhere,) * 4,
        scratch_shapes=[
            pltpu.VMEM((FR, CH, 256), BF16),
            pltpu.VMEM((CH, FR, 256), BF16),
            pltpu.VMEM((NC, 2, 24, 128), F32),
            pltpu.VMEM((4, CH, 256), F32),
            pltpu.VMEM((3, 3, CH, CIN), F32),
            pltpu.VMEM((3, 3, CH, CH), F32),
            dma((9,)),
        ],
        compiler_params=pltpu.CompilerParams(vmem_limit_bytes=60 * 1024 * 1024),
        cost_estimate=pl.CostEstimate(flops=270_000_000, bytes_accessed=4_000_000, transcendentals=0),
    )(fine, grads, block)


def solution(mesh):
    in_specs = (
        P(("row", "col"), None, None),
        P(None, "row", "col"),
        P(None, "row", "col"),
        P(),
        P(),
        P(),
        P(),
        P(("row", "col"), None),
        P(("row", "col"), None),
        P("col"),
    )
    out_specs = (P(None, "row", "col"), P(), P(), P(("row", "col"), None, None))
    return jax.shard_map(local, mesh=mesh, in_specs=in_specs, out_specs=out_specs, check_vma=False)
```

```python
import jax
import jax.numpy as jnp
from jax import lax
from jax.experimental import pallas as pl
from jax.experimental.pallas import tpu as pltpu
from jax.sharding import PartitionSpec as P

F32 = jnp.float32
BF16 = jnp.bfloat16
MESH = pl.DeviceIdType.MESH

NR = 8
NC = 16
HB = 2
K = 4
FR = 32
CH = 64
FS = 16
CIN = 80
CW = 128
NB = NC + 2 * HB

PEERS = (
    ((2, 2), (1, 2), (2, 1), (3, 2), (2, 3), (1, 1), (3, 3), (1, 3))
    + ((3, 1), (0, 2), (2, 0), (0, 1), (1, 0), (0, 3), (3, 0))
)
COT, INP, HID, ACT = range(4)


def iota(shape, dim):
    return lax.broadcasted_iota(jnp.int32, shape, dim)


def dot(a, b):
    return jnp.dot(a, b, preferred_element_type=F32)


def dot_nt(a, b):
    return lax.dot_general(a, b, (((1,), (1,)), ((), ())), preferred_element_type=F32)


def dot_tn(a, b):
    return lax.dot_general(a, b, (((0,), (0,)), ((), ())), preferred_element_type=F32)


def one_hot(hit):
    return jnp.where(hit, 1.0, 0.0).astype(BF16)


def permutation():
    i0, i1 = iota((256, 256), 0), iota((256, 256), 1)
    return one_hot((lax.rem(i0, 16) == lax.div(i1, 16)) & (lax.div(i0, 16) == lax.rem(i1, 16)))


def kernel(
    block_ids,
    weight_ids,
    col_start,
    *rest,
):
    hbm, rest = rest[:7], rest[7:]
    body(block_ids, weight_ids, col_start, hbm, *rest)


def body(
    block_ids,
    weight_ids,
    col_start,
    hbm,
    fine_hbm,
    grads_out,
    coarse_out,
    coarse,
    noisy,
    cot,
    rows,
    cols,
    first_w,
    second_w,
    v_cot,
    v_in,
    v_hid,
    v_act,
    g_cot,
    g_act,
    hgrad,
    pre,
    fine,
    wf1,
    wf2,
    wb1,
    wb2,
    edge,
    edge_in,
    edge_got,
    edge_got_in,
    around,
    around_in,
    fix,
    cs,
    cs_all,
    slab,
    wide_a,
    wide_b,
    gath_a,
    gath_b,
    pieces,
    lmat,
    sec,
    pgrad,
    sbuf,
    rbuf,
    rhalo,
    spots,
    acc1,
    acc2,
    gbuf,
    gpart,
    grow,
    x_send,
    x_recv,
    cs_send,
    cs_recv,
    s1_send,
    s1_recv,
    s2_send,
    s2_recv,
    po_send,
    po_recv,
    rs_send,
    rs_recv,
    rh_send,
    rh_recv,
    w1_send,
    w1_recv,
    w2_send,
    w2_recv,
    w3_send,
    w3_recv,
    out_sem,
    in_sem,
):
    r = lax.axis_index("row")
    c = lax.axis_index("col")
    lane = iota((CH, 128), 1)

    def row_at(d):
        return lax.rem(r + (d + NR), NR)

    def col_at(d):
        return lax.rem(c + (d + NC), NC)

    def peer(n):
        dx, dy = PEERS[n]
        return lax.rem(lax.div(c, 4) + dx, 4) * 4 + lax.rem(c + dy, 4)

    def source(n):
        dx, dy = PEERS[n]
        return lax.rem(lax.div(c, 4) + 4 - dx, 4) * 4 + lax.rem(c + 4 - dy, 4)

    def remote(src, dst, send, recv, device):
        return pltpu.make_async_remote_copy(
            src_ref=src, dst_ref=dst, send_sem=send, recv_sem=recv, device_id=device, device_id_type=MESH
        )

    barrier = pltpu.get_barrier_semaphore()
    met = [(0, d) for d in range(1, NC)] + [(d, 0) for d in range(1, NR)]
    for dr, dc in met:
        pl.semaphore_signal(barrier, inc=1, device_id=(row_at(dr), col_at(dc)), device_id_type=MESH)

    fetched = [
        pltpu.make_async_copy(src, dst, in_sem.at[n])
        for n, (src, dst) in enumerate(zip(hbm, (coarse, noisy, cot, rows, cols, first_w, second_w)))
    ]
    for n in (2, 1, 5, 6, 3, 0, 4):
        fetched[n].start()
    for copy in fetched:
        copy.wait()
    perm = permutation()

    def flip_in(src, dst, c0, h0):
        block = src[c0 : c0 + 16, h0 : h0 + 16, :].reshape(256, 256)
        dst[1 + h0 : 17 + h0, c0 : c0 + 16, :] = dot(perm, block).astype(BF16).reshape(16, 16, 256)

    for c0 in range(0, CH, 16):
        for h0 in range(0, FR, 16):
            flip_in(cot, v_cot, c0, h0)
    for h0 in range(0, FR, 16):
        flip_in(noisy, v_in, 0, h0)

    def place(ins, at):
        return one_hot(iota((ins, 256), 1) == iota((ins, 256), 0) + at)

    wf1[...] = sum(dot(first_w[a].reshape(3 * CH, CIN), place(CIN, a * CIN)) for a in range(3)).astype(BF16)
    for row in range(2):
        flat = sum(dot(second_w[a].reshape(3 * CH, CH), place(CH, (a + row) * CH)) for a in range(3))
        wf2[:, row] = flat.astype(BF16).reshape(3, CH, 256)
    for w, back, ins, skip in ((first_w, wb1, CIN, FS), (second_w, wb2, CH, 0)):
        pick = one_hot(iota((CH, ins), 1) == iota((CH, ins), 0) + skip)
        none = jnp.zeros((CH, ins), BF16)
        for e in range(3):
            taps = [w[2 - a, 2 - e] for a in range(3)]
            back[e, 0] = dot_nt(pick, jnp.concatenate(taps + [none], axis=0)).astype(BF16)
            back[e, 1] = dot_nt(pick, jnp.concatenate([none] + taps, axis=0)).astype(BF16)

    lane256 = iota((FR, 256), 1)
    repeat = one_hot(lax.rem(lax.div(iota((4, 256), 1), 16), 4) == iota((4, 256), 0))
    table = jnp.zeros((FR, 256), F32)
    for k in range(K):
        table = jnp.where(lax.div(lane256, 64) == k, dot_tn(rows[weight_ids[0, k]], repeat), table)
    spread = one_hot(lax.div(iota((512, FR), 0), 16) == iota((512, FR), 1))
    same = lax.rem(iota((512, 256), 0), 16) == lax.rem(iota((512, 256), 1), 16)
    lmat[...] = jnp.where(same, dot(spread, table.astype(BF16)), 0.0).astype(BF16)

    def put_shifted(g, h, t0, t1, count):
        low = iota(t0.shape, 1) == 0
        high = iota(t0.shape, 1) == 127
        r0, r1 = pltpu.roll(t0, 1, 1), pltpu.roll(t1, 1, 1)
        s0, s1 = pltpu.roll(t0, 127, 1), pltpu.roll(t1, 127, 1)

        def put(e, half, value):
            g[pl.ds(h, count), e, :, 128 * half : 128 * half + 128] = value.astype(BF16).reshape(count, CH, 128)

        put(0, 0, jnp.where(high, s1, s0))
        put(0, 1, jnp.where(high, 0.0, s1))
        put(1, 0, t0)
        put(1, 1, t1)
        put(2, 0, jnp.where(low, 0.0, r0))
        put(2, 1, jnp.where(low, r0, r1))

    def shift_cot(h, _):
        put_shifted(g_cot, h, v_cot[h + 1, :, 0:128].astype(F32), v_cot[h + 1, :, 128:256].astype(F32), 1)
        return 0

    bufs = {
        COT: (v_cot, edge.at[0], edge_got.at[0], around.at[0], CH),
        INP: (v_in, edge_in, edge_got_in, around_in, CIN),
        HID: (v_hid, edge.at[1], edge_got.at[1], around.at[1], CH),
        ACT: (v_act, edge.at[2], edge_got.at[2], around.at[2], CH),
    }

    def halo_pack(x):
        v, e, _, _, chans = bufs[x]
        at = iota((chans, 128), 1)

        def pack(h, held):
            t0 = v[h + 1, :, 0:128].astype(F32)
            t1 = v[h + 1, :, 128:256].astype(F32)
            ends = pltpu.roll(jnp.where(at == 127, t1, t0), 2 * h, 1)
            return jnp.where(((at - 2 * h + 1) & 127) < 2, ends, held)

        e[...] = lax.fori_loop(0, FR, pack, jnp.zeros((chans, 128), F32), unroll=8).astype(BF16)

    def halo_copies(x, far):
        v, e, got, _, _ = bufs[x]

        def one(n, src, dst, dr, dc):
            return remote(src, dst, x_send.at[x, n], x_recv.at[x, n], (row_at(dr), col_at(dc)))

        if far:
            return [
                one(2, got.at[0], got.at[2], 1, 0),
                one(3, got.at[1], got.at[3], 1, 0),
                one(4, got.at[0], got.at[4], -1, 0),
                one(5, got.at[1], got.at[5], -1, 0),
            ]
        return [
            one(0, e, got.at[0], 0, 1),
            one(1, e, got.at[1], 0, -1),
            one(6, v.at[FR], v.at[0], 1, 0),
            one(7, v.at[1], v.at[FR + 1], -1, 0),
        ]

    def halo_start(x):
        halo_pack(x)
        for copy in halo_copies(x, False):
            copy.start()

    def set_ring(x, corners):
        _, _, got, ring, chans = bufs[x]
        at = iota((chans, 128), 1)
        top = (r > 0).astype(F32)
        bottom = (r < NR - 1).astype(F32)
        west = (c > 0).astype(F32)
        east = (c < NC - 1).astype(F32)

        def side(mid, up, down, by, by_corner, first, there):
            cells = pltpu.roll(got[mid].astype(F32), by, 1)
            if corners:
                b = pltpu.roll(got[up].astype(F32), by_corner, 1) * top
                d = pltpu.roll(got[down].astype(F32), by_corner, 1) * bottom
                last = (first + 2 * FR + 2) % 128
                cells = jnp.where(at == first, b, jnp.where(at == last, d, cells))
            return cells * there

        both = jnp.where(lax.rem(at, 2) == 0, side(0, 2, 4, 3, 67, 0, west), side(1, 3, 5, 1, 65, 127, east))
        ring[0] = both.astype(BF16)
        ring[1] = pltpu.roll(both, 126, 1).astype(BF16)
        ring[2] = pltpu.roll(both, 124, 1).astype(BF16)

    def halo_near(x):
        v, chans = bufs[x][0], bufs[x][4]
        near = halo_copies(x, False)
        for copy in near[:2]:
            copy.wait()
        for copy in halo_copies(x, True):
            copy.start()
        for copy in near[2:]:
            copy.wait()

        @pl.when(r == 0)
        def _():
            v[0] = jnp.zeros((chans, 256), BF16)

        @pl.when(r == NR - 1)
        def _():
            v[FR + 1] = jnp.zeros((chans, 256), BF16)

    def halo_corners(x):
        for copy in halo_copies(x, True):
            copy.wait()
        set_ring(x, True)

    def combine(prod, n, ends):
        at = iota((n, 128), 1)
        a0, a1 = prod[0:n, 0:128], prod[0:n, 128:256]
        b0, b1 = prod[n : 2 * n, 0:128], prod[n : 2 * n, 128:256]
        d0, d1 = prod[2 * n : 3 * n, 0:128], prod[2 * n : 3 * n, 128:256]
        r0, r1 = pltpu.roll(a0, 1, 1), pltpu.roll(a1, 1, 1)
        s0, s1 = pltpu.roll(d0, 127, 1), pltpu.roll(d1, 127, 1)
        t0 = b0 + jnp.where(at == 0, ends, r0) + jnp.where(at == 127, s1, s0)
        t1 = b1 + jnp.where(at == 0, r0, r1) + jnp.where(at == 127, ends, s1)
        return t0, t1

    def set_fix(x, left, right):
        ring, chans = bufs[x][3], bufs[x][4]
        cells = ring[...].reshape(3 * chans, 128)
        fix[...] = jnp.where(lax.rem(lane, 2) == 0, dot(left, cells), dot(right, cells))

    def fix_of(h):
        return pltpu.roll(fix[...], lax.rem(128 - 2 * h, 128), 1)

    def set_pair_fix(x, weights):
        set_fix(x, weights[0, 0][:, 0 : 3 * CH], weights[2, 0][:, 0 : 3 * CH])

    def conv_pair(weights, v, p):
        prod = dot(weights[...].reshape(6 * CH, 256), v[pl.ds(2 * p, 4)].reshape(256, 256))
        ends = jnp.concatenate([fix_of(2 * p), fix_of(2 * p + 1)], axis=0)
        return combine(prod, 2 * CH, ends)

    halo_pack(COT)

    pl.semaphore_wait(barrier, len(met))

    cs[c] = jnp.full((8, 128), col_start[0], jnp.int32)

    cx, cy = lax.div(c, 4), lax.rem(c, 4)

    def line(axis, d):
        return lax.rem(cx + d, 4) * 4 + cy if axis == 0 else cx * 4 + lax.rem(cy + d, 4)

    mine = (cx, cy)
    wide = (wide_a, wide_b)
    tight = (gath_a, gath_b)

    def s1_copy(axis, d):
        here = mine[axis]
        return remote(
            coarse.at[pl.ds(2 * axis, 2)],
            wide[axis].at[here],
            s1_send.at[axis, d],
            s1_recv.at[axis, here],
            (r, line(axis, d)),
        )

    def s1_arrival(axis, d):
        there = lax.rem(mine[axis] + d, 4)
        ref = wide[axis].at[there]
        return remote(ref, ref, s1_send.at[axis, d], s1_recv.at[axis, there], (r, line(axis, d)))

    def cs_copy(axis, d):
        return remote(
            cs.at[c], cs.at[c], cs_send.at[axis, d], cs_recv.at[axis, mine[axis]], (r, line(axis, d))
        )

    def cs_arrival(axis, d):
        ref = cs.at[line(axis, d)]
        there = lax.rem(mine[axis] + d, 4)
        return remote(ref, ref, cs_send.at[axis, d], cs_recv.at[axis, there], (r, line(axis, d)))

    def group_copy(d):
        group = pl.ds(4 * cx, 4)
        return remote(cs.at[group], cs_all.at[group], cs_send.at[2, d], cs_recv.at[2, cx], (r, line(0, d)))

    def group_arrival(d):
        there = lax.rem(cx + d, 4)
        ref = cs_all.at[pl.ds(4 * there, 4)]
        return remote(ref, ref, cs_send.at[2, d], cs_recv.at[2, there], (r, line(0, d)))

    for d in (2, 1, 3):
        for axis in range(2):
            cs_copy(axis, d).start()
    for d in (2, 1, 3):
        for axis in range(2):
            s1_copy(axis, d).start()
    for axis in range(2):
        wide[axis][mine[axis]] = coarse[2 * axis : 2 * axis + 2]
    for copy in halo_copies(COT, False):
        copy.start()
    lax.fori_loop(0, FR, shift_cot, 0, unroll=4)
    for axis in (1, 0):
        for d in range(1, 4):
            cs_copy(axis, d).wait_send()
            cs_arrival(axis, d).wait_recv()
    cs_all[pl.ds(4 * cx, 4)] = cs[pl.ds(4 * cx, 4)]

    def s2_copy(axis, d):
        here = mine[1 - axis]
        return remote(
            slab.at[axis, d],
            tight[axis].at[pl.ds(4 * here, 4)],
            s2_send.at[axis, d],
            s2_recv.at[axis, here],
            (r, line(1 - axis, d)),
        )

    def s2_arrival(axis, d):
        there = lax.rem(mine[1 - axis] + d, 4)
        ref = tight[axis].at[pl.ds(4 * there, 4)]
        return remote(ref, ref, s2_send.at[axis, d], s2_recv.at[axis, there], (r, line(1 - axis, d)))

    def cut(axis, to):
        pick = one_hot(iota((256, 128), 0) == iota((256, 128), 1) + cs[to][0:1, :])
        return dot(wide[axis][...].reshape(512, 256), pick).astype(BF16).reshape(4, 2, CH, CW)

    for axis in range(2):
        for d in range(1, 4):
            s1_arrival(axis, d).wait_recv()
        for d in (2, 1, 3):
            slab[axis, d] = cut(axis, line(1 - axis, d))
            s2_copy(axis, d).start()
    for d in (2, 1, 3):
        group_copy(d).start()
    for axis in range(2):
        tight[axis][pl.ds(4 * mine[1 - axis], 4)] = cut(axis, c)

    halo_near(COT)
    halo_corners(COT)
    set_pair_fix(COT, wb2)

    def hidden_grad(p, _):
        t0, t1 = conv_pair(wb2, v_cot, p)
        hgrad[pl.ds(2 * p, 2), :, 0:128] = t0.reshape(2, CH, 128)
        hgrad[pl.ds(2 * p, 2), :, 128:256] = t1.reshape(2, CH, 128)
        return 0

    lax.fori_loop(0, FR // 2, hidden_grad, 0, unroll=4)

    for d in range(1, 4):
        group_copy(d).wait_send()
        group_arrival(d).wait_recv()

    def set_spot(n, _):
        start = cs_all[n][0:1, :]
        start = jnp.concatenate([start, start], axis=1)
        spots[n] = one_hot(iota((CW, 256), 1) == iota((CW, 256), 0) + start)
        return 0

    lax.fori_loop(0, NC, set_spot, 0)

    for axis in range(2):
        for d in range(1, 4):
            s1_copy(axis, d).wait_send()
            s2_copy(axis, d).wait_send()
            s2_arrival(axis, d).wait_recv()

    def pass_on(n):
        half, src, dst, count, dr = (
            (0, 11, NC, 1, 1),
            (0, 15, NC + 1, 1, 1),
            (0, 0, NC + 2, 1, -1),
            (0, 4, NC + 3, 1, -1),
            (1, 14, NC, 2, 1),
            (1, 0, NC + 2, 2, -1),
        )[n]
        return remote(
            tight[half].at[pl.ds(src, count)],
            tight[half].at[pl.ds(dst, count)],
            po_send.at[n],
            po_recv.at[n],
            (row_at(dr), c),
        )

    for n in range(6):
        pass_on(n).start()
    for n in range(6):
        pass_on(n).wait()

    first_block = r * NC - HB
    for k in range(K):
        near = jnp.clip(block_ids[0, k] - first_block, 0, NB - 1)
        own = jnp.clip(near - HB, 0, NC - 1)
        outer = jnp.where(near < HB, NC + near, near)
        inside = (near >= HB) & (near < NC + HB)
        for half, at in ((0, lax.rem(own, 4) * 4 + lax.div(own, 4)), (1, own)):
            piece = tight[half][jnp.where(inside, at, outer)]
            for g in range(4):
                row = 64 * k + 32 * half
                pieces[g, row : row + 32, :] = piece[:, 16 * g : 16 * g + 16, :].reshape(32, CW)
    for g in range(4):
        sec[:, 16 * g : 16 * g + 16, :] = dot(lmat[...], pieces[g]).astype(BF16).reshape(FR, 16, CW)

    def regrid(q, _):
        flat = sec[pl.ds(4 * q, 4)].reshape(256, CW)
        v_in[pl.ds(1 + 4 * q, 4), FS:CIN, :] = dot(flat, cols[...]).astype(BF16).reshape(4, CH, 256)
        return 0

    lax.fori_loop(0, FR // 4, regrid, 0, unroll=4)

    halo_start(INP)

    def first_row(h, _):
        prod = dot(wf1[:, 0 : 3 * CIN], v_in[pl.ds(h, 3)].reshape(3 * CIN, 256))
        t0, t1 = combine(prod, CH, 0.0)
        pre[h, :, 0:128] = t0
        pre[h, :, 128:256] = t1
        return 0

    lax.fori_loop(1, FR - 1, first_row, 0, unroll=4)

    halo_near(INP)
    set_ring(INP, False)
    first_row(0, 0)
    first_row(FR - 1, 0)

    def set_first_fix():
        set_fix(INP, wf1[0:CH, 0 : 3 * CIN], wf1[2 * CH : 3 * CH, 0 : 3 * CIN])

    set_first_fix()

    def activate(h, _):
        ends = fix_of(h)
        t0 = pre[h, :, 0:128] + jnp.where(lane == 0, ends, 0.0)
        t1 = pre[h, :, 128:256] + jnp.where(lane == 127, ends, 0.0)
        back = []
        for half, t in ((0, t0), (1, t1)):
            at = slice(128 * half, 128 * half + 128)
            s = 1.0 / (1.0 + jnp.exp(-t))
            v_hid[h + 1, :, at] = (t * s).astype(BF16)
            grad = hgrad[h, :, at] * (s * (1.0 + t * (1.0 - s)))
            v_act[h + 1, :, at] = grad.astype(BF16)
            back.append(grad)
        put_shifted(g_act, h, back[0], back[1], 1)
        return 0

    lax.fori_loop(1, FR - 1, activate, 0, unroll=4)
    halo_corners(INP)
    set_first_fix()
    activate(0, 0)
    activate(FR - 1, 0)

    halo_start(HID)
    halo_start(ACT)

    edges = (one_hot(lax.rem(lane, 2) == 0), one_hot(lax.rem(lane, 2) == 1))

    def edge_terms(x, of):
        ring, chans = bufs[x][3], bufs[x][4]
        mine = bufs[of][1][...]
        both = jnp.concatenate([mine * edges[0], mine * edges[1]], axis=0)
        return dot_nt(both, ring[...].reshape(3 * chans, 128))

    acc1[...] = jnp.zeros(acc1.shape, F32)

    def first_grad(q, _):
        left = [g_act[4 * q + i].reshape(3 * CH, 256) for i in range(4)]
        right = [v_in[pl.ds(4 * q + i, 3)].reshape(3 * CIN, 256) for i in range(4)]
        acc1[:, 0 : 3 * CIN] += dot_nt(jnp.concatenate(left, axis=1), jnp.concatenate(right, axis=1))
        return 0

    lax.fori_loop(0, FR // 4, first_grad, 0, unroll=2)

    extra = edge_terms(INP, ACT)
    acc1[0:CH, 0 : 3 * CIN] += extra[0:CH]
    acc1[2 * CH :, 0 : 3 * CIN] += extra[CH:]

    def w1_copy(n):
        to = peer(n)
        return remote(gbuf.at[to], gpart.at[c], w1_send.at[n], w1_recv.at[c], (r, to))

    def keep(which, acc):
        for half in range(2):
            rows = acc[0 : 3 * CH, 128 * half : 128 * half + 128]
            gbuf[8 * half : 8 * half + 8, which] = rows.reshape(8, 24, 128)

    keep(0, acc1)

    halo_near(HID)
    acc2[...] = jnp.zeros(acc2.shape, F32)

    def second_grad(q, _):
        left = [g_cot[pl.ds(4 * q + i, 2)].reshape(6 * CH, 256) for i in (0, 2)]
        right = [v_hid[pl.ds(4 * q + i, 4)].reshape(256, 256) for i in (0, 2)]
        acc2[...] += dot_nt(jnp.concatenate(left, axis=1), jnp.concatenate(right, axis=1))
        return 0

    lax.fori_loop(0, FR // 4, second_grad, 0, unroll=2)
    halo_near(ACT)
    halo_corners(HID)
    extra = edge_terms(HID, COT)
    acc2[0 : 3 * CH, :] += pltpu.roll(acc2[3 * CH :, :], 192, 1)
    acc2[0:CH, 0 : 3 * CH] += extra[0:CH]
    acc2[2 * CH : 3 * CH, 0 : 3 * CH] += extra[CH:]
    keep(1, acc2)
    for n in range(NC - 1):
        w1_copy(n).start()
    gpart[c] = gbuf[c]

    def w2_copy(d):
        return remote(grow.at[r], grow.at[r], w2_send.at[d], w2_recv.at[r], (row_at(d), c))

    def w2_arrival(d):
        there = grow.at[row_at(d)]
        return remote(there, there, w2_send.at[d], w2_recv.at[row_at(d)], (row_at(d), c))

    def w3_copy(n):
        here = grads_out.at[c]
        return remote(here, here, w3_send.at[n], w3_recv.at[c], (r, peer(n)))

    def w3_arrival(n):
        there = grads_out.at[source(n)]
        return remote(there, there, w3_send.at[n], w3_recv.at[source(n)], (r, source(n)))

    def sum_col():
        for n in range(NC - 1):
            w1_copy(n).wait_send()
            there = gpart.at[source(n)]
            remote(there, there, w1_send.at[n], w1_recv.at[source(n)], (r, source(n))).wait_recv()
        total = gpart[0]
        for n in range(1, NC):
            total = total + gpart[n]
        grow[r] = total
        for d in range(1, NR):
            w2_copy(d).start()

    def spread_sum():
        for d in range(1, NR):
            w2_copy(d).wait_send()
            w2_arrival(d).wait_recv()
        total = grow[0]
        for n in range(1, NR):
            total = total + grow[n]
        grads_out[c] = total
        for n in range(NC - 1):
            w3_copy(n).start()

    set_ring(ACT, False)
    set_pair_fix(ACT, wb1)

    def cond_grad(p, _):
        t0, t1 = conv_pair(wb1, v_act, p)
        fine[pl.ds(2 * p, 2), :, 0:128] = t0.astype(BF16).reshape(2, CH, 128)
        fine[pl.ds(2 * p, 2), :, 128:256] = t1.astype(BF16).reshape(2, CH, 128)
        return 0

    lax.fori_loop(1, FR // 2 - 1, cond_grad, 0, unroll=4)
    halo_corners(ACT)
    set_pair_fix(ACT, wb1)
    cond_grad(0, 0)
    cond_grad(FR // 2 - 1, 0)

    def section_grad(q, _):
        flat = fine[pl.ds(8 * q, 8)].reshape(512, 256)
        sec[pl.ds(8 * q, 8)] = dot_nt(flat, cols[...]).astype(BF16).reshape(8, CH, CW)
        return 0

    lax.fori_loop(0, FR // 8, section_grad, 0)
    eye = one_hot(iota((256, 256), 0) == iota((256, 256), 1))
    lmat_t = dot_nt(eye, lmat[...]).astype(BF16)
    for g in range(4):
        part = dot(lmat_t, sec[:, 16 * g : 16 * g + 16, :].reshape(512, CW))
        pgrad[:, :, 16 * g : 16 * g + 16, :] = part.reshape(K, 4, 16, CW)

    def contribution(b):
        total = None
        for k in range(K):
            hit = (block_ids[0, k] - first_block == b).astype(F32)
            term = pgrad[k] * hit
            total = term if total is None else total + term
        return total

    def rh_copy(n):
        b, dr = ((0, -1), (1, -1), (NB - 2, 1), (NB - 1, 1))[n]
        return remote(sbuf.at[b], rhalo.at[n], rh_send.at[n], rh_recv.at[n], (row_at(dr), c))

    for n, b in enumerate((0, 1, NB - 2, NB - 1)):
        sbuf[b] = contribution(b).astype(BF16)
        rh_copy(n).start()

    def rs_copy(n):
        to = peer(n)
        return remote(sbuf.at[HB + to], rbuf.at[c], rs_send.at[n], rs_recv.at[c], (r, to))

    def is_inner(to):
        return (to >= HB) & (to < NC - HB)

    def send_inner(n):
        to = peer(n)

        @pl.when(is_inner(to))
        def _():
            sbuf[HB + to] = contribution(HB + to).astype(BF16)
            rs_copy(n).start()

    def send_outer(n):
        @pl.when(jnp.logical_not(is_inner(peer(n))))
        def _():
            rs_copy(n).start()

    for n in range(8):
        send_inner(n)
    for n, b in enumerate((NC, NC + 1, HB, HB + 1)):
        rh_copy(n).wait_recv()
        sbuf[b] = (contribution(b) + rhalo[n].astype(F32)).astype(BF16)
    for n in range(8, NC - 1):
        send_inner(n)
        send_outer(n)
        send_outer(n - 8)
    send_outer(7)

    @pl.when(is_inner(c))
    def _():
        sbuf[HB + c] = contribution(HB + c).astype(BF16)

    rbuf[c] = sbuf[HB + c]

    sum_col()
    set_pair_fix(HID, wf2)

    def second_level(p, _):
        t0, t1 = conv_pair(wf2, v_hid, p)
        fine[pl.ds(2 * p, 2), :, 0:128] = t0.astype(BF16).reshape(2, CH, 128)
        fine[pl.ds(2 * p, 2), :, 128:256] = t1.astype(BF16).reshape(2, CH, 128)
        return 0

    lax.fori_loop(0, FR // 4, second_level, 0, unroll=4)
    spread_sum()
    lax.fori_loop(FR // 4, FR // 2, second_level, 0, unroll=4)
    for c0 in range(0, CH, 16):
        for h0 in range(0, FR, 16):
            flat = fine[h0 : h0 + 16, c0 : c0 + 16, :].reshape(256, 256)
            cot[c0 : c0 + 16, h0 : h0 + 16, :] = dot(perm, flat).astype(BF16).reshape(16, 16, 256)
    out = pltpu.make_async_copy(cot, fine_hbm, out_sem)
    out.start()

    for q in range(4):
        senders = [source(n) if n < NC - 1 else c for n in range(4 * q, 4 * q + 4)]
        for n in range(4 * q, min(4 * q + 4, NC - 1)):
            rs_copy(n).wait_send()
            there = rbuf.at[source(n)]
            remote(there, there, rs_send.at[n], rs_recv.at[source(n)], (r, source(n))).wait_recv()
        flat = jnp.concatenate([rbuf[n].reshape(256, CW) for n in senders], axis=1)
        spot = jnp.concatenate([spots[n] for n in senders], axis=0)
        part = dot(flat, spot).reshape(4, CH, 256)
        coarse_out[...] = part if q == 0 else coarse_out[...] + part

    for n in range(4):
        rh_copy(n).wait_send()
    for n in range(NC - 1):
        w3_copy(n).wait_send()
        w3_arrival(n).wait_recv()
    out.wait()


def results(fine, grads, block, fine_out, first_out, second_out, coarse_out, rows, sums, held, first, second, sem):
    fetched = pltpu.make_async_copy(block, held, sem.at[0])
    moved = pltpu.make_async_copy(held, coarse_out, sem.at[1])
    summed = pltpu.make_async_copy(grads, sums, sem.at[2])
    parts = [pl.ds(16 * n, 16) for n in range(4)]
    arrivals = [pltpu.make_async_copy(fine.at[p], rows.at[p], sem.at[5 + n]) for n, p in enumerate(parts)]
    leaving = [pltpu.make_async_copy(rows.at[p], fine_out.at[p], sem.at[9 + n]) for n, p in enumerate(parts)]
    summed.start()
    for copy in arrivals:
        copy.start()
    fetched.start()
    for n in range(4):
        arrivals[n].wait()
        leaving[n].start()
    fetched.wait()
    moved.start()
    summed.wait()
    both = [
        jnp.concatenate([sums[0:8, w].reshape(3 * CH, 128), sums[8:16, w].reshape(3 * CH, 128)], axis=1)
        for w in range(2)
    ]
    for a in range(3):
        for e in range(3):
            first[a, e] = both[0][e * CH : (e + 1) * CH, a * CIN : (a + 1) * CIN]
            second[a, e] = both[1][e * CH : (e + 1) * CH, a * CH : (a + 1) * CH]
    last = [
        pltpu.make_async_copy(first, first_out, sem.at[3]),
        pltpu.make_async_copy(second, second_out, sem.at[4]),
    ]
    for copy in last:
        copy.start()
    for copy in leaving + last + [moved]:
        copy.wait()


def local(
    coarse,
    noisy,
    cotangent,
    interp_rows,
    interp_cols,
    first_weight,
    second_weight,
    block_ids,
    weight_ids,
    col_start,
):
    smem = pl.BlockSpec(memory_space=pltpu.SMEM)
    vmem = pl.BlockSpec(memory_space=pltpu.VMEM)
    dma = pltpu.SemaphoreType.DMA
    fine, grads, block = pl.pallas_call(
        kernel,
        out_shape=(
            jax.ShapeDtypeStruct((CH, FR, 256), BF16),
            jax.ShapeDtypeStruct((NC, 2, 24, 128), F32),
            jax.ShapeDtypeStruct((4, CH, 256), F32),
        ),
        in_specs=[smem] * 3 + [pl.BlockSpec(memory_space=pl.ANY)] * 7,
        out_specs=(pl.BlockSpec(memory_space=pl.ANY), vmem, vmem),
        scratch_shapes=[
            pltpu.VMEM((4, CH, 256), BF16),
            pltpu.VMEM((FS, FR, 256), BF16),
            pltpu.VMEM((CH, FR, 256), BF16),
            pltpu.VMEM((8, 4, FR), BF16),
            pltpu.VMEM((CW, 256), BF16),
            pltpu.VMEM((3, 3, CH, CIN), BF16),
            pltpu.VMEM((3, 3, CH, CH), BF16),
            pltpu.VMEM((FR + 2, CH, 256), BF16),
            pltpu.VMEM((FR + 2, CIN, 256), BF16),
            pltpu.VMEM((FR + 2, CH, 256), BF16),
            pltpu.VMEM((FR + 2, CH, 256), BF16),
            pltpu.VMEM((FR, 3, CH, 256), BF16),
            pltpu.VMEM((FR, 3, CH, 256), BF16),
            pltpu.VMEM((FR, CH, 256), F32),
            pltpu.VMEM((FR, CH, 256), F32),
            pltpu.VMEM((FR, CH, 256), BF16),
            pltpu.VMEM((3 * CH, 256), BF16),
            pltpu.VMEM((3, 2, CH, 256), BF16),
            pltpu.VMEM((3, 2, CH, 256), BF16),
            pltpu.VMEM((3, 2, CH, 256), BF16),
            pltpu.VMEM((3, CH, 128), BF16),
            pltpu.VMEM((CIN, 128), BF16),
            pltpu.VMEM((3, 6, CH, 128), BF16),
            pltpu.VMEM((6, CIN, 128), BF16),
            pltpu.VMEM((3, 3, CH, 128), BF16),
            pltpu.VMEM((3, CIN, 128), BF16),
            pltpu.VMEM((CH, 128), F32),
            pltpu.VMEM((NC, 8, 128), jnp.int32),
            pltpu.VMEM((NC, 8, 128), jnp.int32),
            pltpu.VMEM((2, 4, 4, 2, CH, CW), BF16),
            pltpu.VMEM((4, 2, CH, 256), BF16),
            pltpu.VMEM((4, 2, CH, 256), BF16),
            pltpu.VMEM((NB, 2, CH, CW), BF16),
            pltpu.VMEM((NB, 2, CH, CW), BF16),
            pltpu.VMEM((4, 256, CW), BF16),
            pltpu.VMEM((512, 256), BF16),
            pltpu.VMEM((FR, CH, CW), BF16),
            pltpu.VMEM((K, 4, CH, CW), F32),
            pltpu.VMEM((NB, 4, CH, CW), BF16),
            pltpu.VMEM((NC, 4, CH, CW), BF16),
            pltpu.VMEM((4, 4, CH, CW), BF16),
            pltpu.VMEM((NC, CW, 256), BF16),
            pltpu.VMEM((3 * CH, 256), F32),
            pltpu.VMEM((6 * CH, 256), F32),
            pltpu.VMEM((NC, 2, 24, 128), F32),
            pltpu.VMEM((NC, 2, 24, 128), F32),
            pltpu.VMEM((NR, 2, 24, 128), F32),
            dma((4, 8)),
            dma((4, 8)),
            dma((3, 4)),
            dma((3, 4)),
            dma((2, 4)),
            dma((2, 4)),
            dma((2, 4)),
            dma((2, 4)),
            dma((6,)),
            dma((6,)),
            dma((NC,)),
            dma((NC,)),
            dma((4,)),
            dma((4,)),
            dma((NC,)),
            dma((NC,)),
            dma((NR,)),
            dma((NR,)),
            dma((NC,)),
            dma((NC,)),
            dma,
            dma((7,)),
        ],
        compiler_params=pltpu.CompilerParams(
            collective_id=0, has_side_effects=True, vmem_limit_bytes=56 * 1024 * 1024
        ),
        cost_estimate=pl.CostEstimate(flops=4_000_000_000, bytes_accessed=8_000_000, transcendentals=524_288),
    )(
        block_ids,
        weight_ids,
        col_start,
        coarse,
        noisy,
        cotangent,
        interp_rows.transpose(0, 2, 1),
        interp_cols,
        first_weight,
        second_weight,
    )
    anywhere = pl.BlockSpec(memory_space=pl.ANY)
    return pl.pallas_call(
        results,
        out_shape=(
            jax.ShapeDtypeStruct((CH, FR, 256), BF16),
            jax.ShapeDtypeStruct((3, 3, CH, CIN), F32),
            jax.ShapeDtypeStruct((3, 3, CH, CH), F32),
            jax.ShapeDtypeStruct((4, CH, 256), F32),
        ),
        in_specs=[anywhere] * 3,
        out_specs=(anywhere,) * 4,
        scratch_shapes=[
            pltpu.VMEM((CH, FR, 256), BF16),
            pltpu.VMEM((NC, 2, 24, 128), F32),
            pltpu.VMEM((4, CH, 256), F32),
            pltpu.VMEM((3, 3, CH, CIN), F32),
            pltpu.VMEM((3, 3, CH, CH), F32),
            dma((13,)),
        ],
        compiler_params=pltpu.CompilerParams(vmem_limit_bytes=60 * 1024 * 1024),
        cost_estimate=pl.CostEstimate(flops=270_000_000, bytes_accessed=4_000_000, transcendentals=0),
    )(fine, grads, block)


def solution(mesh):
    in_specs = (
        P(("row", "col"), None, None),
        P(None, "row", "col"),
        P(None, "row", "col"),
        P(),
        P(),
        P(),
        P(),
        P(("row", "col"), None),
        P(("row", "col"), None),
        P("col"),
    )
    out_specs = (P(None, "row", "col"), P(), P(), P(("row", "col"), None, None))
    return jax.shard_map(local, mesh=mesh, in_specs=in_specs, out_specs=out_specs, check_vma=False)
```

```python
import jax
import jax.numpy as jnp
from jax import lax
from jax.experimental import pallas as pl
from jax.experimental.pallas import tpu as pltpu
from jax.sharding import PartitionSpec as P

F32 = jnp.float32
BF16 = jnp.bfloat16
MESH = pl.DeviceIdType.MESH

NR = 8
NC = 16
HB = 2
K = 4
FR = 32
CH = 64
FS = 16
CIN = 80
CW = 128
NB = NC + 2 * HB

PEERS = (
    ((2, 2), (1, 2), (2, 1), (3, 2), (2, 3), (1, 1), (3, 3), (1, 3))
    + ((3, 1), (0, 2), (2, 0), (0, 1), (1, 0), (0, 3), (3, 0))
)
COT, INP, HID, ACT = range(4)


def iota(shape, dim):
    return lax.broadcasted_iota(jnp.int32, shape, dim)


def dot(a, b):
    return jnp.dot(a, b, preferred_element_type=F32)


def dot_nt(a, b):
    return lax.dot_general(a, b, (((1,), (1,)), ((), ())), preferred_element_type=F32)


def dot_tn(a, b):
    return lax.dot_general(a, b, (((0,), (0,)), ((), ())), preferred_element_type=F32)


def one_hot(hit):
    return jnp.where(hit, 1.0, 0.0).astype(BF16)


def permutation():
    i0, i1 = iota((256, 256), 0), iota((256, 256), 1)
    return one_hot((lax.rem(i0, 16) == lax.div(i1, 16)) & (lax.div(i0, 16) == lax.rem(i1, 16)))


def kernel(
    block_ids,
    weight_ids,
    col_start,
    *rest,
):
    hbm, rest = rest[:7], rest[7:]
    body(block_ids, weight_ids, col_start, hbm, *rest)


def body(
    block_ids,
    weight_ids,
    col_start,
    hbm,
    fine_hbm,
    grads_out,
    coarse_out,
    coarse,
    noisy,
    cot,
    rows,
    cols,
    first_w,
    second_w,
    v_cot,
    v_in,
    v_hid,
    v_act,
    g_cot,
    g_act,
    hgrad,
    pre,
    fine,
    wf1,
    wf2,
    wb1,
    wb2,
    edge,
    edge_in,
    edge_got,
    edge_got_in,
    around,
    around_in,
    fix,
    cs,
    cs_all,
    slab,
    wide_a,
    wide_b,
    gath_a,
    gath_b,
    pieces,
    lmat,
    sec,
    pgrad,
    sbuf,
    rbuf,
    rhalo,
    spots,
    acc1,
    acc2,
    gbuf,
    gpart,
    grow,
    x_send,
    x_recv,
    cs_send,
    cs_recv,
    s1_send,
    s1_recv,
    s2_send,
    s2_recv,
    po_send,
    po_recv,
    rs_send,
    rs_recv,
    rh_send,
    rh_recv,
    w1_send,
    w1_recv,
    w2_send,
    w2_recv,
    w3_send,
    w3_recv,
    out_sem,
    in_sem,
):
    r = lax.axis_index("row")
    c = lax.axis_index("col")
    lane = iota((CH, 128), 1)

    def row_at(d):
        return lax.rem(r + (d + NR), NR)

    def col_at(d):
        return lax.rem(c + (d + NC), NC)

    def peer(n):
        dx, dy = PEERS[n]
        return lax.rem(lax.div(c, 4) + dx, 4) * 4 + lax.rem(c + dy, 4)

    def source(n):
        dx, dy = PEERS[n]
        return lax.rem(lax.div(c, 4) + 4 - dx, 4) * 4 + lax.rem(c + 4 - dy, 4)

    def remote(src, dst, send, recv, device):
        return pltpu.make_async_remote_copy(
            src_ref=src, dst_ref=dst, send_sem=send, recv_sem=recv, device_id=device, device_id_type=MESH
        )

    barrier = pltpu.get_barrier_semaphore()
    met = [(0, d) for d in range(1, NC)] + [(d, 0) for d in range(1, NR)]
    for dr, dc in met:
        pl.semaphore_signal(barrier, inc=1, device_id=(row_at(dr), col_at(dc)), device_id_type=MESH)

    fetched = [
        pltpu.make_async_copy(src, dst, in_sem.at[n])
        for n, (src, dst) in enumerate(zip(hbm, (coarse, noisy, cot, rows, cols, first_w, second_w)))
    ]
    for n in (2, 1, 5, 6, 3, 0, 4):
        fetched[n].start()
    for copy in fetched:
        copy.wait()
    perm = permutation()

    def flip_in(src, dst, c0, h0):
        block = src[c0 : c0 + 16, h0 : h0 + 16, :].reshape(256, 256)
        dst[1 + h0 : 17 + h0, c0 : c0 + 16, :] = dot(perm, block).astype(BF16).reshape(16, 16, 256)

    for c0 in range(0, CH, 16):
        for h0 in range(0, FR, 16):
            flip_in(cot, v_cot, c0, h0)
    for h0 in range(0, FR, 16):
        flip_in(noisy, v_in, 0, h0)

    def place(ins, at):
        return one_hot(iota((ins, 256), 1) == iota((ins, 256), 0) + at)

    wf1[...] = sum(dot(first_w[a].reshape(3 * CH, CIN), place(CIN, a * CIN)) for a in range(3)).astype(BF16)
    for row in range(2):
        flat = sum(dot(second_w[a].reshape(3 * CH, CH), place(CH, (a + row) * CH)) for a in range(3))
        wf2[:, row] = flat.astype(BF16).reshape(3, CH, 256)
    for w, back, ins, skip in ((first_w, wb1, CIN, FS), (second_w, wb2, CH, 0)):
        pick = one_hot(iota((CH, ins), 1) == iota((CH, ins), 0) + skip)
        none = jnp.zeros((CH, ins), BF16)
        for e in range(3):
            taps = [w[2 - a, 2 - e] for a in range(3)]
            back[e, 0] = dot_nt(pick, jnp.concatenate(taps + [none], axis=0)).astype(BF16)
            back[e, 1] = dot_nt(pick, jnp.concatenate([none] + taps, axis=0)).astype(BF16)

    lane256 = iota((FR, 256), 1)
    repeat = one_hot(lax.rem(lax.div(iota((4, 256), 1), 16), 4) == iota((4, 256), 0))
    table = jnp.zeros((FR, 256), F32)
    for k in range(K):
        table = jnp.where(lax.div(lane256, 64) == k, dot_tn(rows[weight_ids[0, k]], repeat), table)
    spread = one_hot(lax.div(iota((512, FR), 0), 16) == iota((512, FR), 1))
    same = lax.rem(iota((512, 256), 0), 16) == lax.rem(iota((512, 256), 1), 16)
    lmat[...] = jnp.where(same, dot(spread, table.astype(BF16)), 0.0).astype(BF16)

    def put_shifted(g, h, t0, t1, count):
        low = iota(t0.shape, 1) == 0
        high = iota(t0.shape, 1) == 127
        r0, r1 = pltpu.roll(t0, 1, 1), pltpu.roll(t1, 1, 1)
        s0, s1 = pltpu.roll(t0, 127, 1), pltpu.roll(t1, 127, 1)

        def put(e, half, value):
            g[pl.ds(h, count), e, :, 128 * half : 128 * half + 128] = value.astype(BF16).reshape(count, CH, 128)

        put(0, 0, jnp.where(high, s1, s0))
        put(0, 1, jnp.where(high, 0.0, s1))
        put(1, 0, t0)
        put(1, 1, t1)
        put(2, 0, jnp.where(low, 0.0, r0))
        put(2, 1, jnp.where(low, r0, r1))

    def shift_cot(h, _):
        put_shifted(g_cot, h, v_cot[h + 1, :, 0:128].astype(F32), v_cot[h + 1, :, 128:256].astype(F32), 1)
        return 0

    bufs = {
        COT: (v_cot, edge.at[0], edge_got.at[0], around.at[0], CH),
        INP: (v_in, edge_in, edge_got_in, around_in, CIN),
        HID: (v_hid, edge.at[1], edge_got.at[1], around.at[1], CH),
        ACT: (v_act, edge.at[2], edge_got.at[2], around.at[2], CH),
    }

    def halo_pack(x):
        v, e, _, _, chans = bufs[x]
        at = iota((chans, 128), 1)

        def pack(h, held):
            t0 = v[h + 1, :, 0:128].astype(F32)
            t1 = v[h + 1, :, 128:256].astype(F32)
            ends = pltpu.roll(jnp.where(at == 127, t1, t0), 2 * h, 1)
            return jnp.where(((at - 2 * h + 1) & 127) < 2, ends, held)

        e[...] = lax.fori_loop(0, FR, pack, jnp.zeros((chans, 128), F32), unroll=8).astype(BF16)

    def halo_copies(x, far):
        v, e, got, _, _ = bufs[x]

        def one(n, src, dst, dr, dc):
            return remote(src, dst, x_send.at[x, n], x_recv.at[x, n], (row_at(dr), col_at(dc)))

        if far:
            return [
                one(2, got.at[0], got.at[2], 1, 0),
                one(3, got.at[1], got.at[3], 1, 0),
                one(4, got.at[0], got.at[4], -1, 0),
                one(5, got.at[1], got.at[5], -1, 0),
            ]
        return [
            one(0, e, got.at[0], 0, 1),
            one(1, e, got.at[1], 0, -1),
            one(6, v.at[FR], v.at[0], 1, 0),
            one(7, v.at[1], v.at[FR + 1], -1, 0),
        ]

    def halo_start(x):
        halo_pack(x)
        for copy in halo_copies(x, False):
            copy.start()

    def set_ring(x, corners):
        _, _, got, ring, chans = bufs[x]
        at = iota((chans, 128), 1)
        top = (r > 0).astype(F32)
        bottom = (r < NR - 1).astype(F32)
        west = (c > 0).astype(F32)
        east = (c < NC - 1).astype(F32)

        def side(mid, up, down, by, by_corner, first, there):
            cells = pltpu.roll(got[mid].astype(F32), by, 1)
            if corners:
                b = pltpu.roll(got[up].astype(F32), by_corner, 1) * top
                d = pltpu.roll(got[down].astype(F32), by_corner, 1) * bottom
                last = (first + 2 * FR + 2) % 128
                cells = jnp.where(at == first, b, jnp.where(at == last, d, cells))
            return cells * there

        both = jnp.where(lax.rem(at, 2) == 0, side(0, 2, 4, 3, 67, 0, west), side(1, 3, 5, 1, 65, 127, east))
        ring[0] = both.astype(BF16)
        ring[1] = pltpu.roll(both, 126, 1).astype(BF16)
        ring[2] = pltpu.roll(both, 124, 1).astype(BF16)

    def halo_near(x):
        v, chans = bufs[x][0], bufs[x][4]
        near = halo_copies(x, False)
        for copy in near[:2]:
            copy.wait()
        for copy in halo_copies(x, True):
            copy.start()
        for copy in near[2:]:
            copy.wait()

        @pl.when(r == 0)
        def _():
            v[0] = jnp.zeros((chans, 256), BF16)

        @pl.when(r == NR - 1)
        def _():
            v[FR + 1] = jnp.zeros((chans, 256), BF16)

    def halo_corners(x):
        for copy in halo_copies(x, True):
            copy.wait()
        set_ring(x, True)

    def combine(prod, n, ends):
        at = iota((n, 128), 1)
        a0, a1 = prod[0:n, 0:128], prod[0:n, 128:256]
        b0, b1 = prod[n : 2 * n, 0:128], prod[n : 2 * n, 128:256]
        d0, d1 = prod[2 * n : 3 * n, 0:128], prod[2 * n : 3 * n, 128:256]
        r0, r1 = pltpu.roll(a0, 1, 1), pltpu.roll(a1, 1, 1)
        s0, s1 = pltpu.roll(d0, 127, 1), pltpu.roll(d1, 127, 1)
        t0 = b0 + jnp.where(at == 0, ends, r0) + jnp.where(at == 127, s1, s0)
        t1 = b1 + jnp.where(at == 0, r0, r1) + jnp.where(at == 127, ends, s1)
        return t0, t1

    def set_fix(x, left, right):
        ring, chans = bufs[x][3], bufs[x][4]
        cells = ring[...].reshape(3 * chans, 128)
        fix[...] = jnp.where(lax.rem(lane, 2) == 0, dot(left, cells), dot(right, cells))

    def fix_of(h):
        return pltpu.roll(fix[...], lax.rem(128 - 2 * h, 128), 1)

    def set_pair_fix(x, weights):
        set_fix(x, weights[0, 0][:, 0 : 3 * CH], weights[2, 0][:, 0 : 3 * CH])

    def conv_pair(weights, v, p):
        prod = dot(weights[...].reshape(6 * CH, 256), v[pl.ds(2 * p, 4)].reshape(256, 256))
        ends = jnp.concatenate([fix_of(2 * p), fix_of(2 * p + 1)], axis=0)
        return combine(prod, 2 * CH, ends)

    halo_pack(COT)

    pl.semaphore_wait(barrier, len(met))
    for copy in halo_copies(COT, False):
        copy.start()

    cs[c] = jnp.full((8, 128), col_start[0], jnp.int32)

    cx, cy = lax.div(c, 4), lax.rem(c, 4)

    def line(axis, d):
        return lax.rem(cx + d, 4) * 4 + cy if axis == 0 else cx * 4 + lax.rem(cy + d, 4)

    mine = (cx, cy)
    wide = (wide_a, wide_b)
    tight = (gath_a, gath_b)

    def s1_copy(axis, d):
        here = mine[axis]
        return remote(
            coarse.at[pl.ds(2 * axis, 2)],
            wide[axis].at[here],
            s1_send.at[axis, d],
            s1_recv.at[axis, here],
            (r, line(axis, d)),
        )

    def s1_arrival(axis, d):
        there = lax.rem(mine[axis] + d, 4)
        ref = wide[axis].at[there]
        return remote(ref, ref, s1_send.at[axis, d], s1_recv.at[axis, there], (r, line(axis, d)))

    def cs_copy(axis, d):
        return remote(
            cs.at[c], cs.at[c], cs_send.at[axis, d], cs_recv.at[axis, mine[axis]], (r, line(axis, d))
        )

    def cs_arrival(axis, d):
        ref = cs.at[line(axis, d)]
        there = lax.rem(mine[axis] + d, 4)
        return remote(ref, ref, cs_send.at[axis, d], cs_recv.at[axis, there], (r, line(axis, d)))

    def group_copy(d):
        group = pl.ds(4 * cx, 4)
        return remote(cs.at[group], cs_all.at[group], cs_send.at[2, d], cs_recv.at[2, cx], (r, line(0, d)))

    def group_arrival(d):
        there = lax.rem(cx + d, 4)
        ref = cs_all.at[pl.ds(4 * there, 4)]
        return remote(ref, ref, cs_send.at[2, d], cs_recv.at[2, there], (r, line(0, d)))

    for d in (2, 1, 3):
        for axis in range(2):
            cs_copy(axis, d).start()
    for d in (2, 1, 3):
        for axis in range(2):
            s1_copy(axis, d).start()
    for axis in range(2):
        wide[axis][mine[axis]] = coarse[2 * axis : 2 * axis + 2]
    lax.fori_loop(0, FR, shift_cot, 0, unroll=4)
    for axis in (1, 0):
        for d in range(1, 4):
            cs_copy(axis, d).wait_send()
            cs_arrival(axis, d).wait_recv()
    cs_all[pl.ds(4 * cx, 4)] = cs[pl.ds(4 * cx, 4)]

    def s2_copy(axis, d):
        here = mine[1 - axis]
        return remote(
            slab.at[axis, d],
            tight[axis].at[pl.ds(4 * here, 4)],
            s2_send.at[axis, d],
            s2_recv.at[axis, here],
            (r, line(1 - axis, d)),
        )

    def s2_arrival(axis, d):
        there = lax.rem(mine[1 - axis] + d, 4)
        ref = tight[axis].at[pl.ds(4 * there, 4)]
        return remote(ref, ref, s2_send.at[axis, d], s2_recv.at[axis, there], (r, line(1 - axis, d)))

    def cut(axis, to):
        pick = one_hot(iota((256, 128), 0) == iota((256, 128), 1) + cs[to][0:1, :])
        return dot(wide[axis][...].reshape(512, 256), pick).astype(BF16).reshape(4, 2, CH, CW)

    for axis in range(2):
        for d in range(1, 4):
            s1_arrival(axis, d).wait_recv()
        for d in (2, 1, 3):
            slab[axis, d] = cut(axis, line(1 - axis, d))
            s2_copy(axis, d).start()
    for d in (2, 1, 3):
        group_copy(d).start()
    for axis in range(2):
        tight[axis][pl.ds(4 * mine[1 - axis], 4)] = cut(axis, c)

    halo_near(COT)

    def hidden_grad(p, _):
        t0, t1 = conv_pair(wb2, v_cot, p)
        hgrad[pl.ds(2 * p, 2), :, 0:128] = t0.reshape(2, CH, 128)
        hgrad[pl.ds(2 * p, 2), :, 128:256] = t1.reshape(2, CH, 128)
        return 0


    for d in range(1, 4):
        group_copy(d).wait_send()
        group_arrival(d).wait_recv()

    def set_spot(n, _):
        start = cs_all[n][0:1, :]
        start = jnp.concatenate([start, start], axis=1)
        spots[n] = one_hot(iota((CW, 256), 1) == iota((CW, 256), 0) + start)
        return 0

    lax.fori_loop(0, NC, set_spot, 0)

    for axis in range(2):
        for d in range(1, 4):
            s1_copy(axis, d).wait_send()
            s2_copy(axis, d).wait_send()
            s2_arrival(axis, d).wait_recv()

    def pass_on(n):
        half, src, dst, count, dr = (
            (0, 11, NC, 1, 1),
            (0, 15, NC + 1, 1, 1),
            (0, 0, NC + 2, 1, -1),
            (0, 4, NC + 3, 1, -1),
            (1, 14, NC, 2, 1),
            (1, 0, NC + 2, 2, -1),
        )[n]
        return remote(
            tight[half].at[pl.ds(src, count)],
            tight[half].at[pl.ds(dst, count)],
            po_send.at[n],
            po_recv.at[n],
            (row_at(dr), c),
        )

    for n in range(6):
        pass_on(n).start()
    halo_corners(COT)
    set_pair_fix(COT, wb2)
    lax.fori_loop(0, FR // 2, hidden_grad, 0, unroll=4)
    for n in range(6):
        pass_on(n).wait()

    first_block = r * NC - HB
    for k in range(K):
        near = jnp.clip(block_ids[0, k] - first_block, 0, NB - 1)
        own = jnp.clip(near - HB, 0, NC - 1)
        outer = jnp.where(near < HB, NC + near, near)
        inside = (near >= HB) & (near < NC + HB)
        for half, at in ((0, lax.rem(own, 4) * 4 + lax.div(own, 4)), (1, own)):
            piece = tight[half][jnp.where(inside, at, outer)]
            for g in range(4):
                row = 64 * k + 32 * half
                pieces[g, row : row + 32, :] = piece[:, 16 * g : 16 * g + 16, :].reshape(32, CW)
    for g in range(4):
        sec[:, 16 * g : 16 * g + 16, :] = dot(lmat[...], pieces[g]).astype(BF16).reshape(FR, 16, CW)

    def regrid(q, _):
        flat = sec[pl.ds(4 * q, 4)].reshape(256, CW)
        v_in[pl.ds(1 + 4 * q, 4), FS:CIN, :] = dot(flat, cols[...]).astype(BF16).reshape(4, CH, 256)
        return 0

    lax.fori_loop(0, FR // 4, regrid, 0, unroll=4)

    halo_start(INP)

    def first_row(h, _):
        prod = dot(wf1[:, 0 : 3 * CIN], v_in[pl.ds(h, 3)].reshape(3 * CIN, 256))
        t0, t1 = combine(prod, CH, 0.0)
        pre[h, :, 0:128] = t0
        pre[h, :, 128:256] = t1
        return 0

    lax.fori_loop(1, FR - 1, first_row, 0, unroll=4)

    halo_near(INP)
    set_ring(INP, False)
    first_row(0, 0)
    first_row(FR - 1, 0)

    def set_first_fix():
        set_fix(INP, wf1[0:CH, 0 : 3 * CIN], wf1[2 * CH : 3 * CH, 0 : 3 * CIN])

    set_first_fix()

    def activate(h, _):
        ends = fix_of(h)
        t0 = pre[h, :, 0:128] + jnp.where(lane == 0, ends, 0.0)
        t1 = pre[h, :, 128:256] + jnp.where(lane == 127, ends, 0.0)
        back = []
        for half, t in ((0, t0), (1, t1)):
            at = slice(128 * half, 128 * half + 128)
            s = 1.0 / (1.0 + jnp.exp(-t))
            v_hid[h + 1, :, at] = (t * s).astype(BF16)
            grad = hgrad[h, :, at] * (s * (1.0 + t * (1.0 - s)))
            v_act[h + 1, :, at] = grad.astype(BF16)
            back.append(grad)
        put_shifted(g_act, h, back[0], back[1], 1)
        return 0

    lax.fori_loop(1, FR - 1, activate, 0, unroll=4)
    halo_corners(INP)
    set_first_fix()
    activate(0, 0)
    activate(FR - 1, 0)

    halo_start(HID)
    halo_start(ACT)

    edges = (one_hot(lax.rem(lane, 2) == 0), one_hot(lax.rem(lane, 2) == 1))

    def edge_terms(x, of):
        ring, chans = bufs[x][3], bufs[x][4]
        mine = bufs[of][1][...]
        both = jnp.concatenate([mine * edges[0], mine * edges[1]], axis=0)
        return dot_nt(both, ring[...].reshape(3 * chans, 128))

    acc1[...] = jnp.zeros(acc1.shape, F32)

    def first_grad(q, _):
        left = [g_act[4 * q + i].reshape(3 * CH, 256) for i in range(4)]
        right = [v_in[pl.ds(4 * q + i, 3)].reshape(3 * CIN, 256) for i in range(4)]
        acc1[:, 0 : 3 * CIN] += dot_nt(jnp.concatenate(left, axis=1), jnp.concatenate(right, axis=1))
        return 0

    lax.fori_loop(0, FR // 4, first_grad, 0, unroll=2)

    extra = edge_terms(INP, ACT)
    acc1[0:CH, 0 : 3 * CIN] += extra[0:CH]
    acc1[2 * CH :, 0 : 3 * CIN] += extra[CH:]

    def w1_copy(n):
        to = peer(n)
        return remote(gbuf.at[to], gpart.at[c], w1_send.at[n], w1_recv.at[c], (r, to))

    def keep(which, acc):
        for half in range(2):
            rows = acc[0 : 3 * CH, 128 * half : 128 * half + 128]
            gbuf[8 * half : 8 * half + 8, which] = rows.reshape(8, 24, 128)

    keep(0, acc1)

    halo_near(HID)
    acc2[...] = jnp.zeros(acc2.shape, F32)

    def second_grad(q, _):
        left = [g_cot[pl.ds(4 * q + i, 2)].reshape(6 * CH, 256) for i in (0, 2)]
        right = [v_hid[pl.ds(4 * q + i, 4)].reshape(256, 256) for i in (0, 2)]
        acc2[...] += dot_nt(jnp.concatenate(left, axis=1), jnp.concatenate(right, axis=1))
        return 0

    lax.fori_loop(0, FR // 4, second_grad, 0, unroll=2)
    halo_near(ACT)
    halo_corners(HID)
    extra = edge_terms(HID, COT)
    acc2[0 : 3 * CH, :] += pltpu.roll(acc2[3 * CH :, :], 192, 1)
    acc2[0:CH, 0 : 3 * CH] += extra[0:CH]
    acc2[2 * CH : 3 * CH, 0 : 3 * CH] += extra[CH:]
    keep(1, acc2)
    for n in range(NC - 1):
        w1_copy(n).start()
    gpart[c] = gbuf[c]

    def w2_copy(d):
        return remote(grow.at[r], grow.at[r], w2_send.at[d], w2_recv.at[r], (row_at(d), c))

    def w2_arrival(d):
        there = grow.at[row_at(d)]
        return remote(there, there, w2_send.at[d], w2_recv.at[row_at(d)], (row_at(d), c))

    def w3_copy(n):
        here = grads_out.at[c]
        return remote(here, here, w3_send.at[n], w3_recv.at[c], (r, peer(n)))

    def w3_arrival(n):
        there = grads_out.at[source(n)]
        return remote(there, there, w3_send.at[n], w3_recv.at[source(n)], (r, source(n)))

    def sum_col():
        for n in range(NC - 1):
            w1_copy(n).wait_send()
            there = gpart.at[source(n)]
            remote(there, there, w1_send.at[n], w1_recv.at[source(n)], (r, source(n))).wait_recv()
        total = gpart[0]
        for n in range(1, NC):
            total = total + gpart[n]
        grow[r] = total
        for d in range(1, NR):
            w2_copy(d).start()

    def spread_sum():
        for d in range(1, NR):
            w2_copy(d).wait_send()
            w2_arrival(d).wait_recv()
        total = grow[0]
        for n in range(1, NR):
            total = total + grow[n]
        grads_out[c] = total
        for n in range(NC - 1):
            w3_copy(n).start()

    set_ring(ACT, False)
    set_pair_fix(ACT, wb1)

    def cond_grad(p, _):
        t0, t1 = conv_pair(wb1, v_act, p)
        fine[pl.ds(2 * p, 2), :, 0:128] = t0.astype(BF16).reshape(2, CH, 128)
        fine[pl.ds(2 * p, 2), :, 128:256] = t1.astype(BF16).reshape(2, CH, 128)
        return 0

    lax.fori_loop(1, FR // 2 - 1, cond_grad, 0, unroll=4)
    halo_corners(ACT)
    set_pair_fix(ACT, wb1)
    cond_grad(0, 0)
    cond_grad(FR // 2 - 1, 0)

    def section_grad(q, _):
        flat = fine[pl.ds(8 * q, 8)].reshape(512, 256)
        sec[pl.ds(8 * q, 8)] = dot_nt(flat, cols[...]).astype(BF16).reshape(8, CH, CW)
        return 0

    lax.fori_loop(0, FR // 8, section_grad, 0)
    eye = one_hot(iota((256, 256), 0) == iota((256, 256), 1))
    lmat_t = dot_nt(eye, lmat[...]).astype(BF16)
    for g in range(4):
        part = dot(lmat_t, sec[:, 16 * g : 16 * g + 16, :].reshape(512, CW))
        pgrad[:, :, 16 * g : 16 * g + 16, :] = part.reshape(K, 4, 16, CW)

    def contribution(b):
        total = None
        for k in range(K):
            hit = (block_ids[0, k] - first_block == b).astype(F32)
            term = pgrad[k] * hit
            total = term if total is None else total + term
        return total

    def rh_copy(n):
        b, dr = ((0, -1), (1, -1), (NB - 2, 1), (NB - 1, 1))[n]
        return remote(sbuf.at[b], rhalo.at[n], rh_send.at[n], rh_recv.at[n], (row_at(dr), c))

    for n, b in enumerate((0, 1, NB - 2, NB - 1)):
        sbuf[b] = contribution(b).astype(BF16)
        rh_copy(n).start()

    def rs_copy(n):
        to = peer(n)
        return remote(sbuf.at[HB + to], rbuf.at[c], rs_send.at[n], rs_recv.at[c], (r, to))

    def is_inner(to):
        return (to >= HB) & (to < NC - HB)

    def send_inner(n):
        to = peer(n)

        @pl.when(is_inner(to))
        def _():
            sbuf[HB + to] = contribution(HB + to).astype(BF16)
            rs_copy(n).start()

    def send_outer(n):
        @pl.when(jnp.logical_not(is_inner(peer(n))))
        def _():
            rs_copy(n).start()

    for n in range(8):
        send_inner(n)
    for n, b in enumerate((NC, NC + 1, HB, HB + 1)):
        rh_copy(n).wait_recv()
        sbuf[b] = (contribution(b) + rhalo[n].astype(F32)).astype(BF16)
    for n in range(8, NC - 1):
        send_inner(n)
        send_outer(n)
        send_outer(n - 8)
    send_outer(7)

    @pl.when(is_inner(c))
    def _():
        sbuf[HB + c] = contribution(HB + c).astype(BF16)

    rbuf[c] = sbuf[HB + c]

    sum_col()
    set_pair_fix(HID, wf2)

    def second_level(p, _):
        t0, t1 = conv_pair(wf2, v_hid, p)
        fine[pl.ds(2 * p, 2), :, 0:128] = t0.astype(BF16).reshape(2, CH, 128)
        fine[pl.ds(2 * p, 2), :, 128:256] = t1.astype(BF16).reshape(2, CH, 128)
        return 0

    lax.fori_loop(0, FR // 4, second_level, 0, unroll=4)
    spread_sum()
    lax.fori_loop(FR // 4, FR // 2, second_level, 0, unroll=4)
    for c0 in range(0, CH, 16):
        for h0 in range(0, FR, 16):
            flat = fine[h0 : h0 + 16, c0 : c0 + 16, :].reshape(256, 256)
            cot[c0 : c0 + 16, h0 : h0 + 16, :] = dot(perm, flat).astype(BF16).reshape(16, 16, 256)
    out = pltpu.make_async_copy(cot, fine_hbm, out_sem)
    out.start()

    for q in range(4):
        senders = [source(n) if n < NC - 1 else c for n in range(4 * q, 4 * q + 4)]
        for n in range(4 * q, min(4 * q + 4, NC - 1)):
            rs_copy(n).wait_send()
            there = rbuf.at[source(n)]
            remote(there, there, rs_send.at[n], rs_recv.at[source(n)], (r, source(n))).wait_recv()
        flat = jnp.concatenate([rbuf[n].reshape(256, CW) for n in senders], axis=1)
        spot = jnp.concatenate([spots[n] for n in senders], axis=0)
        part = dot(flat, spot).reshape(4, CH, 256)
        coarse_out[...] = part if q == 0 else coarse_out[...] + part

    for n in range(4):
        rh_copy(n).wait_send()
    for n in range(NC - 1):
        w3_copy(n).wait_send()
        w3_arrival(n).wait_recv()
    out.wait()


def results(fine, grads, block, fine_out, first_out, second_out, coarse_out, rows, sums, held, first, second, sem):
    fetched = pltpu.make_async_copy(block, held, sem.at[0])
    moved = pltpu.make_async_copy(held, coarse_out, sem.at[1])
    summed = pltpu.make_async_copy(grads, sums, sem.at[2])
    parts = [pl.ds(16 * n, 16) for n in range(4)]
    arrivals = [pltpu.make_async_copy(fine.at[p], rows.at[p], sem.at[5 + n]) for n, p in enumerate(parts)]
    leaving = [pltpu.make_async_copy(rows.at[p], fine_out.at[p], sem.at[9 + n]) for n, p in enumerate(parts)]
    summed.start()
    for copy in arrivals:
        copy.start()
    fetched.start()
    for n in range(4):
        arrivals[n].wait()
        leaving[n].start()
    fetched.wait()
    moved.start()
    summed.wait()
    both = [
        jnp.concatenate([sums[0:8, w].reshape(3 * CH, 128), sums[8:16, w].reshape(3 * CH, 128)], axis=1)
        for w in range(2)
    ]
    for a in range(3):
        for e in range(3):
            first[a, e] = both[0][e * CH : (e + 1) * CH, a * CIN : (a + 1) * CIN]
            second[a, e] = both[1][e * CH : (e + 1) * CH, a * CH : (a + 1) * CH]
    last = [
        pltpu.make_async_copy(first, first_out, sem.at[3]),
        pltpu.make_async_copy(second, second_out, sem.at[4]),
    ]
    for copy in last:
        copy.start()
    for copy in leaving + last + [moved]:
        copy.wait()


def local(
    coarse,
    noisy,
    cotangent,
    interp_rows,
    interp_cols,
    first_weight,
    second_weight,
    block_ids,
    weight_ids,
    col_start,
):
    smem = pl.BlockSpec(memory_space=pltpu.SMEM)
    vmem = pl.BlockSpec(memory_space=pltpu.VMEM)
    dma = pltpu.SemaphoreType.DMA
    fine, grads, block = pl.pallas_call(
        kernel,
        out_shape=(
            jax.ShapeDtypeStruct((CH, FR, 256), BF16),
            jax.ShapeDtypeStruct((NC, 2, 24, 128), F32),
            jax.ShapeDtypeStruct((4, CH, 256), F32),
        ),
        in_specs=[smem] * 3 + [pl.BlockSpec(memory_space=pl.ANY)] * 7,
        out_specs=(pl.BlockSpec(memory_space=pl.ANY), vmem, vmem),
        scratch_shapes=[
            pltpu.VMEM((4, CH, 256), BF16),
            pltpu.VMEM((FS, FR, 256), BF16),
            pltpu.VMEM((CH, FR, 256), BF16),
            pltpu.VMEM((8, 4, FR), BF16),
            pltpu.VMEM((CW, 256), BF16),
            pltpu.VMEM((3, 3, CH, CIN), BF16),
            pltpu.VMEM((3, 3, CH, CH), BF16),
            pltpu.VMEM((FR + 2, CH, 256), BF16),
            pltpu.VMEM((FR + 2, CIN, 256), BF16),
            pltpu.VMEM((FR + 2, CH, 256), BF16),
            pltpu.VMEM((FR + 2, CH, 256), BF16),
            pltpu.VMEM((FR, 3, CH, 256), BF16),
            pltpu.VMEM((FR, 3, CH, 256), BF16),
            pltpu.VMEM((FR, CH, 256), F32),
            pltpu.VMEM((FR, CH, 256), F32),
            pltpu.VMEM((FR, CH, 256), BF16),
            pltpu.VMEM((3 * CH, 256), BF16),
            pltpu.VMEM((3, 2, CH, 256), BF16),
            pltpu.VMEM((3, 2, CH, 256), BF16),
            pltpu.VMEM((3, 2, CH, 256), BF16),
            pltpu.VMEM((3, CH, 128), BF16),
            pltpu.VMEM((CIN, 128), BF16),
            pltpu.VMEM((3, 6, CH, 128), BF16),
            pltpu.VMEM((6, CIN, 128), BF16),
            pltpu.VMEM((3, 3, CH, 128), BF16),
            pltpu.VMEM((3, CIN, 128), BF16),
            pltpu.VMEM((CH, 128), F32),
            pltpu.VMEM((NC, 8, 128), jnp.int32),
            pltpu.VMEM((NC, 8, 128), jnp.int32),
            pltpu.VMEM((2, 4, 4, 2, CH, CW), BF16),
            pltpu.VMEM((4, 2, CH, 256), BF16),
            pltpu.VMEM((4, 2, CH, 256), BF16),
            pltpu.VMEM((NB, 2, CH, CW), BF16),
            pltpu.VMEM((NB, 2, CH, CW), BF16),
            pltpu.VMEM((4, 256, CW), BF16),
            pltpu.VMEM((512, 256), BF16),
            pltpu.VMEM((FR, CH, CW), BF16),
            pltpu.VMEM((K, 4, CH, CW), F32),
            pltpu.VMEM((NB, 4, CH, CW), BF16),
            pltpu.VMEM((NC, 4, CH, CW), BF16),
            pltpu.VMEM((4, 4, CH, CW), BF16),
            pltpu.VMEM((NC, CW, 256), BF16),
            pltpu.VMEM((3 * CH, 256), F32),
            pltpu.VMEM((6 * CH, 256), F32),
            pltpu.VMEM((NC, 2, 24, 128), F32),
            pltpu.VMEM((NC, 2, 24, 128), F32),
            pltpu.VMEM((NR, 2, 24, 128), F32),
            dma((4, 8)),
            dma((4, 8)),
            dma((3, 4)),
            dma((3, 4)),
            dma((2, 4)),
            dma((2, 4)),
            dma((2, 4)),
            dma((2, 4)),
            dma((6,)),
            dma((6,)),
            dma((NC,)),
            dma((NC,)),
            dma((4,)),
            dma((4,)),
            dma((NC,)),
            dma((NC,)),
            dma((NR,)),
            dma((NR,)),
            dma((NC,)),
            dma((NC,)),
            dma,
            dma((7,)),
        ],
        compiler_params=pltpu.CompilerParams(
            collective_id=0, has_side_effects=True, vmem_limit_bytes=56 * 1024 * 1024
        ),
        cost_estimate=pl.CostEstimate(flops=4_000_000_000, bytes_accessed=8_000_000, transcendentals=524_288),
    )(
        block_ids,
        weight_ids,
        col_start,
        coarse,
        noisy,
        cotangent,
        interp_rows.transpose(0, 2, 1),
        interp_cols,
        first_weight,
        second_weight,
    )
    anywhere = pl.BlockSpec(memory_space=pl.ANY)
    return pl.pallas_call(
        results,
        out_shape=(
            jax.ShapeDtypeStruct((CH, FR, 256), BF16),
            jax.ShapeDtypeStruct((3, 3, CH, CIN), F32),
            jax.ShapeDtypeStruct((3, 3, CH, CH), F32),
            jax.ShapeDtypeStruct((4, CH, 256), F32),
        ),
        in_specs=[anywhere] * 3,
        out_specs=(anywhere,) * 4,
        scratch_shapes=[
            pltpu.VMEM((CH, FR, 256), BF16),
            pltpu.VMEM((NC, 2, 24, 128), F32),
            pltpu.VMEM((4, CH, 256), F32),
            pltpu.VMEM((3, 3, CH, CIN), F32),
            pltpu.VMEM((3, 3, CH, CH), F32),
            dma((13,)),
        ],
        compiler_params=pltpu.CompilerParams(vmem_limit_bytes=60 * 1024 * 1024),
        cost_estimate=pl.CostEstimate(flops=270_000_000, bytes_accessed=4_000_000, transcendentals=0),
    )(fine, grads, block)


def solution(mesh):
    in_specs = (
        P(("row", "col"), None, None),
        P(None, "row", "col"),
        P(None, "row", "col"),
        P(),
        P(),
        P(),
        P(),
        P(("row", "col"), None),
        P(("row", "col"), None),
        P("col"),
    )
    out_specs = (P(None, "row", "col"), P(), P(), P(("row", "col"), None, None))
    return jax.shard_map(local, mesh=mesh, in_specs=in_specs, out_specs=out_specs, check_vma=False)
```
